128 devices in a mesh: gx: 8 (over y_hi, x), gy: 16 (over y_lo, z, core).
Axes of the slice: x: 4, y: 4 (y_hi: 2, y_lo: 2; y = y_hi * 2 + y_lo), z: 4, core: 2. Of those that a mesh axis runs over, the one named last changes fastest.
Arguments:
- features: bfloat16 [32, 64, 128, 128], P(None, 'gx', 'gy'), may hold values from -6 to 6
- weight_two: bfloat16 [27, 32, 32], replicated, may hold values from -0.21875 to 0.21875
- bias_two: float32 [32], replicated, may hold values from -3 to 3
- weight_three: bfloat16 [27, 64, 32], replicated, may hold values from -0.21875 to 0.21875
- bias_three: float32 [64], replicated, may hold values from -3 to 3
- weight_four: bfloat16 [27, 128, 64], replicated, may hold values from -0.25 to 0.25
- bias_four: float32 [128], replicated, may hold values from -3 to 3
Outputs:
- level_two: bfloat16 [32, 64, 128, 128], P(None, 'gx', 'gy')
- level_three: bfloat16 [64, 32, 64, 64], P(None, 'gx', 'gy')
- bottleneck: bfloat16 [128, 16, 32, 32], P(None, None, None, 'gy')
The draws below stay inside these ranges and needn't reach their ends.
All inputs are finite; a program needn't handle non-finite values.
Results may differ from the reference program's by a relative error of at most 0.0085.
Values may be sent and summed in bfloat16 or wider, within the bound.
A program may use at most 64 MiB of HBM per device.

```python
import jax
import jax.numpy as jnp
from jax import lax

C2 = 32
C3 = 64
C4 = 128
NZ = 128
NX = 64
NY = 128


def steps_of(stream_key, dims, pieces, smallest, top_value):
    loudness = 1.0
    for dim, shards_of in pieces:
        heights = jax.random.uniform(jax.random.fold_in(jax.random.fold_in(stream_key, 6), dim), (shards_of,), jnp.float32, smallest / len(pieces), top_value / len(pieces))
        loudness = loudness * jnp.repeat(jnp.exp(heights), dims[dim] // shards_of).reshape((-1,) + (1,) * (len(dims) - 1 - dim))
    return loudness


def scatter_about(stream_key, shape, width, bound, cuts=(), dtype=jnp.bfloat16):
    gain = steps_of(stream_key, shape, cuts, -0.22, 0.18) if cuts else 1.0
    drawn = jax.random.normal(stream_key, shape, jnp.float32) * width * gain
    return jnp.minimum(jnp.maximum(drawn, -bound), bound).astype(dtype)


def setup_inputs(seed: int = 0) -> dict:
    splits = jax.random.split(jax.random.key(seed), 8)
    features = scatter_about(splits[0], (C2, NX, NY, NZ), 1.0, 6.0, ((1, 8), (2, 16)))
    weight_two = scatter_about(splits[1], (27, C2, C2), (27 * C2) ** -0.5, 0.21875)
    bias_two = scatter_about(splits[2], (C2,), 0.5, 3.0, (), jnp.float32)
    weight_three = scatter_about(splits[3], (27, C3, C2), (27 * C2) ** -0.5, 0.21875)
    bias_three = scatter_about(splits[4], (C3,), 0.5, 3.0, (), jnp.float32)
    weight_four = scatter_about(splits[5], (27, C4, C3), (9 * C3) ** -0.5, 0.25)
    bias_four = scatter_about(splits[6], (C4,), 0.5, 3.0, (), jnp.float32)
    return dict(features=features, weight_two=weight_two, bias_two=bias_two, weight_three=weight_three, bias_three=bias_three, weight_four=weight_four, bias_four=bias_four)


def convolve(source, weights, bias_values):
    in_channels = source.shape[0]
    out_channels = weights.shape[1]
    padded = jnp.pad(source.astype(jnp.float32), ((0, 0), (1, 1), (1, 1), (1, 1)), mode="wrap")
    kernel = weights.astype(jnp.float32).reshape(3, 3, 3, out_channels, in_channels).transpose(3, 4, 0, 1, 2)
    result = lax.conv_general_dilated(padded[None], kernel, (1, 1, 1), "VALID", precision=lax.Precision.HIGHEST)
    result = result[0] + bias_values.astype(jnp.float32)[:, None, None, None]
    return jax.nn.leaky_relu(result, 0.1).astype(jnp.bfloat16)


def average_pool(source):
    channels, extent_x, extent_y, extent_z = source.shape
    blocks = source.astype(jnp.float32).reshape(channels, extent_x // 2, 2, extent_y // 2, 2, extent_z // 2, 2)
    return blocks.mean(axis=(2, 4, 6)).astype(jnp.bfloat16)


def reference(features, weight_two, bias_two, weight_three, bias_three, weight_four, bias_four):
    level_two = convolve(features, weight_two, bias_two)
    level_three = convolve(average_pool(level_two), weight_three, bias_three)
    bottleneck = convolve(average_pool(level_three), weight_four, bias_four)
    return level_two, level_three, bottleneck
```

```python
import functools

import jax
import jax.numpy as jnp
import numpy as np
from jax import lax
from jax.experimental import pallas as pl
from jax.experimental.pallas import tpu as pltpu
from jax.sharding import PartitionSpec as P

BF = jnp.bfloat16
F32 = jnp.float32
MESH = pl.DeviceIdType.MESH


def tables():
    parts, at, row = [], {}, 0

    def add(name, matrix):
        nonlocal row
        rows, lanes = matrix.shape
        full = np.zeros((-(-rows // 16) * 16, 256), np.float32)
        full[:rows, :lanes] = matrix
        at[name] = row
        parts.append(full)
        row += full.shape[0]

    select = np.zeros((64, 256))
    for c in range(32):
        select[c, c * 8] = 1
        select[32 + c, c * 8 + 7] = 1
    add("select_two", select)
    spread = np.zeros((8, 128, 256))
    for y in range(8):
        for dy in range(3):
            if 0 <= y + dy - 1 < 8:
                for c in range(32):
                    spread[y, dy * 32 + c, c * 8 + y + dy - 1] = 1
    add("spread_two", spread.reshape(1024, 256))
    order = np.zeros((256, 256))
    for y in range(8):
        for o in range(32):
            order[o * 8 + y, y * 32 + o] = 1
    add("order_two", order)
    edge = np.zeros((256, 64))
    for o in range(32):
        edge[o * 8, o] = 1
        edge[o * 8 + 7, 32 + o] = 1
    add("edge_two", edge)
    pool = np.zeros((2, 2, 128, 128))
    for half in range(2):
        for x in range(2):
            for z in range(128):
                pool[half, x, z, half * 64 + z // 2] = 0.125
    add("pool_two", pool.reshape(512, 128))
    select = np.zeros((64, 128))
    for c in range(32):
        select[c, c * 4] = 1
        select[32 + c, c * 4 + 3] = 1
    add("select_three", select)
    add("unit", np.eye(64))
    spread = np.zeros((4, 128, 128))
    for y in range(4):
        for dy in range(3):
            if 0 <= y + dy - 1 < 4:
                for c in range(32):
                    spread[y, dy * 32 + c, c * 4 + y + dy - 1] = 1
    add("spread_three", spread.reshape(512, 128))
    order = np.zeros((256, 256))
    for y in range(4):
        for o in range(64):
            order[o * 4 + y, y * 64 + o] = 1
    add("order_three", order)
    edge = np.zeros((256, 128))
    for o in range(64):
        edge[o * 4, o] = 1
        edge[o * 4 + 3, 64 + o] = 1
    add("edge_three", edge)
    pick = np.zeros((2, 16, 2, 2, 2, 4, 64))
    for odd in range(2):
        for target in range(16):
            for half in range(2):
                z = (2 * target - 1 + 2 * half + odd) % 32
                for x in range(2):
                    pick[odd, target, half, x, :, 2 * x : 2 * x + 2, 2 * z : 2 * z + 2] = 0.125
    add("pick_four", pick.reshape(256, 256))
    gather = np.zeros((2, 256, 128))
    for odd in range(2):
        for o in range(64):
            gather[odd, o * 4 : o * 4 + 4, odd * 64 + o] = 1
    add("gather_four", gather.reshape(512, 128))
    turn = np.zeros((3, 2, 2, 32, 16, 2, 2, 2))
    for dy in range(3):
        for half in range(2):
            for x in range(2):
                for y in range(32):
                    source = (y + dy - 1) % 32
                    turn[dy, half, x, y, source // 2, half, x, source % 2] = 1
    add("turn_four", turn.reshape(384, 128))
    return np.concatenate(parts).astype(jnp.bfloat16), at


TABLE, AT = tables()


def mm(a, b):
    return jnp.dot(a, b, preferred_element_type=F32)


def mm_t(a, b):
    return lax.dot_general(a, b, (((1,), (1,)), ((), ())), preferred_element_type=F32)


def leaky(t):
    return jnp.maximum(t, 0.1 * t)


def rolled_64(v, back):
    lane = lax.broadcasted_iota(jnp.int32, v.shape, 1) % 64
    if back:
        return jnp.where(lane == 0, pltpu.roll(v, 65, 1), pltpu.roll(v, 1, 1))
    return jnp.where(lane == 63, pltpu.roll(v, 63, 1), pltpu.roll(v, 127, 1))


def kernel(
    feat, w2_in, b2_in, w3_in, b3_in, w4_in, b4_in, tab_in,
    out2, out3, out4,
    fx, fm, hs, hr, w2, w3, w4, b2, b3, b4, tab, wc2, z2, t2, wc3, z3, t3, bias2, bias3,
    pooled, own3, hs3, hr3, d3, l3, sa, rb, pp,
    load_sem, feat_sem, send_sem, recv_sem, send3_sem, recv3_sem, senda_sem, recva_sem, sendb_sem, recvb_sem,
):
    gx, gy = lax.axis_index("gx"), lax.axis_index("gy")
    xp, xm = lax.rem(gx + 1, 8), lax.rem(gx + 7, 8)
    yp, ym = lax.rem(gy + 1, 16), lax.rem(gy + 15, 16)

    def table(name, rows, lanes, skip=0):
        start = AT[name] + skip
        return tab[start : start + rows, :lanes]

    loads = [
        pltpu.make_async_copy(feat.at[:, x], fx.at[x + 1], feat_sem.at[x]) for x in range(8)
    ]
    others = [
        pltpu.make_async_copy(tab_in, tab, load_sem.at[0]),
        pltpu.make_async_copy(w2_in, w2, load_sem.at[1]),
        pltpu.make_async_copy(b2_in, b2, load_sem.at[2]),
        pltpu.make_async_copy(w3_in, w3, load_sem.at[3]),
        pltpu.make_async_copy(b3_in, b3, load_sem.at[4]),
        pltpu.make_async_copy(b4_in, b4, load_sem.at[5]),
        pltpu.make_async_copy(w4_in, w4.at[:, 0:3, :, 0:128], load_sem.at[6]),
        pltpu.make_async_copy(w4_in, w4.at[:, 1:4, :, 128:256], load_sem.at[7]),
    ]
    for copy in loads:
        copy.start()
    for copy in others:
        copy.start()

    barrier = pltpu.get_barrier_semaphore()

    def greet(x, y):
        pl.semaphore_signal(barrier, inc=1, device_id=(x, y), device_id_type=MESH)

    for x in (xm, xp):
        for y in (ym, yp):
            greet(x, y)
    for k in range(1, 16):
        greet(gx, lax.rem(gy + k, 16))
    for k in range(1, 8):
        greet(lax.rem(gx + k, 8), gy)
    pl.semaphore_wait(barrier, 4 + 15 + 7)

    def remote(src, dst, send, recv, x, y):
        return pltpu.make_async_remote_copy(
            src_ref=src, dst_ref=dst, send_sem=send, recv_sem=recv,
            device_id=(x, y), device_id_type=MESH,
        )

    first = [
        remote(feat.at[:, 7], fx.at[0], send_sem.at[0], recv_sem.at[0], xp, gy),
        remote(feat.at[:, 0], fx.at[9], send_sem.at[1], recv_sem.at[1], xm, gy),
    ]
    for copy in first:
        copy.start()

    def place(x):
        v = fx[x].astype(F32).reshape(256, 128)
        lanes = slice(x * 128, x * 128 + 128)
        fm[0:256, lanes] = pltpu.roll(v, 1, 1).astype(BF)
        fm[256:512, lanes] = v.astype(BF)
        fm[512:768, lanes] = pltpu.roll(v, 127, 1).astype(BF)

    for copy in loads:
        copy.wait()
    for x in range(1, 9):
        place(x)
    others[0].wait()
    edges = mm(table("select_two", 64, 256), fm[256:512, 128:1152]).astype(BF)
    for side in range(2):
        for x in range(8):
            hs[side, x] = edges[side * 32 : side * 32 + 32, x * 128 : x * 128 + 128]
    second = [
        remote(hs.at[1], hr.at[0, 1:9], send_sem.at[2], recv_sem.at[2], gx, yp),
        remote(hs.at[0], hr.at[1, 1:9], send_sem.at[3], recv_sem.at[3], gx, ym),
        remote(hs.at[1, 7], hr.at[0, 0], send_sem.at[4], recv_sem.at[4], xp, yp),
        remote(hs.at[1, 0], hr.at[0, 9], send_sem.at[5], recv_sem.at[5], xm, yp),
        remote(hs.at[0, 7], hr.at[1, 0], send_sem.at[6], recv_sem.at[6], xp, ym),
        remote(hs.at[0, 0], hr.at[1, 9], send_sem.at[7], recv_sem.at[7], xm, ym),
    ]
    for copy in second:
        copy.start()

    for copy in others[1:]:
        copy.wait()
    gap = jnp.zeros((32, 32), F32)
    for dx in range(3):
        for dz in range(3):
            k = 3 * dx + dz
            wc2[k * 32 : k * 32 + 32, :] = jnp.concatenate(
                [w2[9 * dx + 3 * dy + dz].astype(F32) for dy in range(3)] + [gap], axis=1
            ).astype(BF)
    for y in range(8):
        z2[:, y * 32 : y * 32 + 32, :] = (
            mm(wc2[...], table("spread_two", 128, 256, 128 * y)).astype(BF).reshape(9, 32, 256)
        )
    for dx in range(3):
        for dz in range(3):
            t2[dx, :, dz * 256 : dz * 256 + 256] = mm(
                table("order_two", 256, 256), z2[3 * dx + dz]
            ).astype(BF)
        low = [w2[9 * dx + dz].astype(F32) for dz in range(3)]
        high = [w2[9 * dx + 6 + dz].astype(F32) for dz in range(3)]
        z_edge = jnp.concatenate(
            [
                jnp.concatenate([low[0], gap, low[1], gap, low[2], gap, gap, gap], axis=1),
                jnp.concatenate([gap, high[0], gap, high[1], gap, high[2], gap, gap], axis=1),
            ],
            axis=0,
        ).astype(BF)
        t2[dx, :, 768:1024] = mm(table("edge_two", 256, 64), z_edge).astype(BF)
    row = lax.broadcasted_iota(jnp.int32, (256, 32), 0) // 8
    lane = lax.broadcasted_iota(jnp.int32, (256, 32), 1)
    column = jnp.sum(jnp.where(row == lane, b2[...], 0.0), axis=1, keepdims=True)
    bias2[...] = jnp.broadcast_to(column, (256, 128))

    for dx in range(3):
        for dz in range(3):
            k = 3 * dx + dz
            stack = jnp.concatenate(
                [w3[9 * dx + 3 * dy + dz] for dy in range(3)] + [jnp.zeros((32, 64), BF)], axis=0
            )
            wc3[k * 64 : k * 64 + 64, :] = mm_t(table("unit", 64, 64), stack).astype(BF)
    for y in range(4):
        z3[:, y * 64 : y * 64 + 64, :] = (
            mm(wc3[...], table("spread_three", 128, 128, 128 * y)).astype(BF).reshape(9, 64, 128)
        )
    gap = jnp.zeros((64, 32), F32)
    for dx in range(3):
        low, high = [], []
        for dz in range(3):
            k = 3 * dx + dz
            t3[dx, :, dz * 128 : dz * 128 + 128] = mm(table("order_three", 256, 256), z3[k]).astype(BF)
            block = wc3[k * 64 : k * 64 + 64, :].astype(F32)
            low.append(block[:, 0:32])
            high.append(block[:, 64:96])
        z_edge = jnp.concatenate(
            [
                jnp.concatenate([low[0], gap, low[1], gap, low[2], gap, gap, gap], axis=1),
                jnp.concatenate([gap, high[0], gap, high[1], gap, high[2], gap, gap], axis=1),
            ],
            axis=0,
        ).astype(BF)
        t3[dx, :, 384:640] = mm(table("edge_three", 256, 128), z_edge).astype(BF)
    row = lax.broadcasted_iota(jnp.int32, (256, 64), 0) // 4
    lane = lax.broadcasted_iota(jnp.int32, (256, 64), 1)
    column = jnp.sum(jnp.where(row == lane, b3[...], 0.0), axis=1, keepdims=True)
    bias3[...] = jnp.broadcast_to(column, (256, 128))

    w4[:, 3, :, 0:128] = jnp.zeros((9, 64, 128), BF)
    w4[:, 0, :, 128:256] = jnp.zeros((9, 64, 128), BF)

    fm[960:1024, :] = jnp.zeros((64, 1280), BF)
    for copy in first:
        copy.wait()
    place(0)
    place(9)
    for copy in second:
        copy.wait()
    for x in range(10):
        v = jnp.concatenate([hr[0, x], hr[1, x]], axis=0).astype(F32)
        lanes = slice(x * 128, x * 128 + 128)
        fm[768:832, lanes] = pltpu.roll(v, 1, 1).astype(BF)
        fm[832:896, lanes] = v.astype(BF)
        fm[896:960, lanes] = pltpu.roll(v, 127, 1).astype(BF)

    def quad(q, carry):
        total = jnp.zeros((256, 128), F32)
        for half in range(2):
            base = q * 4 + half * 2
            acc = jnp.zeros((256, 256), F32)
            for dx in range(3):
                lanes = pl.ds(pl.multiple_of((base + dx) * 128, 128), 256)
                acc = acc + mm(t2[dx], fm[:, lanes])
            bias = bias2[...]
            for x in range(2):
                v = leaky(acc[:, x * 128 : x * 128 + 128] + bias)
                out2[:, base + x] = v.reshape(32, 8, 128).astype(BF)
                total = total + mm(v.astype(BF), table("pool_two", 128, 128, half * 256 + x * 128))
        pooled[...] = total
        own3[q + 1] = (pooled[pl.ds(0, 128, stride=2), :] + pooled[pl.ds(1, 128, stride=2), :]).astype(BF)
        return carry

    lax.fori_loop(0, 2, quad, 0)

    for q in range(2):
        picked = mm(table("select_three", 64, 128), own3[q + 1]).astype(BF)
        hs3[0, q] = picked[0:32]
        hs3[1, q] = picked[32:64]
    third = [
        remote(own3.at[2], own3.at[0], send3_sem.at[0], recv3_sem.at[0], xp, gy),
        remote(own3.at[1], own3.at[3], send3_sem.at[1], recv3_sem.at[1], xm, gy),
        remote(hs3.at[1], hr3.at[0, 1:3], send3_sem.at[2], recv3_sem.at[2], gx, yp),
        remote(hs3.at[0], hr3.at[1, 1:3], send3_sem.at[3], recv3_sem.at[3], gx, ym),
        remote(hs3.at[1, 1], hr3.at[0, 0], send3_sem.at[4], recv3_sem.at[4], xp, yp),
        remote(hs3.at[1, 0], hr3.at[0, 3], send3_sem.at[5], recv3_sem.at[5], xm, yp),
        remote(hs3.at[0, 1], hr3.at[1, 0], send3_sem.at[6], recv3_sem.at[6], xp, ym),
        remote(hs3.at[0, 0], hr3.at[1, 3], send3_sem.at[7], recv3_sem.at[7], xm, ym),
    ]
    for copy in third:
        copy.start()
    d3[576:640, :] = jnp.zeros((64, 640), BF)
    for copy in third:
        copy.wait()
    tiles = []
    for t in range(4):
        tiles.append(
            jnp.concatenate([own3[t], hr3[0, t], hr3[1, t]], axis=0).astype(F32)
        )
    turned = [pltpu.roll(v, 64, 1) for v in tiles]
    lane = lax.broadcasted_iota(jnp.int32, (192, 128), 1)
    between = [jnp.where(lane < 64, turned[t], turned[t + 1]) for t in range(3)]
    for slot, v in enumerate([tiles[1], tiles[2]] + between):
        lanes = slice(slot * 128, slot * 128 + 128)
        for dz, u in enumerate((rolled_64(v, True), v, rolled_64(v, False))):
            u = u.astype(BF)
            d3[dz * 128 : dz * 128 + 128, lanes] = u[0:128]
            d3[384 + dz * 64 : 448 + dz * 64, lanes] = u[128:192]
    acc = mm(t3[0], d3[:, 256:512]) + mm(t3[1], d3[:, 0:256]) + mm(t3[2], d3[:, 384:640])
    for q in range(2):
        v = leaky(acc[:, q * 128 : q * 128 + 128] + bias3[...])
        l3[:, q * 128 : q * 128 + 128] = v.astype(BF)
        out3[:, 2 * q] = v[:, 0:64].reshape(64, 4, 64).astype(BF)
        out3[:, 2 * q + 1] = v[:, 64:128].reshape(64, 4, 64).astype(BF)

    sums = mm_t(table("pick_four", 256, 256), l3[...])
    row = lax.broadcasted_iota(jnp.int32, (256, 256), 0) % 2
    lane = lax.broadcasted_iota(jnp.int32, (256, 256), 1) % 4 // 2
    sums = jnp.where(row == lane, sums, 0.0)
    head = sums.astype(BF)
    tail = (sums - head.astype(F32)).astype(BF)
    block = jnp.zeros((128, 128), F32)
    for odd in range(2):
        g = table("gather_four", 256, 128, odd * 256)
        block = block + mm(head[odd * 128 : odd * 128 + 128], g) + mm(tail[odd * 128 : odd * 128 + 128], g)
    sa[...] = block.reshape(16, 8, 128).astype(BF)
    rb[gx, gy] = sa[gy]

    def send_a(k, carry):
        target = lax.rem(gy + k, 16)
        remote(sa.at[target], rb.at[gx, gy], senda_sem, recva_sem, gx, target).start()
        return carry

    lax.fori_loop(1, 16, send_a, 0)
    pltpu.make_async_copy(rb.at[gx, 0:15], rb.at[gx, 0:15], recva_sem).wait()

    def send_b(k, carry):
        target = lax.rem(gx + k, 8)
        remote(rb.at[gx], rb.at[gx], sendb_sem, recvb_sem, target, gy).start()
        return carry

    lax.fori_loop(1, 8, send_b, 0)
    pltpu.make_async_copy(sa.at[0:15], sa.at[0:15], senda_sem).wait()
    pltpu.make_async_copy(rb.at[0:7], rb.at[0:7], recvb_sem).wait()

    for x in range(8):
        v = rb[x].astype(F32).reshape(128, 128).astype(BF)
        moved = mm(table("turn_four", 384, 128), v).astype(BF)
        for dy in range(3):
            for half in range(2):
                start = (dy * 2 + half) * 64
                pp[dy, (1 + 2 * x) * 32 : (3 + 2 * x) * 32, half * 128 : half * 128 + 128] = moved[start : start + 64]
    pp[:, 0:32, :] = pp[:, 512:544, :]
    pp[:, 544:576, :] = pp[:, 32:64, :]
    bias = jnp.concatenate([b4[...], b4[...]], axis=1)

    def part(m, carry):
        acc = jnp.zeros((256, 256), F32)
        for dx in range(3):
            for dy in range(3):
                rows = pl.ds(pl.multiple_of(m * 256 + dx * 32, 32), 256)
                acc = acc + mm(pp[dy, rows, :], w4[3 * dx + dy].reshape(256, 256))
        v = leaky(acc + bias)
        out4[pl.ds(pl.multiple_of(m * 256, 256), 256)] = v.reshape(256, 2, 128).astype(BF)
        return carry

    lax.fori_loop(0, 2, part, 0)
    pltpu.make_async_copy(rb.at[0:7], rb.at[0:7], sendb_sem).wait()


def shards(features, weight_two, bias_two, weight_three, bias_three, weight_four, bias_four):
    vm = pl.BlockSpec(memory_space=pltpu.VMEM)
    hbm = pl.BlockSpec(memory_space=pl.ANY)
    table = jnp.asarray(TABLE)
    w3 = weight_three.transpose(0, 2, 1)
    w4 = weight_four.transpose(0, 2, 1).reshape(9, 3, 64, 128)
    dma = pltpu.SemaphoreType.DMA
    level_two, level_three, bottleneck = pl.pallas_call(
        kernel,
        out_shape=(
            jax.ShapeDtypeStruct((32, 8, 8, 128), BF),
            jax.ShapeDtypeStruct((64, 4, 4, 64), BF),
            jax.ShapeDtypeStruct((512, 2, 128), BF),
        ),
        in_specs=[hbm] * 8,
        out_specs=(vm, vm, vm),
        scratch_shapes=[
            pltpu.VMEM((10, 32, 8, 128), BF),
            pltpu.VMEM((1024, 1280), BF),
            pltpu.VMEM((2, 8, 32, 128), BF),
            pltpu.VMEM((2, 10, 32, 128), BF),
            pltpu.VMEM((27, 32, 32), BF),
            pltpu.VMEM((27, 32, 64), BF),
            pltpu.VMEM((9, 4, 64, 256), BF),
            pltpu.VMEM((1, 32), F32),
            pltpu.VMEM((1, 64), F32),
            pltpu.VMEM((1, 128), F32),
            pltpu.VMEM(TABLE.shape, BF),
            pltpu.VMEM((288, 128), BF),
            pltpu.VMEM((9, 256, 256), BF),
            pltpu.VMEM((3, 256, 1024), BF),
            pltpu.VMEM((576, 128), BF),
            pltpu.VMEM((9, 256, 128), BF),
            pltpu.VMEM((3, 256, 640), BF),
            pltpu.VMEM((256, 128), F32),
            pltpu.VMEM((256, 128), F32),
            pltpu.VMEM((256, 128), F32),
            pltpu.VMEM((4, 128, 128), BF),
            pltpu.VMEM((2, 2, 32, 128), BF),
            pltpu.VMEM((2, 4, 32, 128), BF),
            pltpu.VMEM((640, 640), BF),
            pltpu.VMEM((256, 256), BF),
            pltpu.VMEM((16, 8, 128), BF),
            pltpu.VMEM((8, 16, 8, 128), BF),
            pltpu.VMEM((3, 576, 256), BF),
            dma((8,)), dma((8,)), dma((8,)), dma((8,)), dma((8,)), dma((8,)),
            dma, dma, dma, dma,
        ],
        compiler_params=pltpu.CompilerParams(
            collective_id=0, has_side_effects=True, vmem_limit_bytes=40 * 1024 * 1024
        ),
    )(features, weight_two, bias_two[None], w3, bias_three[None], w4, bias_four[None], table)
    return level_two, level_three, bottleneck.reshape(16, 32, 2, 128).transpose(3, 0, 1, 2)


def solution(mesh):
    return jax.shard_map(
        shards,
        mesh=mesh,
        in_specs=(P(None, "gx", "gy", None), P(), P(), P(), P(), P(), P()),
        out_specs=(P(None, "gx", "gy", None), P(None, "gx", "gy", None), P(None, None, None, "gy")),
        check_vma=False,
    )
```

```python
import functools

import jax
import jax.numpy as jnp
import numpy as np
from jax import lax
from jax.experimental import pallas as pl
from jax.experimental.pallas import tpu as pltpu
from jax.sharding import PartitionSpec as P

BF = jnp.bfloat16
F32 = jnp.float32
MESH = pl.DeviceIdType.MESH


def tables():
    parts, at, row = [], {}, 0

    def add(name, matrix):
        nonlocal row
        rows, lanes = matrix.shape
        full = np.zeros((-(-rows // 16) * 16, 256), np.float32)
        full[:rows, :lanes] = matrix
        at[name] = row
        parts.append(full)
        row += full.shape[0]

    spread = np.zeros((8, 128, 256))
    for y in range(8):
        for dy in range(3):
            if 0 <= y + dy - 1 < 8:
                for c in range(32):
                    spread[y, dy * 32 + c, c * 8 + y + dy - 1] = 1
    add("spread_two", spread.reshape(1024, 256))
    order = np.zeros((256, 256))
    for y in range(8):
        for o in range(32):
            order[o * 8 + y, y * 32 + o] = 1
    add("order_two", order)
    edge = np.zeros((256, 64))
    for o in range(32):
        edge[o * 8, o] = 1
        edge[o * 8 + 7, 32 + o] = 1
    add("edge_two", edge)
    pool = np.zeros((2, 2, 128, 128))
    for half in range(2):
        for x in range(2):
            for z in range(128):
                pool[half, x, z, half * 64 + z // 2] = 0.125
    add("pool_two", pool.reshape(512, 128))
    select = np.zeros((64, 128))
    for c in range(32):
        select[c, c * 4] = 1
        select[32 + c, c * 4 + 3] = 1
    add("select_three", select)
    add("unit", np.eye(64))
    spread = np.zeros((4, 128, 128))
    for y in range(4):
        for dy in range(3):
            if 0 <= y + dy - 1 < 4:
                for c in range(32):
                    spread[y, dy * 32 + c, c * 4 + y + dy - 1] = 1
    add("spread_three", spread.reshape(512, 128))
    order = np.zeros((256, 256))
    for y in range(4):
        for o in range(64):
            order[o * 4 + y, y * 64 + o] = 1
    add("order_three", order)
    edge = np.zeros((256, 128))
    for o in range(64):
        edge[o * 4, o] = 1
        edge[o * 4 + 3, 64 + o] = 1
    add("edge_three", edge)
    pick = np.zeros((2, 16, 2, 2, 2, 4, 64))
    for odd in range(2):
        for target in range(16):
            for half in range(2):
                z = (2 * target - 1 + 2 * half + odd) % 32
                for x in range(2):
                    pick[odd, target, half, x, :, 2 * x : 2 * x + 2, 2 * z : 2 * z + 2] = 0.125
    add("pick_four", pick.reshape(256, 256))
    gather = np.zeros((2, 256, 128))
    for odd in range(2):
        for o in range(64):
            gather[odd, o * 4 : o * 4 + 4, odd * 64 + o] = 1
    add("gather_four", gather.reshape(512, 128))
    turn = np.zeros((3, 2, 2, 32, 16, 2, 2, 2))
    for dy in range(3):
        for half in range(2):
            for x in range(2):
                for y in range(32):
                    source = (y + dy - 1) % 32
                    turn[dy, half, x, y, source // 2, half, x, source % 2] = 1
    add("turn_four", turn.reshape(384, 128))
    return np.concatenate(parts).astype(jnp.bfloat16), at


TABLE, AT = tables()


def mm(a, b):
    return jnp.dot(a, b, preferred_element_type=F32)


def mm_t(a, b):
    return lax.dot_general(a, b, (((1,), (1,)), ((), ())), preferred_element_type=F32)


def leaky(t):
    return jnp.maximum(t, 0.1 * t)


def rolled_64(v, back):
    lane = lax.broadcasted_iota(jnp.int32, v.shape, 1) % 64
    if back:
        return jnp.where(lane == 0, pltpu.roll(v, 65, 1), pltpu.roll(v, 1, 1))
    return jnp.where(lane == 63, pltpu.roll(v, 63, 1), pltpu.roll(v, 127, 1))


def kernel(
    feat, w2_in, b2_in, w3_in, b3_in, w4_in, b4_in, tab_in,
    out2, out3, rb, w4, turn, b4,
    fx, fm, hs, hr, w2, w3, b2, b3, tab, wc2, z2, t2, a2, wc3, z3, t3, bias2, bias3,
    pooled, own3, hs3, hr3, d3, l3, sa,
    load_sem, feat_sem, send_sem, recv_sem, send3_sem, recv3_sem, senda_sem, recva_sem, sendb_sem, recvb_sem,
):
    gx, gy = lax.axis_index("gx"), lax.axis_index("gy")
    xp, xm = lax.rem(gx + 1, 8), lax.rem(gx + 7, 8)
    yp, ym = lax.rem(gy + 1, 16), lax.rem(gy + 15, 16)

    def table(name, rows, lanes, skip=0):
        start = AT[name] + skip
        return tab[start : start + rows, :lanes]

    barrier = pltpu.get_barrier_semaphore()

    def greet(x, y):
        pl.semaphore_signal(barrier, inc=1, device_id=(x, y), device_id_type=MESH)

    for x in (xm, xp):
        for y in (ym, yp):
            greet(x, y)
    for k in range(1, 16):
        greet(gx, lax.rem(gy + k, 16))
    for k in range(1, 8):
        greet(lax.rem(gx + k, 8), gy)
    loads = [
        pltpu.make_async_copy(feat.at[:, x], fx.at[x + 1], feat_sem.at[x]) for x in range(8)
    ]
    others = [
        pltpu.make_async_copy(tab_in, tab, load_sem.at[0]),
        pltpu.make_async_copy(w2_in, w2, load_sem.at[1]),
        pltpu.make_async_copy(b2_in, b2, load_sem.at[2]),
        pltpu.make_async_copy(w3_in, w3, load_sem.at[3]),
        pltpu.make_async_copy(b3_in, b3, load_sem.at[4]),
        pltpu.make_async_copy(b4_in, b4, load_sem.at[5]),
        pltpu.make_async_copy(w4_in, w4.at[:, 0:3, :, 0:128], load_sem.at[6]),
        pltpu.make_async_copy(w4_in, w4.at[:, 1:4, :, 128:256], load_sem.at[7]),
    ]
    for copy in loads:
        copy.start()
    for copy in others:
        copy.start()

    pl.semaphore_wait(barrier, 4 + 15 + 7)

    def remote(src, dst, send, recv, x, y):
        return pltpu.make_async_remote_copy(
            src_ref=src, dst_ref=dst, send_sem=send, recv_sem=recv,
            device_id=(x, y), device_id_type=MESH,
        )

    first = [
        remote(feat.at[:, 7], fx.at[0], send_sem.at[0], recv_sem.at[0], xp, gy),
        remote(feat.at[:, 0], fx.at[9], send_sem.at[1], recv_sem.at[1], xm, gy),
    ]
    for copy in first:
        copy.start()

    def place(x):
        v = fx[x].astype(F32).reshape(256, 128)
        lanes = slice(x * 128, x * 128 + 128)
        fm[256:512, lanes] = v.astype(BF)

    def shift(x):
        lanes = slice(x * 128, x * 128 + 128)
        v = fm[256:512, lanes].astype(F32)
        fm[0:256, lanes] = pltpu.roll(v, 1, 1).astype(BF)
        fm[512:768, lanes] = pltpu.roll(v, 127, 1).astype(BF)

    row = lax.broadcasted_iota(jnp.int32, (64, 256), 0)
    lane = lax.broadcasted_iota(jnp.int32, (64, 256), 1)
    select = jnp.where(lane == row % 32 * 8 + row // 32 * 7, 1.0, 0.0).astype(BF)
    for copy in loads:
        copy.wait()
    for x in range(1, 9):
        place(x)
    edges = mm(select, fm[256:512, 128:1152]).astype(BF)
    for side in range(2):
        for x in range(8):
            hs[side, x] = edges[side * 32 : side * 32 + 32, x * 128 : x * 128 + 128]
    second = [
        remote(hs.at[1, 7], hr.at[0, 0], send_sem.at[4], recv_sem.at[4], xp, yp),
        remote(hs.at[1, 0], hr.at[0, 9], send_sem.at[5], recv_sem.at[5], xm, yp),
        remote(hs.at[0, 7], hr.at[1, 0], send_sem.at[6], recv_sem.at[6], xp, ym),
        remote(hs.at[0, 0], hr.at[1, 9], send_sem.at[7], recv_sem.at[7], xm, ym),
        remote(hs.at[1], hr.at[0, 1:9], send_sem.at[2], recv_sem.at[2], gx, yp),
        remote(hs.at[0], hr.at[1, 1:9], send_sem.at[3], recv_sem.at[3], gx, ym),
    ]
    for copy in second:
        copy.start()

    for x in range(1, 9):
        shift(x)
    for copy in others:
        copy.wait()
    gap = jnp.zeros((32, 32), F32)
    for dx in range(3):
        for dz in range(3):
            k = 3 * dx + dz
            wc2[k * 32 : k * 32 + 32, :] = jnp.concatenate(
                [w2[9 * dx + 3 * dy + dz].astype(F32) for dy in range(3)] + [gap], axis=1
            ).astype(BF)
    for y in range(8):
        z2[:, y * 32 : y * 32 + 32, :] = (
            mm(wc2[...], table("spread_two", 128, 256, 128 * y)).astype(BF).reshape(9, 32, 256)
        )
    for dx in range(3):
        for dz in range(3):
            t2[dx, :, dz * 256 : dz * 256 + 256] = mm(
                table("order_two", 256, 256), z2[3 * dx + dz]
            ).astype(BF)
        low = [w2[9 * dx + dz].astype(F32) for dz in range(3)]
        high = [w2[9 * dx + 6 + dz].astype(F32) for dz in range(3)]
        z_edge = jnp.concatenate(
            [
                jnp.concatenate([low[0], gap, low[1], gap, low[2], gap, gap, gap], axis=1),
                jnp.concatenate([gap, high[0], gap, high[1], gap, high[2], gap, gap], axis=1),
            ],
            axis=0,
        ).astype(BF)
        t2[dx, :, 768:1024] = mm(table("edge_two", 256, 64), z_edge).astype(BF)
    row = lax.broadcasted_iota(jnp.int32, (256, 32), 0) // 8
    lane = lax.broadcasted_iota(jnp.int32, (256, 32), 1)
    column = jnp.sum(jnp.where(row == lane, b2[...], 0.0), axis=1, keepdims=True)
    bias2[...] = jnp.broadcast_to(column, (256, 128))

    for dx in range(3):
        for dz in range(3):
            k = 3 * dx + dz
            stack = jnp.concatenate(
                [w3[9 * dx + 3 * dy + dz] for dy in range(3)] + [jnp.zeros((32, 64), BF)], axis=0
            )
            wc3[k * 64 : k * 64 + 64, :] = mm_t(table("unit", 64, 64), stack).astype(BF)
    for y in range(4):
        z3[:, y * 64 : y * 64 + 64, :] = (
            mm(wc3[...], table("spread_three", 128, 128, 128 * y)).astype(BF).reshape(9, 64, 128)
        )
    gap = jnp.zeros((64, 32), F32)
    for dx in range(3):
        low, high = [], []
        for dz in range(3):
            k = 3 * dx + dz
            t3[dx, :, dz * 128 : dz * 128 + 128] = mm(table("order_three", 256, 256), z3[k]).astype(BF)
            block = wc3[k * 64 : k * 64 + 64, :].astype(F32)
            low.append(block[:, 0:32])
            high.append(block[:, 64:96])
        z_edge = jnp.concatenate(
            [
                jnp.concatenate([low[0], gap, low[1], gap, low[2], gap, gap, gap], axis=1),
                jnp.concatenate([gap, high[0], gap, high[1], gap, high[2], gap, gap], axis=1),
            ],
            axis=0,
        ).astype(BF)
        t3[dx, :, 384:640] = mm(table("edge_three", 256, 128), z_edge).astype(BF)
    row = lax.broadcasted_iota(jnp.int32, (256, 64), 0) // 4
    lane = lax.broadcasted_iota(jnp.int32, (256, 64), 1)
    column = jnp.sum(jnp.where(row == lane, b3[...], 0.0), axis=1, keepdims=True)
    bias3[...] = jnp.broadcast_to(column, (256, 128))

    w4[:, 3, :, 0:128] = jnp.zeros((9, 64, 128), BF)
    w4[:, 0, :, 128:256] = jnp.zeros((9, 64, 128), BF)
    turn[...] = table("turn_four", 384, 128)

    fm[0:768, 0:128] = jnp.zeros((768, 128), BF)
    fm[0:768, 1152:1280] = jnp.zeros((768, 128), BF)
    fm[960:1024, :] = jnp.zeros((64, 1280), BF)

    def inner(p, carry):
        acc = jnp.zeros((256, 256), F32)
        for dx in range(3):
            lanes = pl.ds(pl.multiple_of((p * 2 + dx) * 128, 128), 256)
            acc = acc + mm(t2[dx, :, 0:768], fm[0:768, lanes])
        a2[p] = acc
        return carry

    lax.fori_loop(0, 4, inner, 0)

    for copy in first:
        copy.wait()
    for x in (0, 9):
        place(x)
        shift(x)
    a2[0, :, 0:128] += mm(t2[0, :, 0:768], fm[0:768, 0:128])
    a2[3, :, 128:256] += mm(t2[2, :, 0:768], fm[0:768, 1152:1280])
    for copy in second:
        copy.wait()
    for x in range(10):
        v = jnp.concatenate([hr[0, x], hr[1, x]], axis=0).astype(F32)
        lanes = slice(x * 128, x * 128 + 128)
        fm[768:832, lanes] = pltpu.roll(v, 1, 1).astype(BF)
        fm[832:896, lanes] = v.astype(BF)
        fm[896:960, lanes] = pltpu.roll(v, 127, 1).astype(BF)

    third = []
    for q in range(2):
        total = jnp.zeros((256, 128), F32)
        for half in range(2):
            p = 2 * q + half
            acc = a2[p]
            for dx in range(3):
                lanes = slice((p * 2 + dx) * 128, (p * 2 + dx + 2) * 128)
                acc = acc + mm(t2[dx, :, 768:1024], fm[768:1024, lanes])
            for x in range(2):
                v = leaky(acc[:, x * 128 : x * 128 + 128] + bias2[...])
                out2[:, 2 * p + x] = v.reshape(32, 8, 128).astype(BF)
                total = total + mm(v.astype(BF), table("pool_two", 128, 128, half * 256 + x * 128))
        pooled[...] = total
        own3[q + 1] = (pooled[pl.ds(0, 128, stride=2), :] + pooled[pl.ds(1, 128, stride=2), :]).astype(BF)
        far, slot = (xm, 3) if q == 0 else (xp, 0)
        base = 5 * q
        picked = mm(table("select_three", 64, 128), own3[q + 1]).astype(BF)
        hs3[0, q] = picked[0:32]
        hs3[1, q] = picked[32:64]
        copies = [
            remote(hs3.at[1, q], hr3.at[0, slot], send3_sem.at[base], recv3_sem.at[base], far, yp),
            remote(hs3.at[0, q], hr3.at[1, slot], send3_sem.at[base + 1], recv3_sem.at[base + 1], far, ym),
            remote(own3.at[q + 1], own3.at[slot], send3_sem.at[base + 2], recv3_sem.at[base + 2], far, gy),
            remote(hs3.at[1, q], hr3.at[0, q + 1], send3_sem.at[base + 3], recv3_sem.at[base + 3], gx, yp),
            remote(hs3.at[0, q], hr3.at[1, q + 1], send3_sem.at[base + 4], recv3_sem.at[base + 4], gx, ym),
        ]
        for copy in copies:
            copy.start()
        third += copies
    d3[576:640, :] = jnp.zeros((64, 640), BF)
    for copy in third:
        copy.wait()
    tiles = []
    for t in range(4):
        tiles.append(
            jnp.concatenate([own3[t], hr3[0, t], hr3[1, t]], axis=0).astype(F32)
        )
    turned = [pltpu.roll(v, 64, 1) for v in tiles]
    lane = lax.broadcasted_iota(jnp.int32, (192, 128), 1)
    between = [jnp.where(lane < 64, turned[t], turned[t + 1]) for t in range(3)]
    for slot, v in enumerate([tiles[1], tiles[2]] + between):
        lanes = slice(slot * 128, slot * 128 + 128)
        for dz, u in enumerate((rolled_64(v, True), v, rolled_64(v, False))):
            u = u.astype(BF)
            d3[dz * 128 : dz * 128 + 128, lanes] = u[0:128]
            d3[384 + dz * 64 : 448 + dz * 64, lanes] = u[128:192]
    acc = mm(t3[0], d3[:, 256:512]) + mm(t3[1], d3[:, 0:256]) + mm(t3[2], d3[:, 384:640])
    for q in range(2):
        v = leaky(acc[:, q * 128 : q * 128 + 128] + bias3[...])
        l3[:, q * 128 : q * 128 + 128] = v.astype(BF)
        out3[:, 2 * q] = v[:, 0:64].reshape(64, 4, 64).astype(BF)
        out3[:, 2 * q + 1] = v[:, 64:128].reshape(64, 4, 64).astype(BF)

    sums = mm_t(table("pick_four", 256, 256), l3[...])
    row = lax.broadcasted_iota(jnp.int32, (256, 256), 0) % 2
    lane = lax.broadcasted_iota(jnp.int32, (256, 256), 1) % 4 // 2
    sums = jnp.where(row == lane, sums, 0.0)
    head = sums.astype(BF)
    tail = (sums - head.astype(F32)).astype(BF)
    block = jnp.zeros((128, 128), F32)
    for odd in range(2):
        g = table("gather_four", 256, 128, odd * 256)
        block = block + mm(head[odd * 128 : odd * 128 + 128], g) + mm(tail[odd * 128 : odd * 128 + 128], g)
    sa[...] = block.reshape(16, 8, 128).astype(BF)
    rb[gx, gy] = sa[gy]

    def send_a(k, carry):
        target = lax.rem(gy + k, 16)
        remote(sa.at[target], rb.at[gx, gy], senda_sem, recva_sem, gx, target).start()
        return carry

    lax.fori_loop(1, 16, send_a, 0)
    pltpu.make_async_copy(rb.at[gx, 0:15], rb.at[gx, 0:15], recva_sem).wait()

    def send_b(k, carry):
        target = lax.rem(gx + k, 8)
        remote(rb.at[gx], rb.at[gx], sendb_sem, recvb_sem, target, gy).start()
        return carry

    lax.fori_loop(1, 8, send_b, 0)
    pltpu.make_async_copy(sa.at[0:15], sa.at[0:15], senda_sem).wait()
    pltpu.make_async_copy(rb.at[0:7], rb.at[0:7], recvb_sem).wait()

    pltpu.make_async_copy(rb.at[0:7], rb.at[0:7], sendb_sem).wait()


def last(out2_in, out3_in, rb, w4, turn, b4, out2, out3, out4, pp, l4, sem):
    leaving = [
        pltpu.make_async_copy(out2_in, out2, sem.at[0]),
        pltpu.make_async_copy(out3_in, out3, sem.at[1]),
    ]
    for copy in leaving:
        copy.start()
    for x in range(8):
        v = rb[x].astype(F32).reshape(128, 128).astype(BF)
        moved = mm(turn[...], v).astype(BF)
        for dy in range(3):
            for half in range(2):
                start = (dy * 2 + half) * 64
                pp[dy, (1 + 2 * x) * 32 : (3 + 2 * x) * 32, half * 128 : half * 128 + 128] = moved[start : start + 64]
    pp[:, 0:32, :] = pp[:, 512:544, :]
    pp[:, 544:576, :] = pp[:, 32:64, :]
    bias = jnp.concatenate([b4[...], b4[...]], axis=1)
    for m in range(2):
        acc = jnp.zeros((256, 256), F32)
        for dx in range(3):
            for dy in range(3):
                rows = slice(m * 256 + dx * 32, m * 256 + dx * 32 + 256)
                acc = acc + mm(pp[dy, rows, :], w4[3 * dx + dy].reshape(256, 256))
        v = leaky(acc + bias)
        l4[m * 256 : m * 256 + 256] = v.reshape(256, 2, 128).astype(BF)
        piece = pl.ds(m * 256, 256)
        leaving.append(pltpu.make_async_copy(l4.at[piece], out4.at[piece], sem.at[2 + m]))
        leaving[-1].start()
    for copy in leaving:
        copy.wait()


def shards(features, weight_two, bias_two, weight_three, bias_three, weight_four, bias_four):
    vm = pl.BlockSpec(memory_space=pltpu.VMEM)
    hbm = pl.BlockSpec(memory_space=pltpu.HBM)
    table = jnp.asarray(TABLE)
    w3 = weight_three.transpose(0, 2, 1)
    w4 = weight_four.transpose(0, 2, 1).reshape(9, 3, 64, 128)
    dma = pltpu.SemaphoreType.DMA
    held = pl.pallas_call(
        kernel,
        out_shape=(
            jax.ShapeDtypeStruct((32, 8, 8, 128), BF),
            jax.ShapeDtypeStruct((64, 4, 4, 64), BF),
            jax.ShapeDtypeStruct((8, 16, 8, 128), BF),
            jax.ShapeDtypeStruct((9, 4, 64, 256), BF),
            jax.ShapeDtypeStruct((384, 128), BF),
            jax.ShapeDtypeStruct((1, 128), F32),
        ),
        in_specs=[hbm] * 8,
        out_specs=(vm,) * 6,
        scratch_shapes=[
            pltpu.VMEM((10, 32, 8, 128), BF),
            pltpu.VMEM((1024, 1280), BF),
            pltpu.VMEM((2, 8, 32, 128), BF),
            pltpu.VMEM((2, 10, 32, 128), BF),
            pltpu.VMEM((27, 32, 32), BF),
            pltpu.VMEM((27, 32, 64), BF),
            pltpu.VMEM((1, 32), F32),
            pltpu.VMEM((1, 64), F32),
            pltpu.VMEM(TABLE.shape, BF),
            pltpu.VMEM((288, 128), BF),
            pltpu.VMEM((9, 256, 256), BF),
            pltpu.VMEM((3, 256, 1024), BF),
            pltpu.VMEM((4, 256, 256), F32),
            pltpu.VMEM((576, 128), BF),
            pltpu.VMEM((9, 256, 128), BF),
            pltpu.VMEM((3, 256, 640), BF),
            pltpu.VMEM((256, 128), F32),
            pltpu.VMEM((256, 128), F32),
            pltpu.VMEM((256, 128), F32),
            pltpu.VMEM((4, 128, 128), BF),
            pltpu.VMEM((2, 2, 32, 128), BF),
            pltpu.VMEM((2, 4, 32, 128), BF),
            pltpu.VMEM((640, 640), BF),
            pltpu.VMEM((256, 256), BF),
            pltpu.VMEM((16, 8, 128), BF),
            dma((8,)), dma((8,)), dma((8,)), dma((8,)), dma((10,)), dma((10,)),
            dma, dma, dma, dma,
        ],
        compiler_params=pltpu.CompilerParams(
            collective_id=0, has_side_effects=True, vmem_limit_bytes=40 * 1024 * 1024
        ),
    )(
        *(
            pltpu.with_memory_space_constraint(a, pltpu.HBM)
            for a in (features, weight_two, bias_two[None], w3, bias_three[None], w4, bias_four[None], table)
        )
    )
    level_two, level_three, bottleneck = pl.pallas_call(
        last,
        out_shape=(
            jax.ShapeDtypeStruct((32, 8, 8, 128), BF),
            jax.ShapeDtypeStruct((64, 4, 4, 64), BF),
            jax.ShapeDtypeStruct((512, 2, 128), BF),
        ),
        in_specs=[vm] * 6,
        out_specs=(hbm,) * 3,
        scratch_shapes=[
            pltpu.VMEM((3, 576, 256), BF),
            pltpu.VMEM((512, 2, 128), BF),
            dma((4,)),
        ],
        compiler_params=pltpu.CompilerParams(vmem_limit_bytes=40 * 1024 * 1024),
    )(*held)
    return level_two, level_three, bottleneck.reshape(16, 32, 2, 128).transpose(3, 0, 1, 2)


def solution(mesh):
    return jax.shard_map(
        shards,
        mesh=mesh,
        in_specs=(P(None, "gx", "gy", None), P(), P(), P(), P(), P(), P()),
        out_specs=(P(None, "gx", "gy", None), P(None, "gx", "gy", None), P(None, None, None, "gy")),
        check_vma=False,
    )
```

```python
import functools

import jax
import jax.numpy as jnp
import numpy as np
from jax import lax
from jax.experimental import pallas as pl
from jax.experimental.pallas import tpu as pltpu
from jax.sharding import PartitionSpec as P

BF = jnp.bfloat16
F32 = jnp.float32
MESH = pl.DeviceIdType.MESH


def tables():
    parts, at, row = [], {}, 0

    def add(name, matrix):
        nonlocal row
        rows, lanes = matrix.shape
        full = np.zeros((-(-rows // 16) * 16, 256), np.float32)
        full[:rows, :lanes] = matrix
        at[name] = row
        parts.append(full)
        row += full.shape[0]

    spread = np.zeros((8, 128, 256))
    for y in range(8):
        for dy in range(3):
            if 0 <= y + dy - 1 < 8:
                for c in range(32):
                    spread[y, dy * 32 + c, c * 8 + y + dy - 1] = 1
    add("spread_two", spread.reshape(1024, 256))
    order = np.zeros((256, 256))
    for y in range(8):
        for o in range(32):
            order[o * 8 + y, y * 32 + o] = 1
    add("order_two", order)
    edge = np.zeros((256, 64))
    for o in range(32):
        edge[o * 8, o] = 1
        edge[o * 8 + 7, 32 + o] = 1
    add("edge_two", edge)
    pool = np.zeros((2, 2, 128, 128))
    for half in range(2):
        for x in range(2):
            for z in range(128):
                pool[half, x, z, half * 64 + z // 2] = 0.125
    add("pool_two", pool.reshape(512, 128))
    select = np.zeros((64, 128))
    for c in range(32):
        select[c, c * 4] = 1
        select[32 + c, c * 4 + 3] = 1
    add("select_three", select)
    add("unit", np.eye(64))
    spread = np.zeros((4, 128, 128))
    for y in range(4):
        for dy in range(3):
            if 0 <= y + dy - 1 < 4:
                for c in range(32):
                    spread[y, dy * 32 + c, c * 4 + y + dy - 1] = 1
    add("spread_three", spread.reshape(512, 128))
    order = np.zeros((256, 256))
    for y in range(4):
        for o in range(64):
            order[o * 4 + y, y * 64 + o] = 1
    add("order_three", order)
    edge = np.zeros((256, 128))
    for o in range(64):
        edge[o * 4, o] = 1
        edge[o * 4 + 3, 64 + o] = 1
    add("edge_three", edge)
    pick = np.zeros((2, 16, 2, 2, 2, 4, 64))
    for odd in range(2):
        for target in range(16):
            for half in range(2):
                z = (2 * target - 1 + 2 * half + odd) % 32
                for x in range(2):
                    pick[odd, target, half, x, :, 2 * x : 2 * x + 2, 2 * z : 2 * z + 2] = 0.125
    add("pick_four", pick.reshape(256, 256))
    gather = np.zeros((2, 256, 128))
    for odd in range(2):
        for o in range(64):
            gather[odd, o * 4 : o * 4 + 4, odd * 64 + o] = 1
    add("gather_four", gather.reshape(512, 128))
    turn = np.zeros((3, 2, 2, 32, 16, 2, 2, 2))
    for dy in range(3):
        for half in range(2):
            for x in range(2):
                for y in range(32):
                    source = (y + dy - 1) % 32
                    turn[dy, half, x, y, source // 2, half, x, source % 2] = 1
    add("turn_four", turn.reshape(384, 128))
    return np.concatenate(parts).astype(jnp.bfloat16), at


TABLE, AT = tables()


def mm(a, b):
    return jnp.dot(a, b, preferred_element_type=F32)


def mm_t(a, b):
    return lax.dot_general(a, b, (((1,), (1,)), ((), ())), preferred_element_type=F32)


def leaky(t):
    return jnp.maximum(t, 0.1 * t)


def rolled_64(v, back):
    lane = lax.broadcasted_iota(jnp.int32, v.shape, 1) % 64
    if back:
        return jnp.where(lane == 0, pltpu.roll(v, 65, 1), pltpu.roll(v, 1, 1))
    return jnp.where(lane == 63, pltpu.roll(v, 63, 1), pltpu.roll(v, 127, 1))


def kernel(
    feat, w2_in, b2_in, w3_in, b3_in, w4_in, b4_in, tab_in,
    out2, out3, rb, w4, turn, b4,
    fx, fm, hs, hr, w2, w3, b2, b3, tab, wc2, z2, t2, a2, wc3, z3, t3, bias2, bias3,
    pooled, own3, hs3, hr3, d3, l3, sa,
    load_sem, feat_sem, send_sem, recv_sem, send3_sem, recv3_sem, senda_sem, recva_sem, wide_sem,
):
    gx, gy = lax.axis_index("gx"), lax.axis_index("gy")
    xp, xm = lax.rem(gx + 1, 8), lax.rem(gx + 7, 8)
    yp, ym = lax.rem(gy + 1, 16), lax.rem(gy + 15, 16)

    def table(name, rows, lanes, skip=0):
        start = AT[name] + skip
        return tab[start : start + rows, :lanes]

    barrier = pltpu.get_barrier_semaphore()

    def greet(semaphore, dx, dy):
        pl.semaphore_signal(
            semaphore, inc=1, device_id=(lax.rem(gx + dx + 8, 8), lax.rem(gy + dy + 16, 16)), device_id_type=MESH
        )

    around = [(dx, dy) for dx in (-1, 0, 1) for dy in (-1, 0, 1) if dx or dy]
    for dx, dy in around:
        greet(barrier, dx, dy)

    loads = [
        pltpu.make_async_copy(feat.at[:, x], fx.at[x + 1], feat_sem.at[x]) for x in range(8)
    ]
    others = [
        pltpu.make_async_copy(tab_in, tab, load_sem.at[0]),
        pltpu.make_async_copy(w2_in, w2, load_sem.at[1]),
        pltpu.make_async_copy(b2_in, b2, load_sem.at[2]),
        pltpu.make_async_copy(w3_in, w3, load_sem.at[3]),
        pltpu.make_async_copy(b3_in, b3, load_sem.at[4]),
        pltpu.make_async_copy(b4_in, b4, load_sem.at[5]),
        pltpu.make_async_copy(w4_in, w4.at[:, 0:3, :, 0:128], load_sem.at[6]),
        pltpu.make_async_copy(w4_in, w4.at[:, 1:4, :, 128:256], load_sem.at[7]),
    ]
    for copy in loads:
        copy.start()
    for copy in others:
        copy.start()

    pl.semaphore_wait(barrier, 8)

    def remote(src, dst, send, recv, x, y):
        return pltpu.make_async_remote_copy(
            src_ref=src, dst_ref=dst, send_sem=send, recv_sem=recv,
            device_id=(x, y), device_id_type=MESH,
        )

    first = [
        remote(feat.at[:, 7], fx.at[0], send_sem.at[0], recv_sem.at[0], xp, gy),
        remote(feat.at[:, 0], fx.at[9], send_sem.at[1], recv_sem.at[1], xm, gy),
    ]
    for copy in first:
        copy.start()

    def place(x):
        v = fx[x].astype(F32).reshape(256, 128)
        lanes = slice(x * 128, x * 128 + 128)
        fm[256:512, lanes] = v.astype(BF)

    def shift(x):
        lanes = slice(x * 128, x * 128 + 128)
        v = fm[256:512, lanes].astype(F32)
        fm[0:256, lanes] = pltpu.roll(v, 1, 1).astype(BF)
        fm[512:768, lanes] = pltpu.roll(v, 127, 1).astype(BF)

    row = lax.broadcasted_iota(jnp.int32, (64, 256), 0)
    lane = lax.broadcasted_iota(jnp.int32, (64, 256), 1)
    select = jnp.where(lane == row % 32 * 8 + row // 32 * 7, 1.0, 0.0).astype(BF)
    for copy in loads:
        copy.wait()
    for x in range(1, 9):
        place(x)
    edges = mm(select, fm[256:512, 128:1152]).astype(BF)
    for side in range(2):
        for x in range(8):
            hs[side, x] = edges[side * 32 : side * 32 + 32, x * 128 : x * 128 + 128]
    second = [
        remote(hs.at[1, 7], hr.at[0, 0], send_sem.at[4], recv_sem.at[4], xp, yp),
        remote(hs.at[1, 0], hr.at[0, 9], send_sem.at[5], recv_sem.at[5], xm, yp),
        remote(hs.at[0, 7], hr.at[1, 0], send_sem.at[6], recv_sem.at[6], xp, ym),
        remote(hs.at[0, 0], hr.at[1, 9], send_sem.at[7], recv_sem.at[7], xm, ym),
        remote(hs.at[1], hr.at[0, 1:9], send_sem.at[2], recv_sem.at[2], gx, yp),
        remote(hs.at[0], hr.at[1, 1:9], send_sem.at[3], recv_sem.at[3], gx, ym),
    ]
    for copy in second:
        copy.start()

    for dx, dy in around:
        greet(wide_sem.at[0], dx, dy)
    for x in range(1, 9):
        shift(x)
    for copy in others:
        copy.wait()
    gap = jnp.zeros((32, 32), F32)
    for dx in range(3):
        for dz in range(3):
            k = 3 * dx + dz
            wc2[k * 32 : k * 32 + 32, :] = jnp.concatenate(
                [w2[9 * dx + 3 * dy + dz].astype(F32) for dy in range(3)] + [gap], axis=1
            ).astype(BF)
    for y in range(8):
        z2[:, y * 32 : y * 32 + 32, :] = (
            mm(wc2[...], table("spread_two", 128, 256, 128 * y)).astype(BF).reshape(9, 32, 256)
        )
    for dx in range(3):
        for dz in range(3):
            t2[dx, :, dz * 256 : dz * 256 + 256] = mm(
                table("order_two", 256, 256), z2[3 * dx + dz]
            ).astype(BF)
        low = [w2[9 * dx + dz].astype(F32) for dz in range(3)]
        high = [w2[9 * dx + 6 + dz].astype(F32) for dz in range(3)]
        z_edge = jnp.concatenate(
            [
                jnp.concatenate([low[0], gap, low[1], gap, low[2], gap, gap, gap], axis=1),
                jnp.concatenate([gap, high[0], gap, high[1], gap, high[2], gap, gap], axis=1),
            ],
            axis=0,
        ).astype(BF)
        t2[dx, :, 768:1024] = mm(table("edge_two", 256, 64), z_edge).astype(BF)
    row = lax.broadcasted_iota(jnp.int32, (256, 32), 0) // 8
    lane = lax.broadcasted_iota(jnp.int32, (256, 32), 1)
    column = jnp.sum(jnp.where(row == lane, b2[...], 0.0), axis=1, keepdims=True)
    bias2[...] = jnp.broadcast_to(column, (256, 128))

    pl.semaphore_wait(wide_sem.at[0], 8)
    for dx, dy in around:
        greet(wide_sem.at[1], 2 * dx, 2 * dy)

    for dx in range(3):
        for dz in range(3):
            k = 3 * dx + dz
            stack = jnp.concatenate(
                [w3[9 * dx + 3 * dy + dz] for dy in range(3)] + [jnp.zeros((32, 64), BF)], axis=0
            )
            wc3[k * 64 : k * 64 + 64, :] = mm_t(table("unit", 64, 64), stack).astype(BF)
    for y in range(4):
        z3[:, y * 64 : y * 64 + 64, :] = (
            mm(wc3[...], table("spread_three", 128, 128, 128 * y)).astype(BF).reshape(9, 64, 128)
        )
    gap = jnp.zeros((64, 32), F32)
    for dx in range(3):
        low, high = [], []
        for dz in range(3):
            k = 3 * dx + dz
            t3[dx, :, dz * 128 : dz * 128 + 128] = mm(table("order_three", 256, 256), z3[k]).astype(BF)
            block = wc3[k * 64 : k * 64 + 64, :].astype(F32)
            low.append(block[:, 0:32])
            high.append(block[:, 64:96])
        z_edge = jnp.concatenate(
            [
                jnp.concatenate([low[0], gap, low[1], gap, low[2], gap, gap, gap], axis=1),
                jnp.concatenate([gap, high[0], gap, high[1], gap, high[2], gap, gap], axis=1),
            ],
            axis=0,
        ).astype(BF)
        t3[dx, :, 384:640] = mm(table("edge_three", 256, 128), z_edge).astype(BF)
    row = lax.broadcasted_iota(jnp.int32, (256, 64), 0) // 4
    lane = lax.broadcasted_iota(jnp.int32, (256, 64), 1)
    column = jnp.sum(jnp.where(row == lane, b3[...], 0.0), axis=1, keepdims=True)
    bias3[...] = jnp.broadcast_to(column, (256, 128))

    w4[:, 3, :, 0:128] = jnp.zeros((9, 64, 128), BF)
    w4[:, 0, :, 128:256] = jnp.zeros((9, 64, 128), BF)
    turn[...] = table("turn_four", 384, 128)

    pl.semaphore_wait(wide_sem.at[1], 8)
    for dy in (-4, 4):
        greet(wide_sem.at[2], 0, dy)

    fm[0:768, 0:128] = jnp.zeros((768, 128), BF)
    fm[0:768, 1152:1280] = jnp.zeros((768, 128), BF)
    fm[960:1024, :] = jnp.zeros((64, 1280), BF)

    def inner(p, carry):
        acc = jnp.zeros((256, 256), F32)
        for dx in range(3):
            lanes = pl.ds(pl.multiple_of((p * 2 + dx) * 128, 128), 256)
            acc = acc + mm(t2[dx, :, 0:768], fm[0:768, lanes])
        a2[p] = acc
        return carry

    lax.fori_loop(0, 4, inner, 0)

    for copy in first:
        copy.wait()
    for x in (0, 9):
        place(x)
        shift(x)
    a2[0, :, 0:128] += mm(t2[0, :, 0:768], fm[0:768, 0:128])
    a2[3, :, 128:256] += mm(t2[2, :, 0:768], fm[0:768, 1152:1280])
    for copy in second:
        copy.wait()
    for x in range(10):
        v = jnp.concatenate([hr[0, x], hr[1, x]], axis=0).astype(F32)
        lanes = slice(x * 128, x * 128 + 128)
        fm[768:832, lanes] = pltpu.roll(v, 1, 1).astype(BF)
        fm[832:896, lanes] = v.astype(BF)
        fm[896:960, lanes] = pltpu.roll(v, 127, 1).astype(BF)

    third = []
    for q in range(2):
        total = jnp.zeros((256, 128), F32)
        for half in range(2):
            p = 2 * q + half
            acc = a2[p]
            for dx in range(3):
                lanes = slice((p * 2 + dx) * 128, (p * 2 + dx + 2) * 128)
                acc = acc + mm(t2[dx, :, 768:1024], fm[768:1024, lanes])
            for x in range(2):
                v = leaky(acc[:, x * 128 : x * 128 + 128] + bias2[...])
                out2[:, 2 * p + x] = v.reshape(32, 8, 128).astype(BF)
                total = total + mm(v.astype(BF), table("pool_two", 128, 128, half * 256 + x * 128))
        pooled[...] = total
        own3[q + 1] = (pooled[pl.ds(0, 128, stride=2), :] + pooled[pl.ds(1, 128, stride=2), :]).astype(BF)
        far, slot = (xm, 3) if q == 0 else (xp, 0)
        base = 5 * q
        picked = mm(table("select_three", 64, 128), own3[q + 1]).astype(BF)
        hs3[0, q] = picked[0:32]
        hs3[1, q] = picked[32:64]
        copies = [
            remote(hs3.at[1, q], hr3.at[0, slot], send3_sem.at[base], recv3_sem.at[base], far, yp),
            remote(hs3.at[0, q], hr3.at[1, slot], send3_sem.at[base + 1], recv3_sem.at[base + 1], far, ym),
            remote(own3.at[q + 1], own3.at[slot], send3_sem.at[base + 2], recv3_sem.at[base + 2], far, gy),
            remote(hs3.at[1, q], hr3.at[0, q + 1], send3_sem.at[base + 3], recv3_sem.at[base + 3], gx, yp),
            remote(hs3.at[0, q], hr3.at[1, q + 1], send3_sem.at[base + 4], recv3_sem.at[base + 4], gx, ym),
        ]
        for copy in copies:
            copy.start()
        third += copies
    d3[576:640, :] = jnp.zeros((64, 640), BF)
    for copy in third:
        copy.wait()
    tiles = []
    for t in range(4):
        tiles.append(
            jnp.concatenate([own3[t], hr3[0, t], hr3[1, t]], axis=0).astype(F32)
        )
    turned = [pltpu.roll(v, 64, 1) for v in tiles]
    lane = lax.broadcasted_iota(jnp.int32, (192, 128), 1)
    between = [jnp.where(lane < 64, turned[t], turned[t + 1]) for t in range(3)]
    for slot, v in enumerate([tiles[1], tiles[2]] + between):
        lanes = slice(slot * 128, slot * 128 + 128)
        for dz, u in enumerate((rolled_64(v, True), v, rolled_64(v, False))):
            u = u.astype(BF)
            d3[dz * 128 : dz * 128 + 128, lanes] = u[0:128]
            d3[384 + dz * 64 : 448 + dz * 64, lanes] = u[128:192]
    acc = mm(t3[0], d3[:, 256:512]) + mm(t3[1], d3[:, 0:256]) + mm(t3[2], d3[:, 384:640])
    for q in range(2):
        v = leaky(acc[:, q * 128 : q * 128 + 128] + bias3[...])
        l3[:, q * 128 : q * 128 + 128] = v.astype(BF)
        out3[:, 2 * q] = v[:, 0:64].reshape(64, 4, 64).astype(BF)
        out3[:, 2 * q + 1] = v[:, 64:128].reshape(64, 4, 64).astype(BF)

    sums = mm_t(table("pick_four", 256, 256), l3[...])
    row = lax.broadcasted_iota(jnp.int32, (256, 256), 0) % 2
    lane = lax.broadcasted_iota(jnp.int32, (256, 256), 1) % 4 // 2
    sums = jnp.where(row == lane, sums, 0.0)
    head = sums.astype(BF)
    tail = (sums - head.astype(F32)).astype(BF)
    block = jnp.zeros((128, 128), F32)
    for odd in range(2):
        g = table("gather_four", 256, 128, odd * 256)
        block = block + mm(head[odd * 128 : odd * 128 + 128], g) + mm(tail[odd * 128 : odd * 128 + 128], g)
    sa[...] = block.reshape(16, 8, 128).astype(BF)
    pl.semaphore_wait(wide_sem.at[2], 2)
    me = gx * 16 + gy
    mine = pltpu.make_async_copy(sa.at[gy], rb.at[me], recva_sem)
    y_at, x_at, z_at, core_at = gx // 4 * 2 + gy // 8, gx % 4, gy // 2 % 4, gy % 2
    columns, layers = {}, {}
    for d in range(4):
        y = (y_at + d) % 4
        for e in range(4):
            columns[e, d] = y // 2 * 4 + (x_at + e) % 4
            layers[d, e] = y % 2 * 8 + (z_at + e) % 4 * 2
    hops = (0, 1, 2, 1)
    steps = [(dx, dy, dz) for dx in range(4) for dy in range(4) for dz in range(4)]
    steps.sort(key=lambda step: -sum(hops[d] for d in step))
    for dx, dy, dz in steps:
        for flip in range(2):
            if dx or dy or dz or flip:
                layer = layers[dy, dz] + (core_at + flip) % 2
                remote(sa.at[layer], rb.at[me], senda_sem, recva_sem, columns[dx, dy], layer).start()
    mine.start()
    pltpu.make_async_copy(rb, rb, recva_sem).wait()
    pltpu.make_async_copy(rb.at[0:127], rb.at[0:127], senda_sem).wait()


def last(out2_in, out3_in, rb, w4, turn, b4, out2, out3, out4, pp, l4, sem):
    leaving = [
        pltpu.make_async_copy(out2_in, out2, sem.at[0]),
        pltpu.make_async_copy(out3_in, out3, sem.at[1]),
    ]
    for copy in leaving:
        copy.start()
    for x in range(8):
        v = rb[x * 16 : x * 16 + 16].astype(F32).reshape(128, 128).astype(BF)
        moved = mm(turn[...], v).astype(BF)
        for dy in range(3):
            for half in range(2):
                start = (dy * 2 + half) * 64
                pp[dy, (1 + 2 * x) * 32 : (3 + 2 * x) * 32, half * 128 : half * 128 + 128] = moved[start : start + 64]
    pp[:, 0:32, :] = pp[:, 512:544, :]
    pp[:, 544:576, :] = pp[:, 32:64, :]
    bias = jnp.concatenate([b4[...], b4[...]], axis=1)
    for m in range(2):
        acc = jnp.zeros((256, 256), F32)
        for dx in range(3):
            for dy in range(3):
                rows = slice(m * 256 + dx * 32, m * 256 + dx * 32 + 256)
                acc = acc + mm(pp[dy, rows, :], w4[3 * dx + dy].reshape(256, 256))
        v = leaky(acc + bias)
        l4[m * 256 : m * 256 + 256] = v.reshape(256, 2, 128).astype(BF)
        piece = pl.ds(m * 256, 256)
        leaving.append(pltpu.make_async_copy(l4.at[piece], out4.at[piece], sem.at[2 + m]))
        leaving[-1].start()
    for copy in leaving:
        copy.wait()


def shards(features, weight_two, bias_two, weight_three, bias_three, weight_four, bias_four):
    vm = pl.BlockSpec(memory_space=pltpu.VMEM)
    hbm = pl.BlockSpec(memory_space=pltpu.HBM)
    table = jnp.asarray(TABLE)
    w3 = weight_three.transpose(0, 2, 1)
    w4 = weight_four.transpose(0, 2, 1).reshape(9, 3, 64, 128)
    dma = pltpu.SemaphoreType.DMA
    held = pl.pallas_call(
        kernel,
        out_shape=(
            jax.ShapeDtypeStruct((32, 8, 8, 128), BF),
            jax.ShapeDtypeStruct((64, 4, 4, 64), BF),
            jax.ShapeDtypeStruct((128, 8, 128), BF),
            jax.ShapeDtypeStruct((9, 4, 64, 256), BF),
            jax.ShapeDtypeStruct((384, 128), BF),
            jax.ShapeDtypeStruct((1, 128), F32),
        ),
        in_specs=[hbm] * 8,
        out_specs=(vm,) * 6,
        scratch_shapes=[
            pltpu.VMEM((10, 32, 8, 128), BF),
            pltpu.VMEM((1024, 1280), BF),
            pltpu.VMEM((2, 8, 32, 128), BF),
            pltpu.VMEM((2, 10, 32, 128), BF),
            pltpu.VMEM((27, 32, 32), BF),
            pltpu.VMEM((27, 32, 64), BF),
            pltpu.VMEM((1, 32), F32),
            pltpu.VMEM((1, 64), F32),
            pltpu.VMEM(TABLE.shape, BF),
            pltpu.VMEM((288, 128), BF),
            pltpu.VMEM((9, 256, 256), BF),
            pltpu.VMEM((3, 256, 1024), BF),
            pltpu.VMEM((4, 256, 256), F32),
            pltpu.VMEM((576, 128), BF),
            pltpu.VMEM((9, 256, 128), BF),
            pltpu.VMEM((3, 256, 640), BF),
            pltpu.VMEM((256, 128), F32),
            pltpu.VMEM((256, 128), F32),
            pltpu.VMEM((256, 128), F32),
            pltpu.VMEM((4, 128, 128), BF),
            pltpu.VMEM((2, 2, 32, 128), BF),
            pltpu.VMEM((2, 4, 32, 128), BF),
            pltpu.VMEM((640, 640), BF),
            pltpu.VMEM((256, 256), BF),
            pltpu.VMEM((16, 8, 128), BF),
            dma((8,)), dma((8,)), dma((8,)), dma((8,)), dma((10,)), dma((10,)),
            dma, dma, pltpu.SemaphoreType.REGULAR((3,)),
        ],
        compiler_params=pltpu.CompilerParams(
            collective_id=0, has_side_effects=True, vmem_limit_bytes=40 * 1024 * 1024
        ),
    )(
        *(
            pltpu.with_memory_space_constraint(a, pltpu.HBM)
            for a in (features, weight_two, bias_two[None], w3, bias_three[None], w4, bias_four[None], table)
        )
    )
    level_two, level_three, bottleneck = pl.pallas_call(
        last,
        out_shape=(
            jax.ShapeDtypeStruct((32, 8, 8, 128), BF),
            jax.ShapeDtypeStruct((64, 4, 4, 64), BF),
            jax.ShapeDtypeStruct((512, 2, 128), BF),
        ),
        in_specs=[vm] * 6,
        out_specs=(hbm,) * 3,
        scratch_shapes=[
            pltpu.VMEM((3, 576, 256), BF),
            pltpu.VMEM((512, 2, 128), BF),
            dma((4,)),
        ],
        compiler_params=pltpu.CompilerParams(vmem_limit_bytes=40 * 1024 * 1024),
    )(*held)
    return level_two, level_three, bottleneck.reshape(16, 32, 2, 128).transpose(3, 0, 1, 2)


def solution(mesh):
    return jax.shard_map(
        shards,
        mesh=mesh,
        in_specs=(P(None, "gx", "gy", None), P(), P(), P(), P(), P(), P()),
        out_specs=(P(None, "gx", "gy", None), P(None, "gx", "gy", None), P(None, None, None, "gy")),
        check_vma=False,
    )
```

```python
import functools

import jax
import jax.numpy as jnp
import numpy as np
from jax import lax
from jax.experimental import pallas as pl
from jax.experimental.pallas import tpu as pltpu
from jax.sharding import PartitionSpec as P

BF = jnp.bfloat16
F32 = jnp.float32
MESH = pl.DeviceIdType.MESH


def tables():
    parts, at, row = [], {}, 0

    def add(name, matrix):
        nonlocal row
        rows, lanes = matrix.shape
        full = np.zeros((-(-rows // 16) * 16, 256), np.float32)
        full[:rows, :lanes] = matrix
        at[name] = row
        parts.append(full)
        row += full.shape[0]

    spread = np.zeros((8, 128, 256))
    for y in range(8):
        for dy in range(3):
            if 0 <= y + dy - 1 < 8:
                for c in range(32):
                    spread[y, dy * 32 + c, c * 8 + y + dy - 1] = 1
    add("spread_two", spread.reshape(1024, 256))
    order = np.zeros((256, 256))
    for y in range(8):
        for o in range(32):
            order[o * 8 + y, y * 32 + o] = 1
    add("order_two", order)
    edge = np.zeros((256, 64))
    for o in range(32):
        edge[o * 8, o] = 1
        edge[o * 8 + 7, 32 + o] = 1
    add("edge_two", edge)
    pool = np.zeros((2, 2, 128, 128))
    for half in range(2):
        for x in range(2):
            for z in range(128):
                pool[half, x, z, half * 64 + z // 2] = 0.125
    add("pool_two", pool.reshape(512, 128))
    select = np.zeros((64, 128))
    for c in range(32):
        select[c, c * 4] = 1
        select[32 + c, c * 4 + 3] = 1
    add("select_three", select)
    add("unit", np.eye(64))
    spread = np.zeros((4, 128, 128))
    for y in range(4):
        for dy in range(3):
            if 0 <= y + dy - 1 < 4:
                for c in range(32):
                    spread[y, dy * 32 + c, c * 4 + y + dy - 1] = 1
    add("spread_three", spread.reshape(512, 128))
    order = np.zeros((256, 256))
    for y in range(4):
        for o in range(64):
            order[o * 4 + y, y * 64 + o] = 1
    add("order_three", order)
    edge = np.zeros((256, 128))
    for o in range(64):
        edge[o * 4, o] = 1
        edge[o * 4 + 3, 64 + o] = 1
    add("edge_three", edge)
    pick = np.zeros((2, 16, 2, 2, 2, 4, 64))
    for odd in range(2):
        for target in range(16):
            for half in range(2):
                z = (2 * target - 1 + 2 * half + odd) % 32
                for x in range(2):
                    pick[odd, target, half, x, :, 2 * x : 2 * x + 2, 2 * z : 2 * z + 2] = 0.125
    add("pick_four", pick.reshape(256, 256))
    gather = np.zeros((2, 256, 128))
    for odd in range(2):
        for o in range(64):
            gather[odd, o * 4 : o * 4 + 4, odd * 64 + o] = 1
    add("gather_four", gather.reshape(512, 128))
    turn = np.zeros((3, 2, 2, 32, 16, 2, 2, 2))
    for dy in range(3):
        for half in range(2):
            for x in range(2):
                for y in range(32):
                    source = (y + dy - 1) % 32
                    turn[dy, half, x, y, source // 2, half, x, source % 2] = 1
    add("turn_four", turn.reshape(384, 128))
    return np.concatenate(parts).astype(jnp.bfloat16), at


TABLE, AT = tables()


def mm(a, b):
    return jnp.dot(a, b, preferred_element_type=F32)


def mm_t(a, b):
    return lax.dot_general(a, b, (((1,), (1,)), ((), ())), preferred_element_type=F32)


def leaky(t):
    return jnp.maximum(t, 0.1 * t)


def rolled_64(v, back):
    lane = lax.broadcasted_iota(jnp.int32, v.shape, 1) % 64
    if back:
        return jnp.where(lane == 0, pltpu.roll(v, 65, 1), pltpu.roll(v, 1, 1))
    return jnp.where(lane == 63, pltpu.roll(v, 63, 1), pltpu.roll(v, 127, 1))


def kernel(
    feat, w2_in, b2_in, w3_in, b3_in, w4_in, b4_in, tab_in,
    out2, out3, rb, w4, turn, b4,
    fx, fm, hs, hr, w2, w3, b2, b3, tab, wc2, z2, t2, a2, wc3, z3, t3, bias2, bias3,
    pooled, own3, hs3, hr3, d3, l3, sa,
    load_sem, feat_sem, send_sem, recv_sem, send3_sem, recv3_sem, senda_sem, recva_sem, wide_sem,
):
    gx, gy = lax.axis_index("gx"), lax.axis_index("gy")
    xp, xm = lax.rem(gx + 1, 8), lax.rem(gx + 7, 8)
    yp, ym = lax.rem(gy + 1, 16), lax.rem(gy + 15, 16)

    def table(name, rows, lanes, skip=0):
        start = AT[name] + skip
        return tab[start : start + rows, :lanes]

    barrier = pltpu.get_barrier_semaphore()

    def greet(semaphore, dx, dy):
        pl.semaphore_signal(
            semaphore, inc=1, device_id=(lax.rem(gx + dx + 8, 8), lax.rem(gy + dy + 16, 16)), device_id_type=MESH
        )

    around = [(dx, dy) for dx in (-1, 0, 1) for dy in (-1, 0, 1) if dx or dy]
    for dx, dy in around:
        greet(barrier, dx, dy)

    loads = [
        pltpu.make_async_copy(feat.at[:, x], fx.at[x + 1], feat_sem.at[x]) for x in range(8)
    ]
    others = [
        pltpu.make_async_copy(tab_in, tab, load_sem.at[0]),
        pltpu.make_async_copy(w2_in, w2, load_sem.at[1]),
        pltpu.make_async_copy(b2_in, b2, load_sem.at[2]),
        pltpu.make_async_copy(w3_in, w3, load_sem.at[3]),
        pltpu.make_async_copy(b3_in, b3, load_sem.at[4]),
        pltpu.make_async_copy(b4_in, b4, load_sem.at[5]),
        pltpu.make_async_copy(w4_in, w4.at[:, 0:3, :, 0:128], load_sem.at[6]),
        pltpu.make_async_copy(w4_in, w4.at[:, 1:4, :, 128:256], load_sem.at[7]),
    ]
    for copy in loads:
        copy.start()
    for copy in others:
        copy.start()

    pl.semaphore_wait(barrier, 8)

    def remote(src, dst, send, recv, x, y):
        return pltpu.make_async_remote_copy(
            src_ref=src, dst_ref=dst, send_sem=send, recv_sem=recv,
            device_id=(x, y), device_id_type=MESH,
        )

    first = [
        remote(feat.at[:, 7], fx.at[0], send_sem.at[0], recv_sem.at[0], xp, gy),
        remote(feat.at[:, 0], fx.at[9], send_sem.at[1], recv_sem.at[1], xm, gy),
    ]
    for copy in first:
        copy.start()

    def place(x):
        v = fx[x].astype(F32).reshape(256, 128)
        lanes = slice(x * 128, x * 128 + 128)
        fm[256:512, lanes] = v.astype(BF)

    def shift(x):
        lanes = slice(x * 128, x * 128 + 128)
        v = fm[256:512, lanes].astype(F32)
        fm[0:256, lanes] = pltpu.roll(v, 1, 1).astype(BF)
        fm[512:768, lanes] = pltpu.roll(v, 127, 1).astype(BF)

    row = lax.broadcasted_iota(jnp.int32, (64, 256), 0)
    lane = lax.broadcasted_iota(jnp.int32, (64, 256), 1)
    select = jnp.where(lane == row % 32 * 8 + row // 32 * 7, 1.0, 0.0).astype(BF)
    for copy in loads:
        copy.wait()
    for x in range(1, 9):
        place(x)
    edges = mm(select, fm[256:512, 128:1152]).astype(BF)
    for side in range(2):
        for x in range(8):
            hs[side, x] = edges[side * 32 : side * 32 + 32, x * 128 : x * 128 + 128]
    second = [
        remote(hs.at[1, 7], hr.at[0, 0], send_sem.at[4], recv_sem.at[4], xp, yp),
        remote(hs.at[1, 0], hr.at[0, 9], send_sem.at[5], recv_sem.at[5], xm, yp),
        remote(hs.at[0, 7], hr.at[1, 0], send_sem.at[6], recv_sem.at[6], xp, ym),
        remote(hs.at[0, 0], hr.at[1, 9], send_sem.at[7], recv_sem.at[7], xm, ym),
        remote(hs.at[1], hr.at[0, 1:9], send_sem.at[2], recv_sem.at[2], gx, yp),
        remote(hs.at[0], hr.at[1, 1:9], send_sem.at[3], recv_sem.at[3], gx, ym),
    ]
    for copy in second:
        copy.start()

    for x in range(1, 9):
        shift(x)
    for copy in others:
        copy.wait()
    gap = jnp.zeros((32, 32), F32)
    for dx in range(3):
        for dz in range(3):
            k = 3 * dx + dz
            wc2[k * 32 : k * 32 + 32, :] = jnp.concatenate(
                [w2[9 * dx + 3 * dy + dz].astype(F32) for dy in range(3)] + [gap], axis=1
            ).astype(BF)
    for y in range(8):
        z2[:, y * 32 : y * 32 + 32, :] = (
            mm(wc2[...], table("spread_two", 128, 256, 128 * y)).astype(BF).reshape(9, 32, 256)
        )
    for dx in range(3):
        for dz in range(3):
            t2[dx, :, dz * 256 : dz * 256 + 256] = mm(
                table("order_two", 256, 256), z2[3 * dx + dz]
            ).astype(BF)
        low = [w2[9 * dx + dz].astype(F32) for dz in range(3)]
        high = [w2[9 * dx + 6 + dz].astype(F32) for dz in range(3)]
        z_edge = jnp.concatenate(
            [
                jnp.concatenate([low[0], gap, low[1], gap, low[2], gap, gap, gap], axis=1),
                jnp.concatenate([gap, high[0], gap, high[1], gap, high[2], gap, gap], axis=1),
            ],
            axis=0,
        ).astype(BF)
        t2[dx, :, 768:1024] = mm(table("edge_two", 256, 64), z_edge).astype(BF)
    row = lax.broadcasted_iota(jnp.int32, (256, 32), 0) // 8
    lane = lax.broadcasted_iota(jnp.int32, (256, 32), 1)
    column = jnp.sum(jnp.where(row == lane, b2[...], 0.0), axis=1, keepdims=True)
    bias2[...] = jnp.broadcast_to(column, (256, 128))

    for dx in range(3):
        for dz in range(3):
            k = 3 * dx + dz
            stack = jnp.concatenate(
                [w3[9 * dx + 3 * dy + dz] for dy in range(3)] + [jnp.zeros((32, 64), BF)], axis=0
            )
            wc3[k * 64 : k * 64 + 64, :] = mm_t(table("unit", 64, 64), stack).astype(BF)
    for y in range(4):
        z3[:, y * 64 : y * 64 + 64, :] = (
            mm(wc3[...], table("spread_three", 128, 128, 128 * y)).astype(BF).reshape(9, 64, 128)
        )
    gap = jnp.zeros((64, 32), F32)
    for dx in range(3):
        low, high = [], []
        for dz in range(3):
            k = 3 * dx + dz
            t3[dx, :, dz * 128 : dz * 128 + 128] = mm(table("order_three", 256, 256), z3[k]).astype(BF)
            block = wc3[k * 64 : k * 64 + 64, :].astype(F32)
            low.append(block[:, 0:32])
            high.append(block[:, 64:96])
        z_edge = jnp.concatenate(
            [
                jnp.concatenate([low[0], gap, low[1], gap, low[2], gap, gap, gap], axis=1),
                jnp.concatenate([gap, high[0], gap, high[1], gap, high[2], gap, gap], axis=1),
            ],
            axis=0,
        ).astype(BF)
        t3[dx, :, 384:640] = mm(table("edge_three", 256, 128), z_edge).astype(BF)
    row = lax.broadcasted_iota(jnp.int32, (256, 64), 0) // 4
    lane = lax.broadcasted_iota(jnp.int32, (256, 64), 1)
    column = jnp.sum(jnp.where(row == lane, b3[...], 0.0), axis=1, keepdims=True)
    bias3[...] = jnp.broadcast_to(column, (256, 128))

    w4[:, 3, :, 0:128] = jnp.zeros((9, 64, 128), BF)
    w4[:, 0, :, 128:256] = jnp.zeros((9, 64, 128), BF)
    turn[...] = table("turn_four", 384, 128)

    fm[0:768, 0:128] = jnp.zeros((768, 128), BF)
    fm[0:768, 1152:1280] = jnp.zeros((768, 128), BF)
    fm[960:1024, :] = jnp.zeros((64, 1280), BF)

    def inner(p, carry):
        acc = jnp.zeros((256, 256), F32)
        for dx in range(3):
            lanes = pl.ds(pl.multiple_of((p * 2 + dx) * 128, 128), 256)
            acc = acc + mm(t2[dx, :, 0:768], fm[0:768, lanes])
        a2[p] = acc
        return carry

    lax.fori_loop(0, 4, inner, 0)

    for copy in first:
        copy.wait()
    for x in (0, 9):
        place(x)
        shift(x)
    a2[0, :, 0:128] += mm(t2[0, :, 0:768], fm[0:768, 0:128])
    a2[3, :, 128:256] += mm(t2[2, :, 0:768], fm[0:768, 1152:1280])
    for copy in second:
        copy.wait()
    for dx, dy in around:
        greet(wide_sem.at[0], 2 * dx, 2 * dy)
    for x in range(10):
        v = jnp.concatenate([hr[0, x], hr[1, x]], axis=0).astype(F32)
        lanes = slice(x * 128, x * 128 + 128)
        fm[768:832, lanes] = pltpu.roll(v, 1, 1).astype(BF)
        fm[832:896, lanes] = v.astype(BF)
        fm[896:960, lanes] = pltpu.roll(v, 127, 1).astype(BF)

    third = []
    for q in range(2):
        total = jnp.zeros((256, 128), F32)
        for half in range(2):
            p = 2 * q + half
            acc = a2[p]
            for dx in range(3):
                lanes = slice((p * 2 + dx) * 128, (p * 2 + dx + 2) * 128)
                acc = acc + mm(t2[dx, :, 768:1024], fm[768:1024, lanes])
            for x in range(2):
                v = leaky(acc[:, x * 128 : x * 128 + 128] + bias2[...])
                out2[:, 2 * p + x] = v.reshape(32, 8, 128).astype(BF)
                total = total + mm(v.astype(BF), table("pool_two", 128, 128, half * 256 + x * 128))
        pooled[...] = total
        own3[q + 1] = (pooled[pl.ds(0, 128, stride=2), :] + pooled[pl.ds(1, 128, stride=2), :]).astype(BF)
        far, slot = (xm, 3) if q == 0 else (xp, 0)
        base = 5 * q
        picked = mm(table("select_three", 64, 128), own3[q + 1]).astype(BF)
        hs3[0, q] = picked[0:32]
        hs3[1, q] = picked[32:64]
        copies = [
            remote(hs3.at[1, q], hr3.at[0, slot], send3_sem.at[base], recv3_sem.at[base], far, yp),
            remote(hs3.at[0, q], hr3.at[1, slot], send3_sem.at[base + 1], recv3_sem.at[base + 1], far, ym),
            remote(own3.at[q + 1], own3.at[slot], send3_sem.at[base + 2], recv3_sem.at[base + 2], far, gy),
            remote(hs3.at[1, q], hr3.at[0, q + 1], send3_sem.at[base + 3], recv3_sem.at[base + 3], gx, yp),
            remote(hs3.at[0, q], hr3.at[1, q + 1], send3_sem.at[base + 4], recv3_sem.at[base + 4], gx, ym),
        ]
        for copy in copies:
            copy.start()
        third += copies
    d3[576:640, :] = jnp.zeros((64, 640), BF)
    pl.semaphore_wait(wide_sem.at[0], 8)
    for dy in (-4, 4):
        greet(wide_sem.at[1], 0, dy)
    for copy in third:
        copy.wait()
    tiles = []
    for t in range(4):
        tiles.append(
            jnp.concatenate([own3[t], hr3[0, t], hr3[1, t]], axis=0).astype(F32)
        )
    turned = [pltpu.roll(v, 64, 1) for v in tiles]
    lane = lax.broadcasted_iota(jnp.int32, (192, 128), 1)
    between = [jnp.where(lane < 64, turned[t], turned[t + 1]) for t in range(3)]
    for slot, v in enumerate([tiles[1], tiles[2]] + between):
        lanes = slice(slot * 128, slot * 128 + 128)
        for dz, u in enumerate((rolled_64(v, True), v, rolled_64(v, False))):
            u = u.astype(BF)
            d3[dz * 128 : dz * 128 + 128, lanes] = u[0:128]
            d3[384 + dz * 64 : 448 + dz * 64, lanes] = u[128:192]
    acc = mm(t3[0], d3[:, 256:512]) + mm(t3[1], d3[:, 0:256]) + mm(t3[2], d3[:, 384:640])
    for q in range(2):
        v = leaky(acc[:, q * 128 : q * 128 + 128] + bias3[...])
        l3[:, q * 128 : q * 128 + 128] = v.astype(BF)
        out3[:, 2 * q] = v[:, 0:64].reshape(64, 4, 64).astype(BF)
        out3[:, 2 * q + 1] = v[:, 64:128].reshape(64, 4, 64).astype(BF)

    sums = mm_t(table("pick_four", 256, 256), l3[...])
    row = lax.broadcasted_iota(jnp.int32, (256, 256), 0) % 2
    lane = lax.broadcasted_iota(jnp.int32, (256, 256), 1) % 4 // 2
    sums = jnp.where(row == lane, sums, 0.0)
    head = sums.astype(BF)
    tail = (sums - head.astype(F32)).astype(BF)
    block = jnp.zeros((128, 128), F32)
    for odd in range(2):
        g = table("gather_four", 256, 128, odd * 256)
        block = block + mm(head[odd * 128 : odd * 128 + 128], g) + mm(tail[odd * 128 : odd * 128 + 128], g)
    sa[...] = block.reshape(16, 8, 128).astype(BF)
    pl.semaphore_wait(wide_sem.at[1], 2)
    me = gx * 16 + gy
    mine = pltpu.make_async_copy(sa.at[gy], rb.at[me], recva_sem)
    y_at, x_at, z_at, core_at = gx // 4 * 2 + gy // 8, gx % 4, gy // 2 % 4, gy % 2
    columns, layers = {}, {}
    for d in range(4):
        y = (y_at + d) % 4
        for e in range(4):
            columns[e, d] = y // 2 * 4 + (x_at + e) % 4
            layers[d, e] = y % 2 * 8 + (z_at + e) % 4 * 2
    hops = (0, 1, 2, 1)
    steps = [(dx, dy, dz) for dx in range(4) for dy in range(4) for dz in range(4)]
    steps.sort(key=lambda step: -sum(hops[d] for d in step))
    for dx, dy, dz in steps:
        for flip in range(2):
            if dx or dy or dz or flip:
                layer = layers[dy, dz] + (core_at + flip) % 2
                remote(sa.at[layer], rb.at[me], senda_sem, recva_sem, columns[dx, dy], layer).start()
    mine.start()
    pltpu.make_async_copy(rb, rb, recva_sem).wait()
    pltpu.make_async_copy(rb.at[0:127], rb.at[0:127], senda_sem).wait()


def last(out2_in, out3_in, rb, w4, turn, b4, out2, out3, out4, pp, l4, sem):
    leaving = [
        pltpu.make_async_copy(out2_in, out2, sem.at[0]),
        pltpu.make_async_copy(out3_in, out3, sem.at[1]),
    ]
    for copy in leaving:
        copy.start()
    for x in range(8):
        v = rb[x * 16 : x * 16 + 16].astype(F32).reshape(128, 128).astype(BF)
        moved = mm(turn[...], v).astype(BF)
        for dy in range(3):
            for half in range(2):
                start = (dy * 2 + half) * 64
                pp[dy, (1 + 2 * x) * 32 : (3 + 2 * x) * 32, half * 128 : half * 128 + 128] = moved[start : start + 64]
    pp[:, 0:32, :] = pp[:, 512:544, :]
    pp[:, 544:576, :] = pp[:, 32:64, :]
    bias = jnp.concatenate([b4[...], b4[...]], axis=1)
    for m in range(2):
        acc = jnp.zeros((256, 256), F32)
        for dx in range(3):
            for dy in range(3):
                rows = slice(m * 256 + dx * 32, m * 256 + dx * 32 + 256)
                acc = acc + mm(pp[dy, rows, :], w4[3 * dx + dy].reshape(256, 256))
        v = leaky(acc + bias)
        l4[m * 256 : m * 256 + 256] = v.reshape(256, 2, 128).astype(BF)
        piece = pl.ds(m * 256, 256)
        leaving.append(pltpu.make_async_copy(l4.at[piece], out4.at[piece], sem.at[2 + m]))
        leaving[-1].start()
    for copy in leaving:
        copy.wait()


def shards(features, weight_two, bias_two, weight_three, bias_three, weight_four, bias_four):
    vm = pl.BlockSpec(memory_space=pltpu.VMEM)
    hbm = pl.BlockSpec(memory_space=pltpu.HBM)
    table = jnp.asarray(TABLE)
    w3 = weight_three.transpose(0, 2, 1)
    w4 = weight_four.transpose(0, 2, 1).reshape(9, 3, 64, 128)
    dma = pltpu.SemaphoreType.DMA
    held = pl.pallas_call(
        kernel,
        out_shape=(
            jax.ShapeDtypeStruct((32, 8, 8, 128), BF),
            jax.ShapeDtypeStruct((64, 4, 4, 64), BF),
            jax.ShapeDtypeStruct((128, 8, 128), BF),
            jax.ShapeDtypeStruct((9, 4, 64, 256), BF),
            jax.ShapeDtypeStruct((384, 128), BF),
            jax.ShapeDtypeStruct((1, 128), F32),
        ),
        in_specs=[hbm] * 8,
        out_specs=(vm,) * 6,
        scratch_shapes=[
            pltpu.VMEM((10, 32, 8, 128), BF),
            pltpu.VMEM((1024, 1280), BF),
            pltpu.VMEM((2, 8, 32, 128), BF),
            pltpu.VMEM((2, 10, 32, 128), BF),
            pltpu.VMEM((27, 32, 32), BF),
            pltpu.VMEM((27, 32, 64), BF),
            pltpu.VMEM((1, 32), F32),
            pltpu.VMEM((1, 64), F32),
            pltpu.VMEM(TABLE.shape, BF),
            pltpu.VMEM((288, 128), BF),
            pltpu.VMEM((9, 256, 256), BF),
            pltpu.VMEM((3, 256, 1024), BF),
            pltpu.VMEM((4, 256, 256), F32),
            pltpu.VMEM((576, 128), BF),
            pltpu.VMEM((9, 256, 128), BF),
            pltpu.VMEM((3, 256, 640), BF),
            pltpu.VMEM((256, 128), F32),
            pltpu.VMEM((256, 128), F32),
            pltpu.VMEM((256, 128), F32),
            pltpu.VMEM((4, 128, 128), BF),
            pltpu.VMEM((2, 2, 32, 128), BF),
            pltpu.VMEM((2, 4, 32, 128), BF),
            pltpu.VMEM((640, 640), BF),
            pltpu.VMEM((256, 256), BF),
            pltpu.VMEM((16, 8, 128), BF),
            dma((8,)), dma((8,)), dma((8,)), dma((8,)), dma((10,)), dma((10,)),
            dma, dma, pltpu.SemaphoreType.REGULAR((2,)),
        ],
        compiler_params=pltpu.CompilerParams(
            collective_id=0, has_side_effects=True, vmem_limit_bytes=40 * 1024 * 1024
        ),
    )(
        *(
            pltpu.with_memory_space_constraint(a, pltpu.HBM)
            for a in (features, weight_two, bias_two[None], w3, bias_three[None], w4, bias_four[None], table)
        )
    )
    level_two, level_three, bottleneck = pl.pallas_call(
        last,
        out_shape=(
            jax.ShapeDtypeStruct((32, 8, 8, 128), BF),
            jax.ShapeDtypeStruct((64, 4, 4, 64), BF),
            jax.ShapeDtypeStruct((512, 2, 128), BF),
        ),
        in_specs=[vm] * 6,
        out_specs=(hbm,) * 3,
        scratch_shapes=[
            pltpu.VMEM((3, 576, 256), BF),
            pltpu.VMEM((512, 2, 128), BF),
            dma((4,)),
        ],
        compiler_params=pltpu.CompilerParams(vmem_limit_bytes=40 * 1024 * 1024),
    )(*held)
    return level_two, level_three, bottleneck.reshape(16, 32, 2, 128).transpose(3, 0, 1, 2)


def solution(mesh):
    return jax.shard_map(
        shards,
        mesh=mesh,
        in_specs=(P(None, "gx", "gy", None), P(), P(), P(), P(), P(), P()),
        out_specs=(P(None, "gx", "gy", None), P(None, "gx", "gy", None), P(None, None, None, "gy")),
        check_vma=False,
    )
```

```python
import functools

import jax
import jax.numpy as jnp
import numpy as np
from jax import lax
from jax.experimental import pallas as pl
from jax.experimental.pallas import tpu as pltpu
from jax.sharding import PartitionSpec as P

BF = jnp.bfloat16
F32 = jnp.float32
MESH = pl.DeviceIdType.MESH


def tables():
    parts, at, row = [], {}, 0

    def add(name, matrix):
        nonlocal row
        rows, lanes = matrix.shape
        full = np.zeros((-(-rows // 16) * 16, 256), np.float32)
        full[:rows, :lanes] = matrix
        at[name] = row
        parts.append(full)
        row += full.shape[0]

    spread = np.zeros((8, 128, 256))
    for y in range(8):
        for dy in range(3):
            if 0 <= y + dy - 1 < 8:
                for c in range(32):
                    spread[y, dy * 32 + c, c * 8 + y + dy - 1] = 1
    add("spread_two", spread.reshape(1024, 256))
    order = np.zeros((256, 256))
    for y in range(8):
        for o in range(32):
            order[o * 8 + y, y * 32 + o] = 1
    add("order_two", order)
    edge = np.zeros((256, 64))
    for o in range(32):
        edge[o * 8, o] = 1
        edge[o * 8 + 7, 32 + o] = 1
    add("edge_two", edge)
    pool = np.zeros((2, 2, 128, 128))
    for half in range(2):
        for x in range(2):
            for z in range(128):
                pool[half, x, z, half * 64 + z // 2] = 0.125
    add("pool_two", pool.reshape(512, 128))
    select = np.zeros((64, 128))
    for c in range(32):
        select[c, c * 4] = 1
        select[32 + c, c * 4 + 3] = 1
    add("select_three", select)
    add("unit", np.eye(64))
    spread = np.zeros((4, 128, 128))
    for y in range(4):
        for dy in range(3):
            if 0 <= y + dy - 1 < 4:
                for c in range(32):
                    spread[y, dy * 32 + c, c * 4 + y + dy - 1] = 1
    add("spread_three", spread.reshape(512, 128))
    order = np.zeros((256, 256))
    for y in range(4):
        for o in range(64):
            order[o * 4 + y, y * 64 + o] = 1
    add("order_three", order)
    edge = np.zeros((256, 128))
    for o in range(64):
        edge[o * 4, o] = 1
        edge[o * 4 + 3, 64 + o] = 1
    add("edge_three", edge)
    pick = np.zeros((2, 16, 2, 2, 2, 4, 64))
    for odd in range(2):
        for target in range(16):
            for half in range(2):
                z = (2 * target - 1 + 2 * half + odd) % 32
                for x in range(2):
                    pick[odd, target, half, x, :, 2 * x : 2 * x + 2, 2 * z : 2 * z + 2] = 0.125
    add("pick_four", pick.reshape(256, 256))
    gather = np.zeros((2, 256, 128))
    for odd in range(2):
        for o in range(64):
            gather[odd, o * 4 : o * 4 + 4, odd * 64 + o] = 1
    add("gather_four", gather.reshape(512, 128))
    turn = np.zeros((3, 2, 2, 32, 16, 2, 2, 2))
    for dy in range(3):
        for half in range(2):
            for x in range(2):
                for y in range(32):
                    source = (y + dy - 1) % 32
                    turn[dy, half, x, y, source // 2, half, x, source % 2] = 1
    add("turn_four", turn.reshape(384, 128))
    return np.concatenate(parts).astype(jnp.bfloat16), at


TABLE, AT = tables()


def mm(a, b):
    return jnp.dot(a, b, preferred_element_type=F32)


def mm_t(a, b):
    return lax.dot_general(a, b, (((1,), (1,)), ((), ())), preferred_element_type=F32)


def leaky(t):
    return jnp.maximum(t, 0.1 * t)


def rolled_64(v, back):
    lane = lax.broadcasted_iota(jnp.int32, v.shape, 1) % 64
    if back:
        return jnp.where(lane == 0, pltpu.roll(v, 65, 1), pltpu.roll(v, 1, 1))
    return jnp.where(lane == 63, pltpu.roll(v, 63, 1), pltpu.roll(v, 127, 1))


def kernel(
    feat, w2_in, b2_in, w3_in, b3_in, w4_in, b4_in, tab_in,
    out2, out3, rb, w4, turn, b4,
    fx, fm, hs, hr, w2, w3, b2, b3, tab, wc2, z2, t2, a2, wc3, z3, t3, bias2, bias3,
    pooled, own3, hs3, hr3, d3, a3, l3, sa,
    load_sem, feat_sem, send_sem, recv_sem, send3_sem, recv3_sem, senda_sem, recva_sem, wide_sem,
):
    gx, gy = lax.axis_index("gx"), lax.axis_index("gy")
    xp, xm = lax.rem(gx + 1, 8), lax.rem(gx + 7, 8)
    yp, ym = lax.rem(gy + 1, 16), lax.rem(gy + 15, 16)

    def table(name, rows, lanes, skip=0):
        start = AT[name] + skip
        return tab[start : start + rows, :lanes]

    barrier = pltpu.get_barrier_semaphore()

    def greet(semaphore, dx, dy):
        pl.semaphore_signal(
            semaphore, inc=1, device_id=(lax.rem(gx + dx + 8, 8), lax.rem(gy + dy + 16, 16)), device_id_type=MESH
        )

    around = [(dx, dy) for dx in (-1, 0, 1) for dy in (-1, 0, 1) if dx or dy]
    for dx, dy in around:
        greet(barrier, dx, dy)

    loads = [
        pltpu.make_async_copy(feat.at[:, x], fx.at[x + 1], feat_sem.at[x]) for x in range(8)
    ]
    others = [
        pltpu.make_async_copy(tab_in, tab, load_sem.at[0]),
        pltpu.make_async_copy(w2_in, w2, load_sem.at[1]),
        pltpu.make_async_copy(b2_in, b2, load_sem.at[2]),
        pltpu.make_async_copy(w3_in, w3, load_sem.at[3]),
        pltpu.make_async_copy(b3_in, b3, load_sem.at[4]),
        pltpu.make_async_copy(b4_in, b4, load_sem.at[5]),
        pltpu.make_async_copy(w4_in, w4.at[:, 0:3, :, 0:128], load_sem.at[6]),
        pltpu.make_async_copy(w4_in, w4.at[:, 1:4, :, 128:256], load_sem.at[7]),
    ]
    for copy in loads:
        copy.start()
    for copy in others:
        copy.start()


    def remote(src, dst, send, recv, x, y):
        return pltpu.make_async_remote_copy(
            src_ref=src, dst_ref=dst, send_sem=send, recv_sem=recv,
            device_id=(x, y), device_id_type=MESH,
        )

    def place(x):
        v = fx[x].astype(F32).reshape(256, 128)
        lanes = slice(x * 128, x * 128 + 128)
        fm[256:512, lanes] = v.astype(BF)

    def shift(x):
        lanes = slice(x * 128, x * 128 + 128)
        v = fm[256:512, lanes].astype(F32)
        fm[0:256, lanes] = pltpu.roll(v, 1, 1).astype(BF)
        fm[512:768, lanes] = pltpu.roll(v, 127, 1).astype(BF)

    row = lax.broadcasted_iota(jnp.int32, (64, 256), 0)
    lane = lax.broadcasted_iota(jnp.int32, (64, 256), 1)
    select = jnp.where(lane == row % 32 * 8 + row // 32 * 7, 1.0, 0.0).astype(BF)
    for copy in loads:
        copy.wait()
    for x in range(1, 9):
        place(x)
    edges = mm(select, fm[256:512, 128:1152]).astype(BF)
    for side in range(2):
        for x in range(8):
            hs[side, x] = edges[side * 32 : side * 32 + 32, x * 128 : x * 128 + 128]
    pl.semaphore_wait(barrier, 8)
    first = [
        remote(feat.at[:, 7], fx.at[0], send_sem.at[0], recv_sem.at[0], xp, gy),
        remote(feat.at[:, 0], fx.at[9], send_sem.at[1], recv_sem.at[1], xm, gy),
    ]
    for copy in first:
        copy.start()
    second = [
        remote(hs.at[1, 7], hr.at[0, 0], send_sem.at[4], recv_sem.at[4], xp, yp),
        remote(hs.at[1, 0], hr.at[0, 9], send_sem.at[5], recv_sem.at[5], xm, yp),
        remote(hs.at[0, 7], hr.at[1, 0], send_sem.at[6], recv_sem.at[6], xp, ym),
        remote(hs.at[0, 0], hr.at[1, 9], send_sem.at[7], recv_sem.at[7], xm, ym),
        remote(hs.at[1], hr.at[0, 1:9], send_sem.at[2], recv_sem.at[2], gx, yp),
        remote(hs.at[0], hr.at[1, 1:9], send_sem.at[3], recv_sem.at[3], gx, ym),
    ]
    for copy in second:
        copy.start()

    for x in range(1, 9):
        shift(x)
    for copy in others:
        copy.wait()
    gap = jnp.zeros((32, 32), F32)
    for dx in range(3):
        for dz in range(3):
            k = 3 * dx + dz
            wc2[k * 32 : k * 32 + 32, :] = jnp.concatenate(
                [w2[9 * dx + 3 * dy + dz].astype(F32) for dy in range(3)] + [gap], axis=1
            ).astype(BF)
    for y in range(8):
        z2[:, y * 32 : y * 32 + 32, :] = (
            mm(wc2[...], table("spread_two", 128, 256, 128 * y)).astype(BF).reshape(9, 32, 256)
        )
    for dx in range(3):
        for dz in range(3):
            t2[dx, :, dz * 256 : dz * 256 + 256] = mm(
                table("order_two", 256, 256), z2[3 * dx + dz]
            ).astype(BF)
        low = [w2[9 * dx + dz].astype(F32) for dz in range(3)]
        high = [w2[9 * dx + 6 + dz].astype(F32) for dz in range(3)]
        z_edge = jnp.concatenate(
            [
                jnp.concatenate([low[0], gap, low[1], gap, low[2], gap, gap, gap], axis=1),
                jnp.concatenate([gap, high[0], gap, high[1], gap, high[2], gap, gap], axis=1),
            ],
            axis=0,
        ).astype(BF)
        t2[dx, :, 768:1024] = mm(table("edge_two", 256, 64), z_edge).astype(BF)
    row = lax.broadcasted_iota(jnp.int32, (256, 32), 0) // 8
    lane = lax.broadcasted_iota(jnp.int32, (256, 32), 1)
    column = jnp.sum(jnp.where(row == lane, b2[...], 0.0), axis=1, keepdims=True)
    bias2[...] = jnp.broadcast_to(column, (256, 128))

    for dx in range(3):
        for dz in range(3):
            k = 3 * dx + dz
            stack = jnp.concatenate(
                [w3[9 * dx + 3 * dy + dz] for dy in range(3)] + [jnp.zeros((32, 64), BF)], axis=0
            )
            wc3[k * 64 : k * 64 + 64, :] = mm_t(table("unit", 64, 64), stack).astype(BF)
    for y in range(4):
        z3[:, y * 64 : y * 64 + 64, :] = (
            mm(wc3[...], table("spread_three", 128, 128, 128 * y)).astype(BF).reshape(9, 64, 128)
        )
    gap = jnp.zeros((64, 32), F32)
    for dx in range(3):
        low, high = [], []
        for dz in range(3):
            k = 3 * dx + dz
            t3[dx, :, dz * 128 : dz * 128 + 128] = mm(table("order_three", 256, 256), z3[k]).astype(BF)
            block = wc3[k * 64 : k * 64 + 64, :].astype(F32)
            low.append(block[:, 0:32])
            high.append(block[:, 64:96])
        z_edge = jnp.concatenate(
            [
                jnp.concatenate([low[0], gap, low[1], gap, low[2], gap, gap, gap], axis=1),
                jnp.concatenate([gap, high[0], gap, high[1], gap, high[2], gap, gap], axis=1),
            ],
            axis=0,
        ).astype(BF)
        t3[dx, :, 384:640] = mm(table("edge_three", 256, 128), z_edge).astype(BF)
    row = lax.broadcasted_iota(jnp.int32, (256, 64), 0) // 4
    lane = lax.broadcasted_iota(jnp.int32, (256, 64), 1)
    column = jnp.sum(jnp.where(row == lane, b3[...], 0.0), axis=1, keepdims=True)
    bias3[...] = jnp.broadcast_to(column, (256, 128))

    w4[:, 3, :, 0:128] = jnp.zeros((9, 64, 128), BF)
    w4[:, 0, :, 128:256] = jnp.zeros((9, 64, 128), BF)
    turn[...] = table("turn_four", 384, 128)

    fm[0:768, 0:128] = jnp.zeros((768, 128), BF)
    fm[0:768, 1152:1280] = jnp.zeros((768, 128), BF)
    fm[960:1024, :] = jnp.zeros((64, 1280), BF)

    def inner(p, carry):
        acc = jnp.zeros((256, 256), F32)
        for dx in range(3):
            lanes = pl.ds(pl.multiple_of((p * 2 + dx) * 128, 128), 256)
            acc = acc + mm(t2[dx, :, 0:768], fm[0:768, lanes])
        a2[p] = acc
        return carry

    lax.fori_loop(0, 4, inner, 0)

    for copy in first:
        copy.wait()
    for x in (0, 9):
        place(x)
        shift(x)
    a2[0, :, 0:128] += mm(t2[0, :, 0:768], fm[0:768, 0:128])
    a2[3, :, 128:256] += mm(t2[2, :, 0:768], fm[0:768, 1152:1280])
    for copy in second:
        copy.wait()
    for dx, dy in around:
        greet(wide_sem.at[0], 2 * dx, 2 * dy)
    for x in range(10):
        v = jnp.concatenate([hr[0, x], hr[1, x]], axis=0).astype(F32)
        lanes = slice(x * 128, x * 128 + 128)
        fm[768:832, lanes] = pltpu.roll(v, 1, 1).astype(BF)
        fm[832:896, lanes] = v.astype(BF)
        fm[896:960, lanes] = pltpu.roll(v, 127, 1).astype(BF)

    third = []

    def send3(src, dst, x, y):
        k = len(third)
        third.append(remote(src, dst, send3_sem.at[k], recv3_sem.at[k], x, y))
        third[-1].start()

    for q in range(2):
        total = jnp.zeros((256, 128), F32)
        for half in range(2):
            p = ((3, 0), (1, 2))[q][half]
            acc = a2[p]
            for dx in range(3):
                lanes = slice((p * 2 + dx) * 128, (p * 2 + dx + 2) * 128)
                acc = acc + mm(t2[dx, :, 768:1024], fm[768:1024, lanes])
            for x in range(2):
                v = leaky(acc[:, x * 128 : x * 128 + 128] + bias2[...])
                out2[:, 2 * p + x] = v.reshape(32, 8, 128).astype(BF)
                total = total + mm(v.astype(BF), table("pool_two", 128, 128, half * 256 + x * 128))
        pooled[...] = total
        mean = (pooled[pl.ds(0, 128, stride=2), :] + pooled[pl.ds(1, 128, stride=2), :]).astype(BF)
        own3[q + 1] = mean
        picked = mm(table("select_three", 64, 128), mean).astype(BF)
        hs3[0, q] = picked[0:32]
        hs3[1, q] = picked[32:64]
        if q == 0:
            for x, slot in ((xm, 3), (xp, 0)):
                send3(hs3.at[1, 0], hr3.at[0, slot], x, yp)
                send3(hs3.at[0, 0], hr3.at[1, slot], x, ym)
                send3(own3.at[1], own3.at[slot], x, gy)
        send3(hs3.at[1, q], hr3.at[0, q + 1], gx, yp)
        send3(hs3.at[0, q], hr3.at[1, q + 1], gx, ym)

    left = lax.broadcasted_iota(jnp.int32, (128, 128), 1) < 64

    def three(rows, lanes, v):
        for dz, u in enumerate((rolled_64(v, True), v, rolled_64(v, False))):
            start = dz * 128 if rows == 128 else 384 + dz * 64
            d3[start : start + rows, lanes * 128 : lanes * 128 + 128] = u.astype(BF)

    outer, middle = own3[1].astype(F32), own3[2].astype(F32)
    outer_turned, middle_turned = pltpu.roll(outer, 64, 1), pltpu.roll(middle, 64, 1)
    three(128, 0, jnp.where(left, outer_turned, middle_turned))
    three(128, 1, jnp.where(left, middle_turned, outer_turned))
    three(128, 3, middle)
    bias = bias3[...]
    a3[...] = mm(t3[1, :, 0:384], d3[0:384, 0:256]) + jnp.concatenate([bias, bias], axis=1)
    d3[576:640, :] = jnp.zeros((64, 640), BF)
    pl.semaphore_wait(wide_sem.at[0], 8)
    for dy in (-4, 4):
        greet(wide_sem.at[1], 0, dy)
    for copy in third:
        copy.wait()
    three(128, 2, jnp.where(left, own3[0].astype(F32), outer))
    three(128, 4, jnp.where(left, outer, own3[3].astype(F32)))
    edge = [jnp.concatenate([hr3[0, t], hr3[1, t]], axis=0).astype(F32) for t in range(4)]
    turned = [pltpu.roll(edge[t], 64, 1) for t in (1, 2)]
    left = lax.broadcasted_iota(jnp.int32, (64, 128), 1) < 64
    three(64, 0, jnp.where(left, turned[0], turned[1]))
    three(64, 1, jnp.where(left, turned[1], turned[0]))
    three(64, 2, jnp.where(left, edge[0], edge[1]))
    three(64, 3, edge[2])
    three(64, 4, jnp.where(left, edge[1], edge[3]))
    v = leaky(
        a3[...] + mm(t3[0], d3[:, 256:512]) + mm(t3[1, :, 384:640], d3[384:640, 0:256]) + mm(t3[2], d3[:, 384:640])
    )
    l3[...] = v.astype(BF)
    sums = mm_t(table("pick_four", 256, 256), l3[...])
    row = lax.broadcasted_iota(jnp.int32, (256, 256), 0) % 2
    lane = lax.broadcasted_iota(jnp.int32, (256, 256), 1) % 4 // 2
    sums = jnp.where(row == lane, sums, 0.0)
    head = sums.astype(BF)
    tail = (sums - head.astype(F32)).astype(BF)
    block = jnp.zeros((128, 128), F32)
    for odd in range(2):
        g = table("gather_four", 256, 128, odd * 256)
        block = block + mm(head[odd * 128 : odd * 128 + 128], g) + mm(tail[odd * 128 : odd * 128 + 128], g)
    sa[...] = block.reshape(16, 8, 128).astype(BF)
    pl.semaphore_wait(wide_sem.at[1], 2)
    me = gx * 16 + gy
    mine = pltpu.make_async_copy(sa.at[gy], rb.at[me], recva_sem)
    y_at, x_at, z_at, core_at = gx // 4 * 2 + gy // 8, gx % 4, gy // 2 % 4, gy % 2
    columns, layers = {}, {}
    for d in range(4):
        y = (y_at + d) % 4
        for e in range(4):
            columns[e, d] = y // 2 * 4 + (x_at + e) % 4
            layers[d, e] = y % 2 * 8 + (z_at + e) % 4 * 2
    hops = (0, 1, 2, 1)
    steps = [(dx, dy, dz) for dx in range(4) for dy in range(4) for dz in range(4)]
    steps.sort(key=lambda step: -sum(hops[d] for d in step))
    for dx, dy, dz in steps:
        for flip in range(2):
            if dx or dy or dz or flip:
                layer = layers[dy, dz] + (core_at + flip) % 2
                remote(sa.at[layer], rb.at[me], senda_sem, recva_sem, columns[dx, dy], layer).start()
    mine.start()
    for x in range(4):
        out3[:, x] = l3[:, x * 64 : x * 64 + 64].astype(F32).reshape(64, 4, 64).astype(BF)
    pltpu.make_async_copy(rb, rb, recva_sem).wait()
    pltpu.make_async_copy(rb.at[0:127], rb.at[0:127], senda_sem).wait()


def last(out2_in, out3_in, rb, w4, turn, b4, out2, out3, out4, pp, l4, sem):
    leaving = [
        pltpu.make_async_copy(out2_in, out2, sem.at[0]),
        pltpu.make_async_copy(out3_in, out3, sem.at[1]),
    ]
    for copy in leaving:
        copy.start()
    for x in range(0, 8, 2):
        v = jnp.concatenate(
            [rb[k * 16 : k * 16 + 16].astype(F32).reshape(128, 128).astype(BF) for k in (x, x + 1)], axis=1
        )
        moved = mm(turn[...], v).astype(BF)
        for k in range(2):
            rows = slice((1 + 2 * (x + k)) * 32, (3 + 2 * (x + k)) * 32)
            for dy in range(3):
                for half in range(2):
                    start = (dy * 2 + half) * 64
                    pp[dy, rows, half * 128 : half * 128 + 128] = moved[start : start + 64, k * 128 : k * 128 + 128]
    pp[:, 0:32, :] = pp[:, 512:544, :]
    pp[:, 544:576, :] = pp[:, 32:64, :]
    bias = jnp.concatenate([b4[...], b4[...]], axis=1)
    for m in range(2):
        acc = jnp.zeros((256, 256), F32)
        for dx in range(3):
            for dy in range(3):
                rows = slice(m * 256 + dx * 32, m * 256 + dx * 32 + 256)
                acc = acc + mm(pp[dy, rows, :], w4[3 * dx + dy].reshape(256, 256))
        v = leaky(acc + bias)
        l4[m * 256 : m * 256 + 256] = v.reshape(256, 2, 128).astype(BF)
        piece = pl.ds(m * 256, 256)
        leaving.append(pltpu.make_async_copy(l4.at[piece], out4.at[piece], sem.at[2 + m]))
        leaving[-1].start()
    for copy in leaving:
        copy.wait()


def shards(features, weight_two, bias_two, weight_three, bias_three, weight_four, bias_four):
    vm = pl.BlockSpec(memory_space=pltpu.VMEM)
    hbm = pl.BlockSpec(memory_space=pltpu.HBM)
    table = jnp.asarray(TABLE)
    w3 = weight_three.transpose(0, 2, 1)
    w4 = weight_four.transpose(0, 2, 1).reshape(9, 3, 64, 128)
    dma = pltpu.SemaphoreType.DMA
    held = pl.pallas_call(
        kernel,
        out_shape=(
            jax.ShapeDtypeStruct((32, 8, 8, 128), BF),
            jax.ShapeDtypeStruct((64, 4, 4, 64), BF),
            jax.ShapeDtypeStruct((128, 8, 128), BF),
            jax.ShapeDtypeStruct((9, 4, 64, 256), BF),
            jax.ShapeDtypeStruct((384, 128), BF),
            jax.ShapeDtypeStruct((1, 128), F32),
        ),
        in_specs=[hbm] * 8,
        out_specs=(vm,) * 6,
        scratch_shapes=[
            pltpu.VMEM((10, 32, 8, 128), BF),
            pltpu.VMEM((1024, 1280), BF),
            pltpu.VMEM((2, 8, 32, 128), BF),
            pltpu.VMEM((2, 10, 32, 128), BF),
            pltpu.VMEM((27, 32, 32), BF),
            pltpu.VMEM((27, 32, 64), BF),
            pltpu.VMEM((1, 32), F32),
            pltpu.VMEM((1, 64), F32),
            pltpu.VMEM(TABLE.shape, BF),
            pltpu.VMEM((288, 128), BF),
            pltpu.VMEM((9, 256, 256), BF),
            pltpu.VMEM((3, 256, 1024), BF),
            pltpu.VMEM((4, 256, 256), F32),
            pltpu.VMEM((576, 128), BF),
            pltpu.VMEM((9, 256, 128), BF),
            pltpu.VMEM((3, 256, 640), BF),
            pltpu.VMEM((256, 128), F32),
            pltpu.VMEM((256, 128), F32),
            pltpu.VMEM((256, 128), F32),
            pltpu.VMEM((4, 128, 128), BF),
            pltpu.VMEM((2, 2, 32, 128), BF),
            pltpu.VMEM((2, 4, 32, 128), BF),
            pltpu.VMEM((640, 640), BF),
            pltpu.VMEM((256, 256), F32),
            pltpu.VMEM((256, 256), BF),
            pltpu.VMEM((16, 8, 128), BF),
            dma((8,)), dma((8,)), dma((8,)), dma((8,)), dma((10,)), dma((10,)),
            dma, dma, pltpu.SemaphoreType.REGULAR((2,)),
        ],
        compiler_params=pltpu.CompilerParams(
            collective_id=0, has_side_effects=True, vmem_limit_bytes=40 * 1024 * 1024
        ),
    )(
        *(
            pltpu.with_memory_space_constraint(a, pltpu.HBM)
            for a in (features, weight_two, bias_two[None], w3, bias_three[None], w4, bias_four[None], table)
        )
    )
    level_two, level_three, bottleneck = pl.pallas_call(
        last,
        out_shape=(
            jax.ShapeDtypeStruct((32, 8, 8, 128), BF),
            jax.ShapeDtypeStruct((64, 4, 4, 64), BF),
            jax.ShapeDtypeStruct((512, 2, 128), BF),
        ),
        in_specs=[vm] * 6,
        out_specs=(hbm,) * 3,
        scratch_shapes=[
            pltpu.VMEM((3, 576, 256), BF),
            pltpu.VMEM((512, 2, 128), BF),
            dma((4,)),
        ],
        compiler_params=pltpu.CompilerParams(vmem_limit_bytes=40 * 1024 * 1024),
    )(*held)
    return level_two, level_three, bottleneck.reshape(16, 32, 2, 128).transpose(3, 0, 1, 2)


def solution(mesh):
    return jax.shard_map(
        shards,
        mesh=mesh,
        in_specs=(P(None, "gx", "gy", None), P(), P(), P(), P(), P(), P()),
        out_specs=(P(None, "gx", "gy", None), P(None, "gx", "gy", None), P(None, None, None, "gy")),
        check_vma=False,
    )
```

```python
import functools

import jax
import jax.numpy as jnp
import numpy as np
from jax import lax
from jax.experimental import pallas as pl
from jax.experimental.pallas import tpu as pltpu
from jax.sharding import PartitionSpec as P

BF = jnp.bfloat16
F32 = jnp.float32
MESH = pl.DeviceIdType.MESH


def tables():
    parts, at, row = [], {}, 0

    def add(name, matrix):
        nonlocal row
        rows, lanes = matrix.shape
        full = np.zeros((-(-rows // 16) * 16, 256), np.float32)
        full[:rows, :lanes] = matrix
        at[name] = row
        parts.append(full)
        row += full.shape[0]

    spread = np.zeros((8, 128, 256))
    for y in range(8):
        for dy in range(3):
            if 0 <= y + dy - 1 < 8:
                for c in range(32):
                    spread[y, dy * 32 + c, c * 8 + y + dy - 1] = 1
    add("spread_two", spread.reshape(1024, 256))
    order = np.zeros((256, 256))
    for y in range(8):
        for o in range(32):
            order[o * 8 + y, y * 32 + o] = 1
    add("order_two", order)
    edge = np.zeros((256, 64))
    for o in range(32):
        edge[o * 8, o] = 1
        edge[o * 8 + 7, 32 + o] = 1
    add("edge_two", edge)
    pool = np.zeros((2, 2, 128, 128))
    for half in range(2):
        for x in range(2):
            for z in range(128):
                pool[half, x, z, half * 64 + z // 2] = 0.125
    add("pool_two", pool.reshape(512, 128))
    select = np.zeros((64, 128))
    for c in range(32):
        select[c, c * 4] = 1
        select[32 + c, c * 4 + 3] = 1
    add("select_three", select)
    add("unit", np.eye(64))
    spread = np.zeros((4, 128, 128))
    for y in range(4):
        for dy in range(3):
            if 0 <= y + dy - 1 < 4:
                for c in range(32):
                    spread[y, dy * 32 + c, c * 4 + y + dy - 1] = 1
    add("spread_three", spread.reshape(512, 128))
    order = np.zeros((256, 256))
    for y in range(4):
        for o in range(64):
            order[o * 4 + y, y * 64 + o] = 1
    add("order_three", order)
    edge = np.zeros((256, 128))
    for o in range(64):
        edge[o * 4, o] = 1
        edge[o * 4 + 3, 64 + o] = 1
    add("edge_three", edge)
    pick = np.zeros((2, 16, 2, 2, 2, 4, 64))
    for odd in range(2):
        for target in range(16):
            for half in range(2):
                z = (2 * target - 1 + 2 * half + odd) % 32
                for x in range(2):
                    pick[odd, target, half, x, :, 2 * x : 2 * x + 2, 2 * z : 2 * z + 2] = 0.125
    add("pick_four", pick.reshape(256, 256))
    gather = np.zeros((2, 256, 128))
    for odd in range(2):
        for o in range(64):
            gather[odd, o * 4 : o * 4 + 4, odd * 64 + o] = 1
    add("gather_four", gather.reshape(512, 128))
    turn = np.zeros((3, 2, 2, 32, 16, 2, 2, 2))
    for dy in range(3):
        for half in range(2):
            for x in range(2):
                for y in range(32):
                    source = (y + dy - 1) % 32
                    turn[dy, half, x, y, source // 2, half, x, source % 2] = 1
    add("turn_four", turn.reshape(384, 128))
    return np.concatenate(parts).astype(jnp.bfloat16), at


TABLE, AT = tables()


def mm(a, b):
    return jnp.dot(a, b, preferred_element_type=F32)


def mm_t(a, b):
    return lax.dot_general(a, b, (((1,), (1,)), ((), ())), preferred_element_type=F32)


def leaky(t):
    return jnp.maximum(t, 0.1 * t)


def rolled_64(v, back):
    lane = lax.broadcasted_iota(jnp.int32, v.shape, 1) % 64
    if back:
        return jnp.where(lane == 0, pltpu.roll(v, 65, 1), pltpu.roll(v, 1, 1))
    return jnp.where(lane == 63, pltpu.roll(v, 63, 1), pltpu.roll(v, 127, 1))


def kernel(
    feat, w2_in, b2_in, w3_in, b3_in, w4_in, b4_in, tab_in,
    out2, out3, rb, w4, turn, b4,
    fx, fm, hs, hr, w2, w3, b2, b3, tab, wc2, z2, t2, a2, wc3, z3, t3, bias2, bias3,
    pooled, own3, hs3, hr3, d3, a3, l3, sa,
    load_sem, feat_sem, send_sem, recv_sem, send3_sem, recv3_sem, senda_sem, recva_sem, wide_sem,
):
    gx, gy = lax.axis_index("gx"), lax.axis_index("gy")
    xp, xm = lax.rem(gx + 1, 8), lax.rem(gx + 7, 8)
    yp, ym = lax.rem(gy + 1, 16), lax.rem(gy + 15, 16)

    def table(name, rows, lanes, skip=0):
        start = AT[name] + skip
        return tab[start : start + rows, :lanes]

    barrier = pltpu.get_barrier_semaphore()

    def greet(semaphore, dx, dy):
        pl.semaphore_signal(
            semaphore, inc=1, device_id=(lax.rem(gx + dx + 8, 8), lax.rem(gy + dy + 16, 16)), device_id_type=MESH
        )

    around = [(dx, dy) for dx in (-1, 0, 1) for dy in (-1, 0, 1) if dx or dy]
    for dx, dy in around:
        greet(barrier, dx, dy)

    loads = [
        pltpu.make_async_copy(feat.at[:, x], fx.at[x + 1], feat_sem.at[x]) for x in range(8)
    ]
    others = [
        pltpu.make_async_copy(tab_in, tab, load_sem.at[0]),
        pltpu.make_async_copy(w2_in, w2, load_sem.at[1]),
        pltpu.make_async_copy(b2_in, b2, load_sem.at[2]),
        pltpu.make_async_copy(w3_in, w3, load_sem.at[3]),
        pltpu.make_async_copy(b3_in, b3, load_sem.at[4]),
        pltpu.make_async_copy(b4_in, b4, load_sem.at[5]),
        pltpu.make_async_copy(w4_in, w4.at[:, 0:3, :, 0:128], load_sem.at[6]),
        pltpu.make_async_copy(w4_in, w4.at[:, 1:4, :, 128:256], load_sem.at[7]),
    ]
    for copy in loads:
        copy.start()


    def remote(src, dst, send, recv, x, y):
        return pltpu.make_async_remote_copy(
            src_ref=src, dst_ref=dst, send_sem=send, recv_sem=recv,
            device_id=(x, y), device_id_type=MESH,
        )

    def place(x):
        v = fx[x].astype(F32).reshape(256, 128)
        lanes = slice(x * 128, x * 128 + 128)
        fm[256:512, lanes] = v.astype(BF)

    def shift(x):
        lanes = slice(x * 128, x * 128 + 128)
        v = fm[256:512, lanes].astype(F32)
        fm[0:256, lanes] = pltpu.roll(v, 1, 1).astype(BF)
        fm[512:768, lanes] = pltpu.roll(v, 127, 1).astype(BF)

    row = lax.broadcasted_iota(jnp.int32, (64, 256), 0)
    lane = lax.broadcasted_iota(jnp.int32, (64, 256), 1)
    select = jnp.where(lane == row % 32 * 8 + row // 32 * 7, 1.0, 0.0).astype(BF)
    for copy in loads:
        copy.wait()
    for copy in others:
        copy.start()
    for x in range(1, 9):
        place(x)
    edges = mm(select, fm[256:512, 128:1152]).astype(BF)
    for side in range(2):
        for x in range(8):
            hs[side, x] = edges[side * 32 : side * 32 + 32, x * 128 : x * 128 + 128]
    pl.semaphore_wait(barrier, 8)
    second = [
        remote(hs.at[1, 7], hr.at[0, 0], send_sem.at[4], recv_sem.at[4], xp, yp),
        remote(hs.at[1, 0], hr.at[0, 9], send_sem.at[5], recv_sem.at[5], xm, yp),
        remote(hs.at[0, 7], hr.at[1, 0], send_sem.at[6], recv_sem.at[6], xp, ym),
        remote(hs.at[0, 0], hr.at[1, 9], send_sem.at[7], recv_sem.at[7], xm, ym),
        remote(hs.at[1], hr.at[0, 1:9], send_sem.at[2], recv_sem.at[2], gx, yp),
        remote(hs.at[0], hr.at[1, 1:9], send_sem.at[3], recv_sem.at[3], gx, ym),
    ]
    for copy in second[:4]:
        copy.start()
    first = [
        remote(fx.at[8], fx.at[0], send_sem.at[0], recv_sem.at[0], xp, gy),
        remote(fx.at[1], fx.at[9], send_sem.at[1], recv_sem.at[1], xm, gy),
    ]
    for copy in first:
        copy.start()
    for copy in second[4:]:
        copy.start()

    for x in range(1, 9):
        shift(x)
    for copy in others:
        copy.wait()
    gap = jnp.zeros((32, 32), F32)
    for dx in range(3):
        for dz in range(3):
            k = 3 * dx + dz
            wc2[k * 32 : k * 32 + 32, :] = jnp.concatenate(
                [w2[9 * dx + 3 * dy + dz].astype(F32) for dy in range(3)] + [gap], axis=1
            ).astype(BF)
    for y in range(8):
        z2[:, y * 32 : y * 32 + 32, :] = (
            mm(wc2[...], table("spread_two", 128, 256, 128 * y)).astype(BF).reshape(9, 32, 256)
        )
    for dx in range(3):
        for dz in range(3):
            t2[dx, :, dz * 256 : dz * 256 + 256] = mm(
                table("order_two", 256, 256), z2[3 * dx + dz]
            ).astype(BF)
        low = [w2[9 * dx + dz].astype(F32) for dz in range(3)]
        high = [w2[9 * dx + 6 + dz].astype(F32) for dz in range(3)]
        z_edge = jnp.concatenate(
            [
                jnp.concatenate([low[0], gap, low[1], gap, low[2], gap, gap, gap], axis=1),
                jnp.concatenate([gap, high[0], gap, high[1], gap, high[2], gap, gap], axis=1),
            ],
            axis=0,
        ).astype(BF)
        t2[dx, :, 768:1024] = mm(table("edge_two", 256, 64), z_edge).astype(BF)
    row = lax.broadcasted_iota(jnp.int32, (256, 32), 0) // 8
    lane = lax.broadcasted_iota(jnp.int32, (256, 32), 1)
    column = jnp.sum(jnp.where(row == lane, b2[...], 0.0), axis=1, keepdims=True)
    bias2[...] = jnp.broadcast_to(column, (256, 128))

    fm[0:768, 0:128] = jnp.zeros((768, 128), BF)
    fm[0:768, 1152:1280] = jnp.zeros((768, 128), BF)
    fm[960:1024, :] = jnp.zeros((64, 1280), BF)

    def inner(p, carry):
        a2[p] = mm(
            jnp.concatenate([t2[dx, :, 0:768] for dx in range(3)], axis=1),
            jnp.concatenate(
                [fm[0:768, pl.ds(pl.multiple_of((p * 2 + dx) * 128, 128), 256)] for dx in range(3)], axis=0
            ),
        )
        return carry

    lax.fori_loop(0, 4, inner, 0)

    for copy in first:
        copy.wait()
    for x in (0, 9):
        place(x)
        shift(x)
    a2[0, :, 0:128] += mm(t2[0, :, 0:768], fm[0:768, 0:128])
    a2[3, :, 128:256] += mm(t2[2, :, 0:768], fm[0:768, 1152:1280])
    for copy in second:
        copy.wait()
    for dx, dy in around:
        greet(wide_sem.at[0], 2 * dx, 2 * dy)
    for x in range(10):
        v = jnp.concatenate([hr[0, x], hr[1, x]], axis=0).astype(F32)
        lanes = slice(x * 128, x * 128 + 128)
        fm[768:832, lanes] = pltpu.roll(v, 1, 1).astype(BF)
        fm[832:896, lanes] = v.astype(BF)
        fm[896:960, lanes] = pltpu.roll(v, 127, 1).astype(BF)

    third = []

    def send3(src, dst, x, y):
        k = len(third)
        third.append(remote(src, dst, send3_sem.at[k], recv3_sem.at[k], x, y))
        third[-1].start()

    for q in range(2):
        total = jnp.zeros((256, 128), F32)
        for half in range(2):
            p = ((3, 0), (1, 2))[q][half]
            acc = a2[p] + mm(
                jnp.concatenate([t2[dx, :, 768:1024] for dx in range(3)], axis=1),
                jnp.concatenate(
                    [fm[768:1024, (p * 2 + dx) * 128 : (p * 2 + dx + 2) * 128] for dx in range(3)], axis=0
                ),
            )
            for x in range(2):
                v = leaky(acc[:, x * 128 : x * 128 + 128] + bias2[...])
                out2[:, 2 * p + x] = v.reshape(32, 8, 128).astype(BF)
                total = total + mm(v.astype(BF), table("pool_two", 128, 128, half * 256 + x * 128))
        pooled[...] = total
        mean = (pooled[pl.ds(0, 128, stride=2), :] + pooled[pl.ds(1, 128, stride=2), :]).astype(BF)
        own3[q + 1] = mean
        picked = mm(table("select_three", 64, 128), mean).astype(BF)
        hs3[0, q] = picked[0:32]
        hs3[1, q] = picked[32:64]
        if q == 0:
            for x, slot in ((xm, 3), (xp, 0)):
                send3(hs3.at[1, 0], hr3.at[0, slot], x, yp)
                send3(hs3.at[0, 0], hr3.at[1, slot], x, ym)
                send3(own3.at[1], own3.at[slot], x, gy)
        send3(hs3.at[1, q], hr3.at[0, q + 1], gx, yp)
        send3(hs3.at[0, q], hr3.at[1, q + 1], gx, ym)

    for dx in range(3):
        for dz in range(3):
            k = 3 * dx + dz
            stack = jnp.concatenate(
                [w3[9 * dx + 3 * dy + dz] for dy in range(3)] + [jnp.zeros((32, 64), BF)], axis=0
            )
            wc3[k * 64 : k * 64 + 64, :] = mm_t(table("unit", 64, 64), stack).astype(BF)
    for y in range(4):
        z3[:, y * 64 : y * 64 + 64, :] = (
            mm(wc3[...], table("spread_three", 128, 128, 128 * y)).astype(BF).reshape(9, 64, 128)
        )
    gap = jnp.zeros((64, 32), F32)
    for dx in range(3):
        low, high = [], []
        for dz in range(3):
            k = 3 * dx + dz
            t3[dx, :, dz * 128 : dz * 128 + 128] = mm(table("order_three", 256, 256), z3[k]).astype(BF)
            block = wc3[k * 64 : k * 64 + 64, :].astype(F32)
            low.append(block[:, 0:32])
            high.append(block[:, 64:96])
        z_edge = jnp.concatenate(
            [
                jnp.concatenate([low[0], gap, low[1], gap, low[2], gap, gap, gap], axis=1),
                jnp.concatenate([gap, high[0], gap, high[1], gap, high[2], gap, gap], axis=1),
            ],
            axis=0,
        ).astype(BF)
        t3[dx, :, 384:640] = mm(table("edge_three", 256, 128), z_edge).astype(BF)
    row = lax.broadcasted_iota(jnp.int32, (256, 64), 0) // 4
    lane = lax.broadcasted_iota(jnp.int32, (256, 64), 1)
    column = jnp.sum(jnp.where(row == lane, b3[...], 0.0), axis=1, keepdims=True)
    bias3[...] = jnp.broadcast_to(column, (256, 128))

    w4[:, 3, :, 0:128] = jnp.zeros((9, 64, 128), BF)
    w4[:, 0, :, 128:256] = jnp.zeros((9, 64, 128), BF)
    turn[...] = table("turn_four", 384, 128)

    left = lax.broadcasted_iota(jnp.int32, (128, 128), 1) < 64

    def three(rows, lanes, v):
        for dz, u in enumerate((rolled_64(v, True), v, rolled_64(v, False))):
            start = dz * 128 if rows == 128 else 384 + dz * 64
            d3[start : start + rows, lanes * 128 : lanes * 128 + 128] = u.astype(BF)

    outer, middle = own3[1].astype(F32), own3[2].astype(F32)
    outer_turned, middle_turned = pltpu.roll(outer, 64, 1), pltpu.roll(middle, 64, 1)
    three(128, 0, jnp.where(left, outer_turned, middle_turned))
    three(128, 1, jnp.where(left, middle_turned, outer_turned))
    three(128, 3, middle)
    bias = bias3[...]
    a3[...] = mm(t3[1, :, 0:384], d3[0:384, 0:256]) + jnp.concatenate([bias, bias], axis=1)
    d3[576:640, :] = jnp.zeros((64, 640), BF)
    pl.semaphore_wait(wide_sem.at[0], 8)
    for dy in (-4, 4):
        greet(wide_sem.at[1], 0, dy)
    for copy in third:
        copy.wait()
    three(128, 2, jnp.where(left, own3[0].astype(F32), outer))
    three(128, 4, jnp.where(left, outer, own3[3].astype(F32)))
    edge = [jnp.concatenate([hr3[0, t], hr3[1, t]], axis=0).astype(F32) for t in range(4)]
    turned = [pltpu.roll(edge[t], 64, 1) for t in (1, 2)]
    left = lax.broadcasted_iota(jnp.int32, (64, 128), 1) < 64
    three(64, 0, jnp.where(left, turned[0], turned[1]))
    three(64, 1, jnp.where(left, turned[1], turned[0]))
    three(64, 2, jnp.where(left, edge[0], edge[1]))
    three(64, 3, edge[2])
    three(64, 4, jnp.where(left, edge[1], edge[3]))
    v = leaky(
        a3[...] + mm(t3[0], d3[:, 256:512]) + mm(t3[1, :, 384:640], d3[384:640, 0:256]) + mm(t3[2], d3[:, 384:640])
    )
    l3[...] = v.astype(BF)
    sums = mm_t(table("pick_four", 256, 256), l3[...])
    row = lax.broadcasted_iota(jnp.int32, (256, 256), 0) % 2
    lane = lax.broadcasted_iota(jnp.int32, (256, 256), 1) % 4 // 2
    sums = jnp.where(row == lane, sums, 0.0)
    head = sums.astype(BF)
    tail = (sums - head.astype(F32)).astype(BF)
    block = jnp.zeros((128, 128), F32)
    for odd in range(2):
        g = table("gather_four", 256, 128, odd * 256)
        block = block + mm(head[odd * 128 : odd * 128 + 128], g) + mm(tail[odd * 128 : odd * 128 + 128], g)
    sa[...] = block.reshape(16, 8, 128).astype(BF)
    pl.semaphore_wait(wide_sem.at[1], 2)
    me = gx * 16 + gy
    mine = pltpu.make_async_copy(sa.at[gy], rb.at[me], recva_sem)
    y_at, x_at, z_at, core_at = gx // 4 * 2 + gy // 8, gx % 4, gy // 2 % 4, gy % 2
    columns, layers = {}, {}
    for d in range(4):
        y = (y_at + d) % 4
        for e in range(4):
            columns[e, d] = y // 2 * 4 + (x_at + e) % 4
            layers[d, e] = y % 2 * 8 + (z_at + e) % 4 * 2
    hops = (0, 1, 2, 1)
    steps = [(dx, dy, dz) for dx in range(4) for dy in range(4) for dz in range(4)]
    steps.sort(key=lambda step: -sum(hops[d] for d in step))
    for dx, dy, dz in steps:
        for flip in range(2):
            if dx or dy or dz or flip:
                layer = layers[dy, dz] + (core_at + flip) % 2
                remote(sa.at[layer], rb.at[me], senda_sem, recva_sem, columns[dx, dy], layer).start()
    mine.start()
    for x in range(4):
        out3[:, x] = l3[:, x * 64 : x * 64 + 64].astype(F32).reshape(64, 4, 64).astype(BF)
    pltpu.make_async_copy(rb, rb, recva_sem).wait()
    pltpu.make_async_copy(rb.at[0:127], rb.at[0:127], senda_sem).wait()


def last(out2_in, out3_in, rb, w4, turn, b4, out2, out3, out4, pp, l4, sem):
    leaving = [
        pltpu.make_async_copy(out2_in, out2, sem.at[0]),
        pltpu.make_async_copy(out3_in, out3, sem.at[1]),
    ]
    for copy in leaving:
        copy.start()
    for x in range(0, 8, 2):
        v = jnp.concatenate(
            [rb[k * 16 : k * 16 + 16].astype(F32).reshape(128, 128).astype(BF) for k in (x, x + 1)], axis=1
        )
        moved = mm(turn[...], v).astype(BF)
        for k in range(2):
            rows = slice((1 + 2 * (x + k)) * 32, (3 + 2 * (x + k)) * 32)
            for dy in range(3):
                for half in range(2):
                    start = (dy * 2 + half) * 64
                    pp[dy, rows, half * 128 : half * 128 + 128] = moved[start : start + 64, k * 128 : k * 128 + 128]
    pp[:, 0:32, :] = pp[:, 512:544, :]
    pp[:, 544:576, :] = pp[:, 32:64, :]
    bias = jnp.concatenate([b4[...], b4[...]], axis=1)
    for m in range(2):
        rows = [pp[dy, m * 256 + dx * 32 : m * 256 + dx * 32 + 256, :] for dx in range(3) for dy in range(3)]
        v = leaky(mm(jnp.concatenate(rows, axis=1), w4[...].reshape(2304, 256)) + bias)
        l4[m * 256 : m * 256 + 256] = v.reshape(256, 2, 128).astype(BF)
        piece = pl.ds(m * 256, 256)
        leaving.append(pltpu.make_async_copy(l4.at[piece], out4.at[piece], sem.at[2 + m]))
        leaving[-1].start()
    for copy in leaving:
        copy.wait()


def shards(features, weight_two, bias_two, weight_three, bias_three, weight_four, bias_four):
    vm = pl.BlockSpec(memory_space=pltpu.VMEM)
    hbm = pl.BlockSpec(memory_space=pltpu.HBM)
    table = jnp.asarray(TABLE)
    w3 = weight_three.transpose(0, 2, 1)
    w4 = weight_four.transpose(0, 2, 1).reshape(9, 3, 64, 128)
    dma = pltpu.SemaphoreType.DMA
    held = pl.pallas_call(
        kernel,
        out_shape=(
            jax.ShapeDtypeStruct((32, 8, 8, 128), BF),
            jax.ShapeDtypeStruct((64, 4, 4, 64), BF),
            jax.ShapeDtypeStruct((128, 8, 128), BF),
            jax.ShapeDtypeStruct((9, 4, 64, 256), BF),
            jax.ShapeDtypeStruct((384, 128), BF),
            jax.ShapeDtypeStruct((1, 128), F32),
        ),
        in_specs=[hbm] * 8,
        out_specs=(vm,) * 6,
        scratch_shapes=[
            pltpu.VMEM((10, 32, 8, 128), BF),
            pltpu.VMEM((1024, 1280), BF),
            pltpu.VMEM((2, 8, 32, 128), BF),
            pltpu.VMEM((2, 10, 32, 128), BF),
            pltpu.VMEM((27, 32, 32), BF),
            pltpu.VMEM((27, 32, 64), BF),
            pltpu.VMEM((1, 32), F32),
            pltpu.VMEM((1, 64), F32),
            pltpu.VMEM(TABLE.shape, BF),
            pltpu.VMEM((288, 128), BF),
            pltpu.VMEM((9, 256, 256), BF),
            pltpu.VMEM((3, 256, 1024), BF),
            pltpu.VMEM((4, 256, 256), F32),
            pltpu.VMEM((576, 128), BF),
            pltpu.VMEM((9, 256, 128), BF),
            pltpu.VMEM((3, 256, 640), BF),
            pltpu.VMEM((256, 128), F32),
            pltpu.VMEM((256, 128), F32),
            pltpu.VMEM((256, 128), F32),
            pltpu.VMEM((4, 128, 128), BF),
            pltpu.VMEM((2, 2, 32, 128), BF),
            pltpu.VMEM((2, 4, 32, 128), BF),
            pltpu.VMEM((640, 640), BF),
            pltpu.VMEM((256, 256), F32),
            pltpu.VMEM((256, 256), BF),
            pltpu.VMEM((16, 8, 128), BF),
            dma((8,)), dma((8,)), dma((8,)), dma((8,)), dma((10,)), dma((10,)),
            dma, dma, pltpu.SemaphoreType.REGULAR((2,)),
        ],
        compiler_params=pltpu.CompilerParams(
            collective_id=0, has_side_effects=True, vmem_limit_bytes=40 * 1024 * 1024
        ),
    )(
        *(
            pltpu.with_memory_space_constraint(a, pltpu.HBM)
            for a in (features, weight_two, bias_two[None], w3, bias_three[None], w4, bias_four[None], table)
        )
    )
    level_two, level_three, bottleneck = pl.pallas_call(
        last,
        out_shape=(
            jax.ShapeDtypeStruct((32, 8, 8, 128), BF),
            jax.ShapeDtypeStruct((64, 4, 4, 64), BF),
            jax.ShapeDtypeStruct((512, 2, 128), BF),
        ),
        in_specs=[vm] * 6,
        out_specs=(hbm,) * 3,
        scratch_shapes=[
            pltpu.VMEM((3, 576, 256), BF),
            pltpu.VMEM((512, 2, 128), BF),
            dma((4,)),
        ],
        compiler_params=pltpu.CompilerParams(vmem_limit_bytes=40 * 1024 * 1024),
    )(*held)
    return level_two, level_three, bottleneck.reshape(16, 32, 2, 128).transpose(3, 0, 1, 2)


def solution(mesh):
    return jax.shard_map(
        shards,
        mesh=mesh,
        in_specs=(P(None, "gx", "gy", None), P(), P(), P(), P(), P(), P()),
        out_specs=(P(None, "gx", "gy", None), P(None, "gx", "gy", None), P(None, None, None, "gy")),
        check_vma=False,
    )
```

```python
import functools

import jax
import jax.numpy as jnp
import numpy as np
from jax import lax
from jax.experimental import pallas as pl
from jax.experimental.pallas import tpu as pltpu
from jax.sharding import PartitionSpec as P

BF = jnp.bfloat16
F32 = jnp.float32
MESH = pl.DeviceIdType.MESH
PIECES = 2


def tables():
    parts, at, row = [], {}, 0

    def add(name, matrix):
        nonlocal row
        rows, lanes = matrix.shape
        full = np.zeros((-(-rows // 16) * 16, 256), np.float32)
        full[:rows, :lanes] = matrix
        at[name] = row
        parts.append(full)
        row += full.shape[0]

    spread = np.zeros((8, 128, 256))
    for y in range(8):
        for dy in range(3):
            if 0 <= y + dy - 1 < 8:
                for c in range(32):
                    spread[y, dy * 32 + c, c * 8 + y + dy - 1] = 1
    add("spread_two", spread.reshape(1024, 256))
    order = np.zeros((256, 256))
    for y in range(8):
        for o in range(32):
            order[o * 8 + y, y * 32 + o] = 1
    add("order_two", order)
    edge = np.zeros((256, 64))
    for o in range(32):
        edge[o * 8, o] = 1
        edge[o * 8 + 7, 32 + o] = 1
    add("edge_two", edge)
    pool = np.zeros((2, 2, 128, 128))
    for half in range(2):
        for x in range(2):
            for z in range(128):
                pool[half, x, z, half * 64 + z // 2] = 0.125
    add("pool_two", pool.reshape(512, 128))
    select = np.zeros((64, 128))
    for c in range(32):
        select[c, c * 4] = 1
        select[32 + c, c * 4 + 3] = 1
    add("select_three", select)
    add("unit", np.eye(64))
    spread = np.zeros((4, 128, 128))
    for y in range(4):
        for dy in range(3):
            if 0 <= y + dy - 1 < 4:
                for c in range(32):
                    spread[y, dy * 32 + c, c * 4 + y + dy - 1] = 1
    add("spread_three", spread.reshape(512, 128))
    order = np.zeros((256, 256))
    for y in range(4):
        for o in range(64):
            order[o * 4 + y, y * 64 + o] = 1
    add("order_three", order)
    edge = np.zeros((256, 128))
    for o in range(64):
        edge[o * 4, o] = 1
        edge[o * 4 + 3, 64 + o] = 1
    add("edge_three", edge)
    pick = np.zeros((2, 16, 2, 2, 2, 4, 64))
    for odd in range(2):
        for target in range(16):
            for half in range(2):
                z = (2 * target - 1 + 2 * half + odd) % 32
                for x in range(2):
                    pick[odd, target, half, x, :, 2 * x : 2 * x + 2, 2 * z : 2 * z + 2] = 0.125
    add("pick_four", pick.reshape(256, 256))
    gather = np.zeros((2, 256, 128))
    for odd in range(2):
        for o in range(64):
            gather[odd, o * 4 : o * 4 + 4, odd * 64 + o] = 1
    add("gather_four", gather.reshape(512, 128))
    turn = np.zeros((3, 2, 2, 32, 16, 2, 2, 2))
    for dy in range(3):
        for half in range(2):
            for x in range(2):
                for y in range(32):
                    source = (y + dy - 1) % 32
                    turn[dy, half, x, y, source // 2, half, x, source % 2] = 1
    add("turn_four", turn.reshape(384, 128))
    return np.concatenate(parts).astype(jnp.bfloat16), at


TABLE, AT = tables()


def mm(a, b):
    return jnp.dot(a, b, preferred_element_type=F32)


def mm_t(a, b):
    return lax.dot_general(a, b, (((1,), (1,)), ((), ())), preferred_element_type=F32)


def leaky(t):
    return jnp.maximum(t, 0.1 * t)


def rolled_64(v, back):
    lane = lax.broadcasted_iota(jnp.int32, v.shape, 1) % 64
    if back:
        return jnp.where(lane == 0, pltpu.roll(v, 65, 1), pltpu.roll(v, 1, 1))
    return jnp.where(lane == 63, pltpu.roll(v, 63, 1), pltpu.roll(v, 127, 1))


def kernel(
    feat, w2_in, b2_in, w3_in, b3_in, w4_in, b4_in, tab_in,
    out2, out3, pp, w4, b4,
    fx, fm, hs, hr, w2, w3, b2, b3, tab, wc2, z2, t2, a2, wc3, z3, t3, bias2, bias3,
    pooled, own3, hs3, hr3, d3, a3, l3, sa, rb,
    load_sem, feat_sem, send_sem, recv_sem, send3_sem, recv3_sem, senda_sem, recva_sem, wide_sem,
):
    gx, gy = lax.axis_index("gx"), lax.axis_index("gy")
    xp, xm = lax.rem(gx + 1, 8), lax.rem(gx + 7, 8)
    yp, ym = lax.rem(gy + 1, 16), lax.rem(gy + 15, 16)

    def table(name, rows, lanes, skip=0):
        start = AT[name] + skip
        return tab[start : start + rows, :lanes]

    barrier = pltpu.get_barrier_semaphore()

    def greet(semaphore, dx, dy):
        pl.semaphore_signal(
            semaphore, inc=1, device_id=(lax.rem(gx + dx + 8, 8), lax.rem(gy + dy + 16, 16)), device_id_type=MESH
        )

    around = [(dx, dy) for dx in (-1, 0, 1) for dy in (-1, 0, 1) if dx or dy]
    for dx, dy in around:
        greet(barrier, dx, dy)

    loads = [
        pltpu.make_async_copy(feat.at[:, x], fx.at[x + 1], feat_sem.at[x]) for x in range(8)
    ]
    others = [
        pltpu.make_async_copy(tab_in, tab, load_sem.at[0]),
        pltpu.make_async_copy(w2_in, w2, load_sem.at[1]),
        pltpu.make_async_copy(b2_in, b2, load_sem.at[2]),
        pltpu.make_async_copy(w3_in, w3, load_sem.at[3]),
        pltpu.make_async_copy(b3_in, b3, load_sem.at[4]),
        pltpu.make_async_copy(b4_in, b4, load_sem.at[5]),
        pltpu.make_async_copy(w4_in, w4.at[:, 0:3, :, 0:128], load_sem.at[6]),
        pltpu.make_async_copy(w4_in, w4.at[:, 1:4, :, 128:256], load_sem.at[7]),
    ]
    for x in (0, 7, 1, 2, 3, 4, 5, 6):
        loads[x].start()


    def remote(src, dst, send, recv, x, y):
        return pltpu.make_async_remote_copy(
            src_ref=src, dst_ref=dst, send_sem=send, recv_sem=recv,
            device_id=(x, y), device_id_type=MESH,
        )

    def place(x):
        v = fx[x].astype(F32).reshape(256, 128)
        lanes = slice(x * 128, x * 128 + 128)
        fm[256:512, lanes] = v.astype(BF)

    def shift(x):
        lanes = slice(x * 128, x * 128 + 128)
        v = fm[256:512, lanes].astype(F32)
        fm[0:256, lanes] = pltpu.roll(v, 1, 1).astype(BF)
        fm[512:768, lanes] = pltpu.roll(v, 127, 1).astype(BF)

    row = lax.broadcasted_iota(jnp.int32, (64, 256), 0)
    lane = lax.broadcasted_iota(jnp.int32, (64, 256), 1)
    select = jnp.where(lane == row % 32 * 8 + row // 32 * 7, 1.0, 0.0).astype(BF)
    def cut(side_rows, x):
        for side in range(2):
            hs[side, x] = side_rows[side * 32 : side * 32 + 32]

    for x in (0, 7):
        loads[x].wait()
        place(x + 1)
        cut(mm(select, fm[256:512, x * 128 + 128 : x * 128 + 256]).astype(BF), x)
    pl.semaphore_wait(barrier, 8)
    first = [
        remote(fx.at[8], fx.at[0], send_sem.at[0], recv_sem.at[0], xp, gy),
        remote(fx.at[1], fx.at[9], send_sem.at[1], recv_sem.at[1], xm, gy),
    ]
    second = [
        remote(hs.at[1, 7], hr.at[0, 0], send_sem.at[4], recv_sem.at[4], xp, yp),
        remote(hs.at[1, 0], hr.at[0, 9], send_sem.at[5], recv_sem.at[5], xm, yp),
        remote(hs.at[0, 7], hr.at[1, 0], send_sem.at[6], recv_sem.at[6], xp, ym),
        remote(hs.at[0, 0], hr.at[1, 9], send_sem.at[7], recv_sem.at[7], xm, ym),
        remote(hs.at[1], hr.at[0, 1:9], send_sem.at[2], recv_sem.at[2], gx, yp),
        remote(hs.at[0], hr.at[1, 1:9], send_sem.at[3], recv_sem.at[3], gx, ym),
    ]
    for copy in second[:4] + first:
        copy.start()
    for x in range(1, 7):
        loads[x].wait()
        place(x + 1)
    for copy in others:
        copy.start()
    edges = mm(select, fm[256:512, 256:1024]).astype(BF)
    for x in range(1, 7):
        cut(edges[:, (x - 1) * 128 : x * 128], x)
    for copy in second[4:]:
        copy.start()

    for x in range(1, 9):
        shift(x)
    for copy in others:
        copy.wait()
    gap = jnp.zeros((32, 32), F32)
    for dx in range(3):
        for dz in range(3):
            k = 3 * dx + dz
            wc2[k * 32 : k * 32 + 32, :] = jnp.concatenate(
                [w2[9 * dx + 3 * dy + dz].astype(F32) for dy in range(3)] + [gap], axis=1
            ).astype(BF)
    for y in range(8):
        z2[:, y * 32 : y * 32 + 32, :] = (
            mm(wc2[...], table("spread_two", 128, 256, 128 * y)).astype(BF).reshape(9, 32, 256)
        )
    for dx in range(3):
        for dz in range(3):
            t2[dx, :, dz * 256 : dz * 256 + 256] = mm(
                table("order_two", 256, 256), z2[3 * dx + dz]
            ).astype(BF)
        low = [w2[9 * dx + dz].astype(F32) for dz in range(3)]
        high = [w2[9 * dx + 6 + dz].astype(F32) for dz in range(3)]
        z_edge = jnp.concatenate(
            [
                jnp.concatenate([low[0], gap, low[1], gap, low[2], gap, gap, gap], axis=1),
                jnp.concatenate([gap, high[0], gap, high[1], gap, high[2], gap, gap], axis=1),
            ],
            axis=0,
        ).astype(BF)
        t2[dx, :, 768:1024] = mm(table("edge_two", 256, 64), z_edge).astype(BF)
    row = lax.broadcasted_iota(jnp.int32, (256, 32), 0) // 8
    lane = lax.broadcasted_iota(jnp.int32, (256, 32), 1)
    column = jnp.sum(jnp.where(row == lane, b2[...], 0.0), axis=1, keepdims=True)
    bias2[...] = jnp.broadcast_to(column, (256, 128))

    fm[0:768, 0:128] = jnp.zeros((768, 128), BF)
    fm[0:768, 1152:1280] = jnp.zeros((768, 128), BF)
    fm[960:1024, :] = jnp.zeros((64, 1280), BF)

    def inner(p, carry):
        a2[p] = mm(
            jnp.concatenate([t2[dx, :, 0:768] for dx in range(3)], axis=1),
            jnp.concatenate(
                [fm[0:768, pl.ds(pl.multiple_of((p * 2 + dx) * 128, 128), 256)] for dx in range(3)], axis=0
            ),
        )
        return carry

    lax.fori_loop(0, 4, inner, 0)

    for copy in first:
        copy.wait()
    for x in (0, 9):
        place(x)
        shift(x)
    a2[0, :, 0:128] += mm(t2[0, :, 0:768], fm[0:768, 0:128])
    a2[3, :, 128:256] += mm(t2[2, :, 0:768], fm[0:768, 1152:1280])
    for copy in second:
        copy.wait()
    for dx, dy in around:
        greet(wide_sem.at[0], 2 * dx, 2 * dy)
    for x in range(10):
        v = jnp.concatenate([hr[0, x], hr[1, x]], axis=0).astype(F32)
        lanes = slice(x * 128, x * 128 + 128)
        fm[768:832, lanes] = pltpu.roll(v, 1, 1).astype(BF)
        fm[832:896, lanes] = v.astype(BF)
        fm[896:960, lanes] = pltpu.roll(v, 127, 1).astype(BF)

    third = []

    def send3(src, dst, x, y):
        k = len(third)
        third.append(remote(src, dst, send3_sem.at[k], recv3_sem.at[k], x, y))
        third[-1].start()

    for q in range(2):
        total = jnp.zeros((256, 128), F32)
        for half in range(2):
            p = ((3, 0), (1, 2))[q][half]
            acc = a2[p] + mm(
                jnp.concatenate([t2[dx, :, 768:1024] for dx in range(3)], axis=1),
                jnp.concatenate(
                    [fm[768:1024, (p * 2 + dx) * 128 : (p * 2 + dx + 2) * 128] for dx in range(3)], axis=0
                ),
            )
            for x in range(2):
                v = leaky(acc[:, x * 128 : x * 128 + 128] + bias2[...])
                out2[:, 2 * p + x] = v.reshape(32, 8, 128).astype(BF)
                total = total + mm(v.astype(BF), table("pool_two", 128, 128, half * 256 + x * 128))
        pooled[...] = total
        mean = (pooled[pl.ds(0, 128, stride=2), :] + pooled[pl.ds(1, 128, stride=2), :]).astype(BF)
        own3[q + 1] = mean
        picked = mm(table("select_three", 64, 128), mean).astype(BF)
        hs3[0, q] = picked[0:32]
        hs3[1, q] = picked[32:64]
        if q == 0:
            for x, slot in ((xm, 3), (xp, 0)):
                send3(hs3.at[1, 0], hr3.at[0, slot], x, yp)
                send3(hs3.at[0, 0], hr3.at[1, slot], x, ym)
                send3(own3.at[1], own3.at[slot], x, gy)
        send3(hs3.at[1, q], hr3.at[0, q + 1], gx, yp)
        send3(hs3.at[0, q], hr3.at[1, q + 1], gx, ym)

    for dx in range(3):
        for dz in range(3):
            k = 3 * dx + dz
            stack = jnp.concatenate(
                [w3[9 * dx + 3 * dy + dz] for dy in range(3)] + [jnp.zeros((32, 64), BF)], axis=0
            )
            wc3[k * 64 : k * 64 + 64, :] = mm_t(table("unit", 64, 64), stack).astype(BF)
    for y in range(4):
        z3[:, y * 64 : y * 64 + 64, :] = (
            mm(wc3[...], table("spread_three", 128, 128, 128 * y)).astype(BF).reshape(9, 64, 128)
        )
    gap = jnp.zeros((64, 32), F32)
    for dx in range(3):
        low, high = [], []
        for dz in range(3):
            k = 3 * dx + dz
            t3[dx, :, dz * 128 : dz * 128 + 128] = mm(table("order_three", 256, 256), z3[k]).astype(BF)
            block = wc3[k * 64 : k * 64 + 64, :].astype(F32)
            low.append(block[:, 0:32])
            high.append(block[:, 64:96])
        z_edge = jnp.concatenate(
            [
                jnp.concatenate([low[0], gap, low[1], gap, low[2], gap, gap, gap], axis=1),
                jnp.concatenate([gap, high[0], gap, high[1], gap, high[2], gap, gap], axis=1),
            ],
            axis=0,
        ).astype(BF)
        t3[dx, :, 384:640] = mm(table("edge_three", 256, 128), z_edge).astype(BF)
    row = lax.broadcasted_iota(jnp.int32, (256, 64), 0) // 4
    lane = lax.broadcasted_iota(jnp.int32, (256, 64), 1)
    column = jnp.sum(jnp.where(row == lane, b3[...], 0.0), axis=1, keepdims=True)
    bias3[...] = jnp.broadcast_to(column, (256, 128))

    w4[:, 3, :, 0:128] = jnp.zeros((9, 64, 128), BF)
    w4[:, 0, :, 128:256] = jnp.zeros((9, 64, 128), BF)

    left = lax.broadcasted_iota(jnp.int32, (128, 128), 1) < 64

    def three(rows, lanes, v):
        for dz, u in enumerate((rolled_64(v, True), v, rolled_64(v, False))):
            start = dz * 128 if rows == 128 else 384 + dz * 64
            d3[start : start + rows, lanes * 128 : lanes * 128 + 128] = u.astype(BF)

    outer, middle = own3[1].astype(F32), own3[2].astype(F32)
    outer_turned, middle_turned = pltpu.roll(outer, 64, 1), pltpu.roll(middle, 64, 1)
    three(128, 0, jnp.where(left, outer_turned, middle_turned))
    three(128, 1, jnp.where(left, middle_turned, outer_turned))
    three(128, 3, middle)
    bias = bias3[...]
    a3[...] = mm(t3[1, :, 0:384], d3[0:384, 0:256]) + jnp.concatenate([bias, bias], axis=1)
    d3[576:640, :] = jnp.zeros((64, 640), BF)
    pl.semaphore_wait(wide_sem.at[0], 8)
    for dy in (-4, 4):
        greet(wide_sem.at[1], 0, dy)
    for copy in third:
        copy.wait()
    three(128, 2, jnp.where(left, own3[0].astype(F32), outer))
    three(128, 4, jnp.where(left, outer, own3[3].astype(F32)))
    edge = [jnp.concatenate([hr3[0, t], hr3[1, t]], axis=0).astype(F32) for t in range(4)]
    turned = [pltpu.roll(edge[t], 64, 1) for t in (1, 2)]
    left = lax.broadcasted_iota(jnp.int32, (64, 128), 1) < 64
    three(64, 0, jnp.where(left, turned[0], turned[1]))
    three(64, 1, jnp.where(left, turned[1], turned[0]))
    three(64, 2, jnp.where(left, edge[0], edge[1]))
    three(64, 3, edge[2])
    three(64, 4, jnp.where(left, edge[1], edge[3]))
    v = leaky(
        a3[...] + mm(t3[0], d3[:, 256:512]) + mm(t3[1, :, 384:640], d3[384:640, 0:256]) + mm(t3[2], d3[:, 384:640])
    )
    l3[...] = v.astype(BF)
    sums = mm_t(table("pick_four", 256, 256), l3[...])
    row = lax.broadcasted_iota(jnp.int32, (256, 256), 0) % 2
    lane = lax.broadcasted_iota(jnp.int32, (256, 256), 1) % 4 // 2
    sums = jnp.where(row == lane, sums, 0.0)
    head = sums.astype(BF)
    tail = (sums - head.astype(F32)).astype(BF)
    block = jnp.zeros((128, 128), F32)
    for odd in range(2):
        g = table("gather_four", 256, 128, odd * 256)
        block = block + mm(head[odd * 128 : odd * 128 + 128], g) + mm(tail[odd * 128 : odd * 128 + 128], g)
    sa[...] = block.reshape(16, 8, 128).astype(BF)
    pl.semaphore_wait(wide_sem.at[1], 2)
    me = gx * 16 + gy
    mine = pltpu.make_async_copy(sa.at[gy], rb.at[me], recva_sem.at[gx])
    y_at, x_at, z_at, core_at = gx // 4 * 2 + gy // 8, gx % 4, gy // 2 % 4, gy % 2
    columns, layers = {}, {}
    for d in range(4):
        y = (y_at + d) % 4
        for e in range(4):
            columns[e, d] = y // 2 * 4 + (x_at + e) % 4
            layers[d, e] = y % 2 * 8 + (z_at + e) % 4 * 2
    hops = (0, 1, 2, 1)
    steps = [(dx, dy, dz) for dx in range(4) for dy in range(4) for dz in range(4)]
    steps.sort(key=lambda step: -sum(hops[d] for d in step))
    for dx, dy, dz in steps:
        for flip in range(2):
            if dx or dy or dz or flip:
                layer = layers[dy, dz] + (core_at + flip) % 2
                remote(sa.at[layer], rb.at[me], senda_sem, recva_sem.at[gx], columns[dx, dy], layer).start()
    mine.start()
    for x in range(4):
        out3[:, x] = l3[:, x * 64 : x * 64 + 64].astype(F32).reshape(64, 4, 64).astype(BF)
    for dy in (0, 2):
        for dx in (0, 1, 3, 2):
            g = columns[dx, dy]
            here = pl.ds(g * 16, 16)
            pltpu.make_async_copy(rb.at[here], rb.at[here], recva_sem.at[g]).wait()
            moved = mm(table("turn_four", 384, 128), rb[here].astype(F32).reshape(128, 128).astype(BF)).astype(BF)
            rows = pl.ds(pl.multiple_of(g * 64, 64), 64)
            for k in range(6):
                lanes = slice(k % 2 * 128, k % 2 * 128 + 128)
                pp[k // 2, rows, lanes] = moved[k * 64 : k * 64 + 64]
    pltpu.make_async_copy(rb.at[0:127], rb.at[0:127], senda_sem).wait()


def last(out2_in, out3_in, pp, w4, b4, out2, out3, out4, l4, sem):
    leaving = [
        pltpu.make_async_copy(out2_in, out2, sem.at[0]),
        pltpu.make_async_copy(out3_in, out3, sem.at[1]),
    ]
    for copy in leaving:
        copy.start()
    bias = jnp.concatenate([b4[...], b4[...]], axis=1)
    size = 512 // PIECES
    for m in range(PIECES):
        operands = []
        for dx in range(3):
            start = m * size + (dx - 1) * 32
            for dy in range(3):
                if start < 0:
                    v = jnp.concatenate([pp[dy, 480:512, :], pp[dy, 0 : size - 32, :]], axis=0)
                elif start + size > 512:
                    v = jnp.concatenate([pp[dy, start:512, :], pp[dy, 0:32, :]], axis=0)
                else:
                    v = pp[dy, start : start + size, :]
                operands.append(v)
        v = leaky(mm(jnp.concatenate(operands, axis=1), w4[...].reshape(2304, 256)) + bias)
        piece = slice(m * size, m * size + size)
        l4[piece] = v.reshape(size, 2, 128).astype(BF)
        leaving.append(pltpu.make_async_copy(l4.at[piece], out4.at[piece], sem.at[2 + m]))
        leaving[-1].start()
    for copy in leaving:
        copy.wait()


def shards(features, weight_two, bias_two, weight_three, bias_three, weight_four, bias_four):
    vm = pl.BlockSpec(memory_space=pltpu.VMEM)
    hbm = pl.BlockSpec(memory_space=pltpu.HBM)
    table = jnp.asarray(TABLE)
    w3 = weight_three.transpose(0, 2, 1)
    w4 = weight_four.transpose(0, 2, 1).reshape(9, 3, 64, 128)
    dma = pltpu.SemaphoreType.DMA
    held = pl.pallas_call(
        kernel,
        out_shape=(
            jax.ShapeDtypeStruct((32, 8, 8, 128), BF),
            jax.ShapeDtypeStruct((64, 4, 4, 64), BF),
            jax.ShapeDtypeStruct((3, 512, 256), BF),
            jax.ShapeDtypeStruct((9, 4, 64, 256), BF),
            jax.ShapeDtypeStruct((1, 128), F32),
        ),
        in_specs=[hbm] * 8,
        out_specs=(vm,) * 5,
        scratch_shapes=[
            pltpu.VMEM((10, 32, 8, 128), BF),
            pltpu.VMEM((1024, 1280), BF),
            pltpu.VMEM((2, 8, 32, 128), BF),
            pltpu.VMEM((2, 10, 32, 128), BF),
            pltpu.VMEM((27, 32, 32), BF),
            pltpu.VMEM((27, 32, 64), BF),
            pltpu.VMEM((1, 32), F32),
            pltpu.VMEM((1, 64), F32),
            pltpu.VMEM(TABLE.shape, BF),
            pltpu.VMEM((288, 128), BF),
            pltpu.VMEM((9, 256, 256), BF),
            pltpu.VMEM((3, 256, 1024), BF),
            pltpu.VMEM((4, 256, 256), F32),
            pltpu.VMEM((576, 128), BF),
            pltpu.VMEM((9, 256, 128), BF),
            pltpu.VMEM((3, 256, 640), BF),
            pltpu.VMEM((256, 128), F32),
            pltpu.VMEM((256, 128), F32),
            pltpu.VMEM((256, 128), F32),
            pltpu.VMEM((4, 128, 128), BF),
            pltpu.VMEM((2, 2, 32, 128), BF),
            pltpu.VMEM((2, 4, 32, 128), BF),
            pltpu.VMEM((640, 640), BF),
            pltpu.VMEM((256, 256), F32),
            pltpu.VMEM((256, 256), BF),
            pltpu.VMEM((16, 8, 128), BF),
            pltpu.VMEM((128, 8, 128), BF),
            dma((8,)), dma((8,)), dma((8,)), dma((8,)), dma((10,)), dma((10,)),
            dma, dma((8,)), pltpu.SemaphoreType.REGULAR((2,)),
        ],
        compiler_params=pltpu.CompilerParams(
            collective_id=0, has_side_effects=True, vmem_limit_bytes=40 * 1024 * 1024
        ),
    )(
        *(
            pltpu.with_memory_space_constraint(a, pltpu.HBM)
            for a in (features, weight_two, bias_two[None], w3, bias_three[None], w4, bias_four[None], table)
        )
    )
    level_two, level_three, bottleneck = pl.pallas_call(
        last,
        out_shape=(
            jax.ShapeDtypeStruct((32, 8, 8, 128), BF),
            jax.ShapeDtypeStruct((64, 4, 4, 64), BF),
            jax.ShapeDtypeStruct((512, 2, 128), BF),
        ),
        in_specs=[vm] * 5,
        out_specs=(hbm,) * 3,
        scratch_shapes=[
            pltpu.VMEM((512, 2, 128), BF),
            dma((2 + PIECES,)),
        ],
        compiler_params=pltpu.CompilerParams(vmem_limit_bytes=40 * 1024 * 1024),
    )(*held)
    return level_two, level_three, bottleneck.reshape(16, 32, 2, 128).transpose(3, 0, 1, 2)


def solution(mesh):
    return jax.shard_map(
        shards,
        mesh=mesh,
        in_specs=(P(None, "gx", "gy", None), P(), P(), P(), P(), P(), P()),
        out_specs=(P(None, "gx", "gy", None), P(None, "gx", "gy", None), P(None, None, None, "gy")),
        check_vma=False,
    )
```

```python
import functools

import jax
import jax.numpy as jnp
import numpy as np
from jax import lax
from jax.experimental import pallas as pl
from jax.experimental.pallas import tpu as pltpu
from jax.sharding import PartitionSpec as P

BF = jnp.bfloat16
F32 = jnp.float32
MESH = pl.DeviceIdType.MESH
PIECES = 2


def tables():
    parts, at, row = [], {}, 0

    def add(name, matrix):
        nonlocal row
        rows, lanes = matrix.shape
        full = np.zeros((-(-rows // 16) * 16, 256), np.float32)
        full[:rows, :lanes] = matrix
        at[name] = row
        parts.append(full)
        row += full.shape[0]

    spread = np.zeros((8, 128, 256))
    for y in range(8):
        for dy in range(3):
            if 0 <= y + dy - 1 < 8:
                for c in range(32):
                    spread[y, dy * 32 + c, c * 8 + y + dy - 1] = 1
    add("spread_two", spread.reshape(1024, 256))
    order = np.zeros((256, 256))
    for y in range(8):
        for o in range(32):
            order[o * 8 + y, y * 32 + o] = 1
    add("order_two", order)
    edge = np.zeros((256, 64))
    for o in range(32):
        edge[o * 8, o] = 1
        edge[o * 8 + 7, 32 + o] = 1
    add("edge_two", edge)
    pool = np.zeros((2, 2, 128, 128))
    for half in range(2):
        for x in range(2):
            for z in range(128):
                pool[half, x, z, half * 64 + z // 2] = 0.125
    add("pool_two", pool.reshape(512, 128))
    select = np.zeros((64, 128))
    for c in range(32):
        select[c, c * 4] = 1
        select[32 + c, c * 4 + 3] = 1
    add("select_three", select)
    add("unit", np.eye(64))
    spread = np.zeros((4, 128, 128))
    for y in range(4):
        for dy in range(3):
            if 0 <= y + dy - 1 < 4:
                for c in range(32):
                    spread[y, dy * 32 + c, c * 4 + y + dy - 1] = 1
    add("spread_three", spread.reshape(512, 128))
    order = np.zeros((256, 256))
    for y in range(4):
        for o in range(64):
            order[o * 4 + y, y * 64 + o] = 1
    add("order_three", order)
    edge = np.zeros((256, 128))
    for o in range(64):
        edge[o * 4, o] = 1
        edge[o * 4 + 3, 64 + o] = 1
    add("edge_three", edge)
    pick = np.zeros((2, 16, 2, 2, 2, 4, 64))
    for odd in range(2):
        for target in range(16):
            for half in range(2):
                z = (2 * target - 1 + 2 * half + odd) % 32
                for x in range(2):
                    pick[odd, target, half, x, :, 2 * x : 2 * x + 2, 2 * z : 2 * z + 2] = 0.125
    add("pick_four", pick.reshape(256, 256))
    gather = np.zeros((2, 256, 128))
    for odd in range(2):
        for o in range(64):
            gather[odd, o * 4 : o * 4 + 4, odd * 64 + o] = 1
    add("gather_four", gather.reshape(512, 128))
    turn = np.zeros((3, 2, 2, 32, 16, 2, 2, 2))
    for dy in range(3):
        for half in range(2):
            for x in range(2):
                for y in range(32):
                    source = (y + dy - 1) % 32
                    turn[dy, half, x, y, source // 2, half, x, source % 2] = 1
    add("turn_four", turn.reshape(384, 128))
    return np.concatenate(parts).astype(jnp.bfloat16), at


TABLE, AT = tables()


def mm(a, b):
    return jnp.dot(a, b, preferred_element_type=F32)


def mm_t(a, b):
    return lax.dot_general(a, b, (((1,), (1,)), ((), ())), preferred_element_type=F32)


def leaky(t):
    return jnp.maximum(t, 0.1 * t)


def rolled_64(v, back):
    lane = lax.broadcasted_iota(jnp.int32, v.shape, 1) % 64
    if back:
        return jnp.where(lane == 0, pltpu.roll(v, 65, 1), pltpu.roll(v, 1, 1))
    return jnp.where(lane == 63, pltpu.roll(v, 63, 1), pltpu.roll(v, 127, 1))


def kernel(
    feat, w2_in, b2_in, w3_in, b3_in, w4_in, b4_in, tab_in,
    out2, out3, rb, w4, turn, b4,
    fx, fm, hs, hr, w2, w3, b2, b3, tab, wc2, z2, t2, a2, wc3, z3, t3, bias2, bias3,
    pooled, own3, hs3, hr3, d3, a3, l3, sa,
    load_sem, feat_sem, send_sem, recv_sem, send3_sem, recv3_sem, senda_sem, recva_sem, wide_sem,
):
    gx, gy = lax.axis_index("gx"), lax.axis_index("gy")
    xp, xm = lax.rem(gx + 1, 8), lax.rem(gx + 7, 8)
    yp, ym = lax.rem(gy + 1, 16), lax.rem(gy + 15, 16)

    def table(name, rows, lanes, skip=0):
        start = AT[name] + skip
        return tab[start : start + rows, :lanes]

    barrier = pltpu.get_barrier_semaphore()

    def greet(semaphore, dx, dy):
        pl.semaphore_signal(
            semaphore, inc=1, device_id=(lax.rem(gx + dx + 8, 8), lax.rem(gy + dy + 16, 16)), device_id_type=MESH
        )

    around = [(dx, dy) for dx in (-1, 0, 1) for dy in (-1, 0, 1) if dx or dy]
    for dx, dy in around:
        greet(barrier, dx, dy)

    loads = [
        pltpu.make_async_copy(feat.at[:, x], fx.at[x + 1], feat_sem.at[x]) for x in range(8)
    ]
    others = [
        pltpu.make_async_copy(tab_in, tab, load_sem.at[0]),
        pltpu.make_async_copy(w2_in, w2, load_sem.at[1]),
        pltpu.make_async_copy(b2_in, b2, load_sem.at[2]),
        pltpu.make_async_copy(w3_in, w3, load_sem.at[3]),
        pltpu.make_async_copy(b3_in, b3, load_sem.at[4]),
        pltpu.make_async_copy(b4_in, b4, load_sem.at[5]),
        pltpu.make_async_copy(w4_in, w4.at[:, 0:3, :, 0:128], load_sem.at[6]),
        pltpu.make_async_copy(w4_in, w4.at[:, 1:4, :, 128:256], load_sem.at[7]),
    ]
    for x in (0, 7, 1, 2, 3, 4, 5, 6):
        loads[x].start()
    for copy in others:
        copy.start()


    def remote(src, dst, send, recv, x, y):
        return pltpu.make_async_remote_copy(
            src_ref=src, dst_ref=dst, send_sem=send, recv_sem=recv,
            device_id=(x, y), device_id_type=MESH,
        )

    def place(x):
        v = fx[x].astype(F32).reshape(256, 128)
        lanes = slice(x * 128, x * 128 + 128)
        fm[256:512, lanes] = v.astype(BF)

    def shift(x):
        lanes = slice(x * 128, x * 128 + 128)
        v = fm[256:512, lanes].astype(F32)
        fm[0:256, lanes] = pltpu.roll(v, 1, 1).astype(BF)
        fm[512:768, lanes] = pltpu.roll(v, 127, 1).astype(BF)

    row = lax.broadcasted_iota(jnp.int32, (64, 256), 0)
    lane = lax.broadcasted_iota(jnp.int32, (64, 256), 1)
    select = jnp.where(lane == row % 32 * 8 + row // 32 * 7, 1.0, 0.0).astype(BF)
    def cut(side_rows, x):
        for side in range(2):
            hs[side, x] = side_rows[side * 32 : side * 32 + 32]

    for x in (0, 7):
        loads[x].wait()
        place(x + 1)
        cut(mm(select, fm[256:512, x * 128 + 128 : x * 128 + 256]).astype(BF), x)
    pl.semaphore_wait(barrier, 8)
    first = [
        remote(fx.at[8], fx.at[0], send_sem.at[0], recv_sem.at[0], xp, gy),
        remote(fx.at[1], fx.at[9], send_sem.at[1], recv_sem.at[1], xm, gy),
    ]
    second = [
        remote(hs.at[1, 7], hr.at[0, 0], send_sem.at[4], recv_sem.at[4], xp, yp),
        remote(hs.at[1, 0], hr.at[0, 9], send_sem.at[5], recv_sem.at[5], xm, yp),
        remote(hs.at[0, 7], hr.at[1, 0], send_sem.at[6], recv_sem.at[6], xp, ym),
        remote(hs.at[0, 0], hr.at[1, 9], send_sem.at[7], recv_sem.at[7], xm, ym),
        remote(hs.at[1], hr.at[0, 1:9], send_sem.at[2], recv_sem.at[2], gx, yp),
        remote(hs.at[0], hr.at[1, 1:9], send_sem.at[3], recv_sem.at[3], gx, ym),
    ]
    for copy in second[:4] + first:
        copy.start()
    for x in range(1, 7):
        loads[x].wait()
        place(x + 1)
    edges = mm(select, fm[256:512, 256:1024]).astype(BF)
    for x in range(1, 7):
        cut(edges[:, (x - 1) * 128 : x * 128], x)
    for copy in second[4:]:
        copy.start()

    for x in range(1, 9):
        shift(x)
    for copy in others:
        copy.wait()
    gap = jnp.zeros((32, 32), F32)
    for dx in range(3):
        for dz in range(3):
            k = 3 * dx + dz
            wc2[k * 32 : k * 32 + 32, :] = jnp.concatenate(
                [w2[9 * dx + 3 * dy + dz].astype(F32) for dy in range(3)] + [gap], axis=1
            ).astype(BF)
    for y in range(8):
        z2[:, y * 32 : y * 32 + 32, :] = (
            mm(wc2[...], table("spread_two", 128, 256, 128 * y)).astype(BF).reshape(9, 32, 256)
        )
    for dx in range(3):
        for dz in range(3):
            t2[dx, :, dz * 256 : dz * 256 + 256] = mm(
                table("order_two", 256, 256), z2[3 * dx + dz]
            ).astype(BF)
        low = [w2[9 * dx + dz].astype(F32) for dz in range(3)]
        high = [w2[9 * dx + 6 + dz].astype(F32) for dz in range(3)]
        z_edge = jnp.concatenate(
            [
                jnp.concatenate([low[0], gap, low[1], gap, low[2], gap, gap, gap], axis=1),
                jnp.concatenate([gap, high[0], gap, high[1], gap, high[2], gap, gap], axis=1),
            ],
            axis=0,
        ).astype(BF)
        t2[dx, :, 768:1024] = mm(table("edge_two", 256, 64), z_edge).astype(BF)
    row = lax.broadcasted_iota(jnp.int32, (256, 32), 0) // 8
    lane = lax.broadcasted_iota(jnp.int32, (256, 32), 1)
    column = jnp.sum(jnp.where(row == lane, b2[...], 0.0), axis=1, keepdims=True)
    bias2[...] = jnp.broadcast_to(column, (256, 128))

    fm[0:768, 0:128] = jnp.zeros((768, 128), BF)
    fm[0:768, 1152:1280] = jnp.zeros((768, 128), BF)
    fm[960:1024, :] = jnp.zeros((64, 1280), BF)

    def inner(p, carry):
        a2[p] = mm(
            jnp.concatenate([t2[dx, :, 0:768] for dx in range(3)], axis=1),
            jnp.concatenate(
                [fm[0:768, pl.ds(pl.multiple_of((p * 2 + dx) * 128, 128), 256)] for dx in range(3)], axis=0
            ),
        )
        return carry

    lax.fori_loop(0, 4, inner, 0)

    for copy in first:
        copy.wait()
    for x in (0, 9):
        place(x)
        shift(x)
    a2[0, :, 0:128] += mm(t2[0, :, 0:768], fm[0:768, 0:128])
    a2[3, :, 128:256] += mm(t2[2, :, 0:768], fm[0:768, 1152:1280])
    for copy in second:
        copy.wait()
    for dx, dy in around:
        greet(wide_sem.at[0], 2 * dx, 2 * dy)
    for x in range(10):
        v = jnp.concatenate([hr[0, x], hr[1, x]], axis=0).astype(F32)
        lanes = slice(x * 128, x * 128 + 128)
        fm[768:832, lanes] = pltpu.roll(v, 1, 1).astype(BF)
        fm[832:896, lanes] = v.astype(BF)
        fm[896:960, lanes] = pltpu.roll(v, 127, 1).astype(BF)

    third = []

    def send3(src, dst, x, y):
        k = len(third)
        third.append(remote(src, dst, send3_sem.at[k], recv3_sem.at[k], x, y))
        third[-1].start()

    for q in range(2):
        total = jnp.zeros((256, 128), F32)
        for half in range(2):
            p = ((3, 0), (1, 2))[q][half]
            acc = a2[p] + mm(
                jnp.concatenate([t2[dx, :, 768:1024] for dx in range(3)], axis=1),
                jnp.concatenate(
                    [fm[768:1024, (p * 2 + dx) * 128 : (p * 2 + dx + 2) * 128] for dx in range(3)], axis=0
                ),
            )
            for x in range(2):
                v = leaky(acc[:, x * 128 : x * 128 + 128] + bias2[...])
                out2[:, 2 * p + x] = v.reshape(32, 8, 128).astype(BF)
                total = total + mm(v.astype(BF), table("pool_two", 128, 128, half * 256 + x * 128))
        pooled[...] = total
        mean = (pooled[pl.ds(0, 128, stride=2), :] + pooled[pl.ds(1, 128, stride=2), :]).astype(BF)
        own3[q + 1] = mean
        picked = mm(table("select_three", 64, 128), mean).astype(BF)
        hs3[0, q] = picked[0:32]
        hs3[1, q] = picked[32:64]
        if q == 0:
            for x, slot in ((xm, 3), (xp, 0)):
                send3(hs3.at[1, 0], hr3.at[0, slot], x, yp)
                send3(hs3.at[0, 0], hr3.at[1, slot], x, ym)
                send3(own3.at[1], own3.at[slot], x, gy)
        send3(hs3.at[1, q], hr3.at[0, q + 1], gx, yp)
        send3(hs3.at[0, q], hr3.at[1, q + 1], gx, ym)

    for dx in range(3):
        for dz in range(3):
            k = 3 * dx + dz
            stack = jnp.concatenate(
                [w3[9 * dx + 3 * dy + dz] for dy in range(3)] + [jnp.zeros((32, 64), BF)], axis=0
            )
            wc3[k * 64 : k * 64 + 64, :] = mm_t(table("unit", 64, 64), stack).astype(BF)
    for y in range(4):
        z3[:, y * 64 : y * 64 + 64, :] = (
            mm(wc3[...], table("spread_three", 128, 128, 128 * y)).astype(BF).reshape(9, 64, 128)
        )
    gap = jnp.zeros((64, 32), F32)
    for dx in range(3):
        low, high = [], []
        for dz in range(3):
            k = 3 * dx + dz
            t3[dx, :, dz * 128 : dz * 128 + 128] = mm(table("order_three", 256, 256), z3[k]).astype(BF)
            block = wc3[k * 64 : k * 64 + 64, :].astype(F32)
            low.append(block[:, 0:32])
            high.append(block[:, 64:96])
        z_edge = jnp.concatenate(
            [
                jnp.concatenate([low[0], gap, low[1], gap, low[2], gap, gap, gap], axis=1),
                jnp.concatenate([gap, high[0], gap, high[1], gap, high[2], gap, gap], axis=1),
            ],
            axis=0,
        ).astype(BF)
        t3[dx, :, 384:640] = mm(table("edge_three", 256, 128), z_edge).astype(BF)
    row = lax.broadcasted_iota(jnp.int32, (256, 64), 0) // 4
    lane = lax.broadcasted_iota(jnp.int32, (256, 64), 1)
    column = jnp.sum(jnp.where(row == lane, b3[...], 0.0), axis=1, keepdims=True)
    bias3[...] = jnp.broadcast_to(column, (256, 128))

    w4[:, 3, :, 0:128] = jnp.zeros((9, 64, 128), BF)
    w4[:, 0, :, 128:256] = jnp.zeros((9, 64, 128), BF)

    left = lax.broadcasted_iota(jnp.int32, (128, 128), 1) < 64

    def three(rows, lanes, v):
        for dz, u in enumerate((rolled_64(v, True), v, rolled_64(v, False))):
            start = dz * 128 if rows == 128 else 384 + dz * 64
            d3[start : start + rows, lanes * 128 : lanes * 128 + 128] = u.astype(BF)

    outer, middle = own3[1].astype(F32), own3[2].astype(F32)
    outer_turned, middle_turned = pltpu.roll(outer, 64, 1), pltpu.roll(middle, 64, 1)
    three(128, 0, jnp.where(left, outer_turned, middle_turned))
    three(128, 1, jnp.where(left, middle_turned, outer_turned))
    three(128, 3, middle)
    bias = bias3[...]
    a3[...] = mm(t3[1, :, 0:384], d3[0:384, 0:256]) + jnp.concatenate([bias, bias], axis=1)
    d3[576:640, :] = jnp.zeros((64, 640), BF)
    pl.semaphore_wait(wide_sem.at[0], 8)
    for dy in (-4, 4):
        greet(wide_sem.at[1], 0, dy)
    for copy in third:
        copy.wait()
    three(128, 2, jnp.where(left, own3[0].astype(F32), outer))
    three(128, 4, jnp.where(left, outer, own3[3].astype(F32)))
    edge = [jnp.concatenate([hr3[0, t], hr3[1, t]], axis=0).astype(F32) for t in range(4)]
    turned = [pltpu.roll(edge[t], 64, 1) for t in (1, 2)]
    left = lax.broadcasted_iota(jnp.int32, (64, 128), 1) < 64
    three(64, 0, jnp.where(left, turned[0], turned[1]))
    three(64, 1, jnp.where(left, turned[1], turned[0]))
    three(64, 2, jnp.where(left, edge[0], edge[1]))
    three(64, 3, edge[2])
    three(64, 4, jnp.where(left, edge[1], edge[3]))
    v = leaky(
        a3[...] + mm(t3[0], d3[:, 256:512]) + mm(t3[1, :, 384:640], d3[384:640, 0:256]) + mm(t3[2], d3[:, 384:640])
    )
    l3[...] = v.astype(BF)
    sums = mm_t(table("pick_four", 256, 256), l3[...])
    row = lax.broadcasted_iota(jnp.int32, (256, 256), 0) % 2
    lane = lax.broadcasted_iota(jnp.int32, (256, 256), 1) % 4 // 2
    sums = jnp.where(row == lane, sums, 0.0)
    head = sums.astype(BF)
    tail = (sums - head.astype(F32)).astype(BF)
    block = jnp.zeros((128, 128), F32)
    for odd in range(2):
        g = table("gather_four", 256, 128, odd * 256)
        block = block + mm(head[odd * 128 : odd * 128 + 128], g) + mm(tail[odd * 128 : odd * 128 + 128], g)
    sa[...] = block.reshape(16, 8, 128).astype(BF)
    pl.semaphore_wait(wide_sem.at[1], 2)
    me = gx * 16 + gy
    mine = pltpu.make_async_copy(sa.at[gy], rb.at[me], recva_sem)
    y_at, x_at, z_at, core_at = gx // 4 * 2 + gy // 8, gx % 4, gy // 2 % 4, gy % 2
    columns, layers = {}, {}
    for d in range(4):
        y = (y_at + d) % 4
        for e in range(4):
            columns[e, d] = y // 2 * 4 + (x_at + e) % 4
            layers[d, e] = y % 2 * 8 + (z_at + e) % 4 * 2
    hops = (0, 1, 2, 1)
    steps = [(dx, dy, dz) for dx in range(4) for dy in range(4) for dz in range(4)]
    steps.sort(key=lambda step: -sum(hops[d] for d in step))
    for dx, dy, dz in steps:
        for flip in range(2):
            if dx or dy or dz or flip:
                layer = layers[dy, dz] + (core_at + flip) % 2
                remote(sa.at[layer], rb.at[me], senda_sem, recva_sem, columns[dx, dy], layer).start()
    mine.start()
    for x in range(4):
        out3[:, x] = l3[:, x * 64 : x * 64 + 64].astype(F32).reshape(64, 4, 64).astype(BF)
    turn[...] = table("turn_four", 384, 128)
    pltpu.make_async_copy(rb, rb, recva_sem).wait()
    pltpu.make_async_copy(rb.at[0:127], rb.at[0:127], senda_sem).wait()


def last(out2_in, out3_in, rb, w4, turn, b4, out2, out3, out4, pp, l4, sem):
    leaving = [
        pltpu.make_async_copy(out2_in, out2, sem.at[0]),
        pltpu.make_async_copy(out3_in, out3, sem.at[1]),
    ]
    for copy in leaving:
        copy.start()
    for x in range(0, 8, 2):
        v = jnp.concatenate(
            [rb[k * 16 : k * 16 + 16].astype(F32).reshape(128, 128).astype(BF) for k in (x, x + 1)], axis=1
        )
        moved = mm(turn[...], v).astype(BF)
        for k in range(2):
            rows = slice((x + k) * 64, (x + k) * 64 + 64)
            for dy in range(3):
                for half in range(2):
                    start = (dy * 2 + half) * 64
                    pp[dy, rows, half * 128 : half * 128 + 128] = moved[start : start + 64, k * 128 : k * 128 + 128]
    bias = jnp.concatenate([b4[...], b4[...]], axis=1)
    size = 512 // PIECES
    for m in range(PIECES):
        operands = []
        for dx in range(3):
            start = m * size + (dx - 1) * 32
            for dy in range(3):
                if start < 0:
                    v = jnp.concatenate([pp[dy, 480:512, :], pp[dy, 0 : size - 32, :]], axis=0)
                elif start + size > 512:
                    v = jnp.concatenate([pp[dy, start:512, :], pp[dy, 0:32, :]], axis=0)
                else:
                    v = pp[dy, start : start + size, :]
                operands.append(v)
        v = leaky(mm(jnp.concatenate(operands, axis=1), w4[...].reshape(2304, 256)) + bias)
        piece = slice(m * size, m * size + size)
        l4[piece] = v.reshape(size, 2, 128).astype(BF)
        leaving.append(pltpu.make_async_copy(l4.at[piece], out4.at[piece], sem.at[2 + m]))
        leaving[-1].start()
    for copy in leaving:
        copy.wait()


def shards(features, weight_two, bias_two, weight_three, bias_three, weight_four, bias_four):
    vm = pl.BlockSpec(memory_space=pltpu.VMEM)
    hbm = pl.BlockSpec(memory_space=pltpu.HBM)
    table = jnp.asarray(TABLE)
    w3 = weight_three.transpose(0, 2, 1)
    w4 = weight_four.transpose(0, 2, 1).reshape(9, 3, 64, 128)
    dma = pltpu.SemaphoreType.DMA
    held = pl.pallas_call(
        kernel,
        out_shape=(
            jax.ShapeDtypeStruct((32, 8, 8, 128), BF),
            jax.ShapeDtypeStruct((64, 4, 4, 64), BF),
            jax.ShapeDtypeStruct((128, 8, 128), BF),
            jax.ShapeDtypeStruct((9, 4, 64, 256), BF),
            jax.ShapeDtypeStruct((384, 128), BF),
            jax.ShapeDtypeStruct((1, 128), F32),
        ),
        in_specs=[hbm] * 8,
        out_specs=(vm,) * 6,
        scratch_shapes=[
            pltpu.VMEM((10, 32, 8, 128), BF),
            pltpu.VMEM((1024, 1280), BF),
            pltpu.VMEM((2, 8, 32, 128), BF),
            pltpu.VMEM((2, 10, 32, 128), BF),
            pltpu.VMEM((27, 32, 32), BF),
            pltpu.VMEM((27, 32, 64), BF),
            pltpu.VMEM((1, 32), F32),
            pltpu.VMEM((1, 64), F32),
            pltpu.VMEM(TABLE.shape, BF),
            pltpu.VMEM((288, 128), BF),
            pltpu.VMEM((9, 256, 256), BF),
            pltpu.VMEM((3, 256, 1024), BF),
            pltpu.VMEM((4, 256, 256), F32),
            pltpu.VMEM((576, 128), BF),
            pltpu.VMEM((9, 256, 128), BF),
            pltpu.VMEM((3, 256, 640), BF),
            pltpu.VMEM((256, 128), F32),
            pltpu.VMEM((256, 128), F32),
            pltpu.VMEM((256, 128), F32),
            pltpu.VMEM((4, 128, 128), BF),
            pltpu.VMEM((2, 2, 32, 128), BF),
            pltpu.VMEM((2, 4, 32, 128), BF),
            pltpu.VMEM((640, 640), BF),
            pltpu.VMEM((256, 256), F32),
            pltpu.VMEM((256, 256), BF),
            pltpu.VMEM((16, 8, 128), BF),
            dma((8,)), dma((8,)), dma((8,)), dma((8,)), dma((10,)), dma((10,)),
            dma, dma, pltpu.SemaphoreType.REGULAR((2,)),
        ],
        compiler_params=pltpu.CompilerParams(
            collective_id=0, has_side_effects=True, vmem_limit_bytes=40 * 1024 * 1024
        ),
    )(
        *(
            pltpu.with_memory_space_constraint(a, pltpu.HBM)
            for a in (features, weight_two, bias_two[None], w3, bias_three[None], w4, bias_four[None], table)
        )
    )
    level_two, level_three, bottleneck = pl.pallas_call(
        last,
        out_shape=(
            jax.ShapeDtypeStruct((32, 8, 8, 128), BF),
            jax.ShapeDtypeStruct((64, 4, 4, 64), BF),
            jax.ShapeDtypeStruct((512, 2, 128), BF),
        ),
        in_specs=[vm] * 6,
        out_specs=(hbm,) * 3,
        scratch_shapes=[
            pltpu.VMEM((3, 512, 256), BF),
            pltpu.VMEM((512, 2, 128), BF),
            dma((2 + PIECES,)),
        ],
        compiler_params=pltpu.CompilerParams(vmem_limit_bytes=40 * 1024 * 1024),
    )(*held)
    return level_two, level_three, bottleneck.reshape(16, 32, 2, 128).transpose(3, 0, 1, 2)


def solution(mesh):
    return jax.shard_map(
        shards,
        mesh=mesh,
        in_specs=(P(None, "gx", "gy", None), P(), P(), P(), P(), P(), P()),
        out_specs=(P(None, "gx", "gy", None), P(None, "gx", "gy", None), P(None, None, None, "gy")),
        check_vma=False,
    )
```

```python
import functools

import jax
import jax.numpy as jnp
import numpy as np
from jax import lax
from jax.experimental import pallas as pl
from jax.experimental.pallas import tpu as pltpu
from jax.sharding import PartitionSpec as P

BF = jnp.bfloat16
F32 = jnp.float32
MESH = pl.DeviceIdType.MESH
PIECES = 2


def tables():
    parts, at, row = [], {}, 0

    def add(name, matrix):
        nonlocal row
        rows, lanes = matrix.shape
        full = np.zeros((-(-rows // 16) * 16, 256), np.float32)
        full[:rows, :lanes] = matrix
        at[name] = row
        parts.append(full)
        row += full.shape[0]

    spread = np.zeros((8, 128, 256))
    for y in range(8):
        for dy in range(3):
            if 0 <= y + dy - 1 < 8:
                for c in range(32):
                    spread[y, dy * 32 + c, c * 8 + y + dy - 1] = 1
    add("spread_two", spread.reshape(1024, 256))
    order = np.zeros((256, 256))
    for y in range(8):
        for o in range(32):
            order[o * 8 + y, y * 32 + o] = 1
    add("order_two", order)
    edge = np.zeros((256, 64))
    for o in range(32):
        edge[o * 8, o] = 1
        edge[o * 8 + 7, 32 + o] = 1
    add("edge_two", edge)
    pool = np.zeros((2, 2, 128, 128))
    for half in range(2):
        for x in range(2):
            for z in range(128):
                pool[half, x, z, half * 64 + z // 2] = 0.125
    add("pool_two", pool.reshape(512, 128))
    select = np.zeros((64, 128))
    for c in range(32):
        select[c, c * 4] = 1
        select[32 + c, c * 4 + 3] = 1
    add("select_three", select)
    add("unit", np.eye(64))
    spread = np.zeros((4, 128, 128))
    for y in range(4):
        for dy in range(3):
            if 0 <= y + dy - 1 < 4:
                for c in range(32):
                    spread[y, dy * 32 + c, c * 4 + y + dy - 1] = 1
    add("spread_three", spread.reshape(512, 128))
    order = np.zeros((256, 256))
    for y in range(4):
        for o in range(64):
            order[o * 4 + y, y * 64 + o] = 1
    add("order_three", order)
    edge = np.zeros((256, 128))
    for o in range(64):
        edge[o * 4, o] = 1
        edge[o * 4 + 3, 64 + o] = 1
    add("edge_three", edge)
    pick = np.zeros((2, 16, 2, 2, 2, 4, 64))
    for odd in range(2):
        for target in range(16):
            for half in range(2):
                z = (2 * target - 1 + 2 * half + odd) % 32
                for x in range(2):
                    pick[odd, target, half, x, :, 2 * x : 2 * x + 2, 2 * z : 2 * z + 2] = 0.125
    add("pick_four", pick.reshape(256, 256))
    gather = np.zeros((2, 256, 128))
    for odd in range(2):
        for o in range(64):
            gather[odd, o * 4 : o * 4 + 4, odd * 64 + o] = 1
    add("gather_four", gather.reshape(512, 128))
    turn = np.zeros((3, 2, 2, 32, 16, 2, 2, 2))
    for dy in range(3):
        for half in range(2):
            for x in range(2):
                for y in range(32):
                    source = (y + dy - 1) % 32
                    turn[dy, half, x, y, source // 2, half, x, source % 2] = 1
    add("turn_four", turn.reshape(384, 128))
    return np.concatenate(parts).astype(jnp.bfloat16), at


TABLE, AT = tables()


def mm(a, b):
    return jnp.dot(a, b, preferred_element_type=F32)


def mm_t(a, b):
    return lax.dot_general(a, b, (((1,), (1,)), ((), ())), preferred_element_type=F32)


def leaky(t):
    return jnp.maximum(t, 0.1 * t)


def rolled_64(v, back):
    lane = lax.broadcasted_iota(jnp.int32, v.shape, 1) % 64
    if back:
        return jnp.where(lane == 0, pltpu.roll(v, 65, 1), pltpu.roll(v, 1, 1))
    return jnp.where(lane == 63, pltpu.roll(v, 63, 1), pltpu.roll(v, 127, 1))


def kernel(
    feat, w2_in, b2_in, w3_in, b3_in, w4_in, b4_in, tab_in,
    out2, out3, rb, w4, turn, b4,
    fx, fm, hs, hr, w2, w3, b2, b3, tab, wc2, z2, t2, a2, wc3, z3, t3, bias2, bias3,
    pooled, l2, own3, hs3, hr3, d3, a3, l3, sa,
    load_sem, feat_sem, send_sem, recv_sem, send3_sem, recv3_sem, senda_sem, recva_sem, wide_sem,
):
    gx, gy = lax.axis_index("gx"), lax.axis_index("gy")
    xp, xm = lax.rem(gx + 1, 8), lax.rem(gx + 7, 8)
    yp, ym = lax.rem(gy + 1, 16), lax.rem(gy + 15, 16)

    def table(name, rows, lanes, skip=0):
        start = AT[name] + skip
        return tab[start : start + rows, :lanes]

    barrier = pltpu.get_barrier_semaphore()

    def greet(semaphore, dx, dy):
        pl.semaphore_signal(
            semaphore, inc=1, device_id=(lax.rem(gx + dx + 8, 8), lax.rem(gy + dy + 16, 16)), device_id_type=MESH
        )

    around = [(dx, dy) for dx in (-1, 0, 1) for dy in (-1, 0, 1) if dx or dy]
    for dx, dy in around:
        greet(barrier, dx, dy)

    loads = [
        pltpu.make_async_copy(feat.at[:, x], fx.at[x + 1], feat_sem.at[x]) for x in range(8)
    ]
    others = [
        pltpu.make_async_copy(tab_in, tab, load_sem.at[0]),
        pltpu.make_async_copy(w2_in, w2, load_sem.at[1]),
        pltpu.make_async_copy(b2_in, b2, load_sem.at[2]),
        pltpu.make_async_copy(w3_in, w3, load_sem.at[3]),
        pltpu.make_async_copy(b3_in, b3, load_sem.at[4]),
        pltpu.make_async_copy(b4_in, b4, load_sem.at[5]),
        pltpu.make_async_copy(w4_in, w4.at[:, 0:3, :, 0:128], load_sem.at[6]),
        pltpu.make_async_copy(w4_in, w4.at[:, 1:4, :, 128:256], load_sem.at[7]),
    ]
    for x in (0, 7, 1, 2, 3, 4, 5, 6):
        loads[x].start()
    for copy in others:
        copy.start()


    def remote(src, dst, send, recv, x, y):
        return pltpu.make_async_remote_copy(
            src_ref=src, dst_ref=dst, send_sem=send, recv_sem=recv,
            device_id=(x, y), device_id_type=MESH,
        )

    def place(x):
        v = fx[x].astype(F32).reshape(256, 128)
        lanes = slice(x * 128, x * 128 + 128)
        fm[256:512, lanes] = v.astype(BF)

    def shift(x):
        lanes = slice(x * 128, x * 128 + 128)
        v = fm[256:512, lanes].astype(F32)
        fm[0:256, lanes] = pltpu.roll(v, 1, 1).astype(BF)
        fm[512:768, lanes] = pltpu.roll(v, 127, 1).astype(BF)

    row = lax.broadcasted_iota(jnp.int32, (64, 256), 0)
    lane = lax.broadcasted_iota(jnp.int32, (64, 256), 1)
    select = jnp.where(lane == row % 32 * 8 + row // 32 * 7, 1.0, 0.0).astype(BF)
    def cut(side_rows, x):
        for side in range(2):
            hs[side, x] = side_rows[side * 32 : side * 32 + 32]

    for x in (0, 7):
        loads[x].wait()
        place(x + 1)
        cut(mm(select, fm[256:512, x * 128 + 128 : x * 128 + 256]).astype(BF), x)
    pl.semaphore_wait(barrier, 8)
    first = [
        remote(fx.at[8], fx.at[0], send_sem.at[0], recv_sem.at[0], xp, gy),
        remote(fx.at[1], fx.at[9], send_sem.at[1], recv_sem.at[1], xm, gy),
    ]
    second = [
        remote(hs.at[1, 7], hr.at[0, 0], send_sem.at[4], recv_sem.at[4], xp, yp),
        remote(hs.at[1, 0], hr.at[0, 9], send_sem.at[5], recv_sem.at[5], xm, yp),
        remote(hs.at[0, 7], hr.at[1, 0], send_sem.at[6], recv_sem.at[6], xp, ym),
        remote(hs.at[0, 0], hr.at[1, 9], send_sem.at[7], recv_sem.at[7], xm, ym),
        remote(hs.at[1], hr.at[0, 1:9], send_sem.at[2], recv_sem.at[2], gx, yp),
        remote(hs.at[0], hr.at[1, 1:9], send_sem.at[3], recv_sem.at[3], gx, ym),
    ]
    for copy in second[:4] + first:
        copy.start()
    for x in range(1, 7):
        loads[x].wait()
        place(x + 1)
    edges = mm(select, fm[256:512, 256:1024]).astype(BF)
    for x in range(1, 7):
        cut(edges[:, (x - 1) * 128 : x * 128], x)
    for copy in second[4:]:
        copy.start()

    for x in range(1, 9):
        shift(x)
    for copy in others:
        copy.wait()
    gap = jnp.zeros((32, 32), F32)
    for dx in range(3):
        for dz in range(3):
            k = 3 * dx + dz
            wc2[k * 32 : k * 32 + 32, :] = jnp.concatenate(
                [w2[9 * dx + 3 * dy + dz].astype(F32) for dy in range(3)] + [gap], axis=1
            ).astype(BF)
    for y in range(8):
        z2[:, y * 32 : y * 32 + 32, :] = (
            mm(wc2[...], table("spread_two", 128, 256, 128 * y)).astype(BF).reshape(9, 32, 256)
        )
    for dx in range(3):
        for dz in range(3):
            t2[dx, :, dz * 256 : dz * 256 + 256] = mm(
                table("order_two", 256, 256), z2[3 * dx + dz]
            ).astype(BF)
        low = [w2[9 * dx + dz].astype(F32) for dz in range(3)]
        high = [w2[9 * dx + 6 + dz].astype(F32) for dz in range(3)]
        z_edge = jnp.concatenate(
            [
                jnp.concatenate([low[0], gap, low[1], gap, low[2], gap, gap, gap], axis=1),
                jnp.concatenate([gap, high[0], gap, high[1], gap, high[2], gap, gap], axis=1),
            ],
            axis=0,
        ).astype(BF)
        t2[dx, :, 768:1024] = mm(table("edge_two", 256, 64), z_edge).astype(BF)
    row = lax.broadcasted_iota(jnp.int32, (256, 32), 0) // 8
    lane = lax.broadcasted_iota(jnp.int32, (256, 32), 1)
    column = jnp.sum(jnp.where(row == lane, b2[...], 0.0), axis=1, keepdims=True)
    bias2[...] = jnp.broadcast_to(column, (256, 128))

    fm[0:768, 0:128] = jnp.zeros((768, 128), BF)
    fm[0:768, 1152:1280] = jnp.zeros((768, 128), BF)
    fm[960:1024, :] = jnp.zeros((64, 1280), BF)

    def inner(p, carry):
        a2[p] = mm(
            jnp.concatenate([t2[dx, :, 0:768] for dx in range(3)], axis=1),
            jnp.concatenate(
                [fm[0:768, pl.ds(pl.multiple_of((p * 2 + dx) * 128, 128), 256)] for dx in range(3)], axis=0
            ),
        )
        return carry

    lax.fori_loop(0, 4, inner, 0)

    def edge_rows(x):
        v = jnp.concatenate([hr[0, x], hr[1, x]], axis=0).astype(F32)
        lanes = slice(x * 128, x * 128 + 128)
        fm[768:832, lanes] = pltpu.roll(v, 1, 1).astype(BF)
        fm[832:896, lanes] = v.astype(BF)
        fm[896:960, lanes] = pltpu.roll(v, 127, 1).astype(BF)

    third = []

    def send3(src, dst, x, y):
        k = len(third)
        third.append(remote(src, dst, send3_sem.at[k], recv3_sem.at[k], x, y))
        third[-1].start()

    def pool_two(q):
        total = jnp.zeros((256, 128), F32)
        for half in range(2):
            p = ((3, 0), (1, 2))[q][half]
            acc = a2[p] + mm(
                jnp.concatenate([t2[dx, :, 768:1024] for dx in range(3)], axis=1),
                jnp.concatenate(
                    [fm[768:1024, (p * 2 + dx) * 128 : (p * 2 + dx + 2) * 128] for dx in range(3)], axis=0
                ),
            )
            for x in range(2):
                v = leaky(acc[:, x * 128 : x * 128 + 128] + bias2[...]).astype(BF)
                l2[2 * p + x] = v
                total = total + mm(v, table("pool_two", 128, 128, half * 256 + x * 128))
        pooled[...] = total
        mean = (pooled[pl.ds(0, 128, stride=2), :] + pooled[pl.ds(1, 128, stride=2), :]).astype(BF)
        own3[q + 1] = mean
        picked = mm(table("select_three", 64, 128), mean).astype(BF)
        hs3[0, q] = picked[0:32]
        hs3[1, q] = picked[32:64]
        if q == 0:
            for x, slot in ((xm, 3), (xp, 0)):
                send3(hs3.at[1, 0], hr3.at[0, slot], x, yp)
                send3(hs3.at[0, 0], hr3.at[1, slot], x, ym)
                send3(own3.at[1], own3.at[slot], x, gy)
        send3(hs3.at[1, q], hr3.at[0, q + 1], gx, yp)
        send3(hs3.at[0, q], hr3.at[1, q + 1], gx, ym)

    for copy in second[4:]:
        copy.wait()
    for x in range(1, 9):
        edge_rows(x)
    pool_two(1)
    for copy in second[:4]:
        copy.wait()
    for x in (0, 9):
        edge_rows(x)
    for copy in first:
        copy.wait()
    for x in (0, 9):
        place(x)
        shift(x)
    a2[0, :, 0:128] += mm(t2[0, :, 0:768], fm[0:768, 0:128])
    a2[3, :, 128:256] += mm(t2[2, :, 0:768], fm[0:768, 1152:1280])
    pool_two(0)
    for dx, dy in around:
        greet(wide_sem.at[0], 2 * dx, 2 * dy)
    for x in range(8):
        out2[:, x] = l2[x].astype(F32).reshape(32, 8, 128).astype(BF)

    for dx in range(3):
        for dz in range(3):
            k = 3 * dx + dz
            stack = jnp.concatenate(
                [w3[9 * dx + 3 * dy + dz] for dy in range(3)] + [jnp.zeros((32, 64), BF)], axis=0
            )
            wc3[k * 64 : k * 64 + 64, :] = mm_t(table("unit", 64, 64), stack).astype(BF)
    for y in range(4):
        z3[:, y * 64 : y * 64 + 64, :] = (
            mm(wc3[...], table("spread_three", 128, 128, 128 * y)).astype(BF).reshape(9, 64, 128)
        )
    gap = jnp.zeros((64, 32), F32)
    for dx in range(3):
        low, high = [], []
        for dz in range(3):
            k = 3 * dx + dz
            t3[dx, :, dz * 128 : dz * 128 + 128] = mm(table("order_three", 256, 256), z3[k]).astype(BF)
            block = wc3[k * 64 : k * 64 + 64, :].astype(F32)
            low.append(block[:, 0:32])
            high.append(block[:, 64:96])
        z_edge = jnp.concatenate(
            [
                jnp.concatenate([low[0], gap, low[1], gap, low[2], gap, gap, gap], axis=1),
                jnp.concatenate([gap, high[0], gap, high[1], gap, high[2], gap, gap], axis=1),
            ],
            axis=0,
        ).astype(BF)
        t3[dx, :, 384:640] = mm(table("edge_three", 256, 128), z_edge).astype(BF)
    row = lax.broadcasted_iota(jnp.int32, (256, 64), 0) // 4
    lane = lax.broadcasted_iota(jnp.int32, (256, 64), 1)
    column = jnp.sum(jnp.where(row == lane, b3[...], 0.0), axis=1, keepdims=True)
    bias3[...] = jnp.broadcast_to(column, (256, 128))

    w4[:, 3, :, 0:128] = jnp.zeros((9, 64, 128), BF)
    w4[:, 0, :, 128:256] = jnp.zeros((9, 64, 128), BF)

    left = lax.broadcasted_iota(jnp.int32, (128, 128), 1) < 64

    def three(rows, lanes, v):
        for dz, u in enumerate((rolled_64(v, True), v, rolled_64(v, False))):
            start = dz * 128 if rows == 128 else 384 + dz * 64
            d3[start : start + rows, lanes * 128 : lanes * 128 + 128] = u.astype(BF)

    outer, middle = own3[1].astype(F32), own3[2].astype(F32)
    outer_turned, middle_turned = pltpu.roll(outer, 64, 1), pltpu.roll(middle, 64, 1)
    three(128, 0, jnp.where(left, outer_turned, middle_turned))
    three(128, 1, jnp.where(left, middle_turned, outer_turned))
    three(128, 3, middle)
    bias = bias3[...]
    a3[...] = mm(t3[1, :, 0:384], d3[0:384, 0:256]) + jnp.concatenate([bias, bias], axis=1)
    d3[576:640, :] = jnp.zeros((64, 640), BF)
    pl.semaphore_wait(wide_sem.at[0], 8)
    for dy in (-4, 4):
        greet(wide_sem.at[1], 0, dy)
    for copy in third:
        copy.wait()
    three(128, 2, jnp.where(left, own3[0].astype(F32), outer))
    three(128, 4, jnp.where(left, outer, own3[3].astype(F32)))
    edge = [jnp.concatenate([hr3[0, t], hr3[1, t]], axis=0).astype(F32) for t in range(4)]
    turned = [pltpu.roll(edge[t], 64, 1) for t in (1, 2)]
    left = lax.broadcasted_iota(jnp.int32, (64, 128), 1) < 64
    three(64, 0, jnp.where(left, turned[0], turned[1]))
    three(64, 1, jnp.where(left, turned[1], turned[0]))
    three(64, 2, jnp.where(left, edge[0], edge[1]))
    three(64, 3, edge[2])
    three(64, 4, jnp.where(left, edge[1], edge[3]))
    v = leaky(
        a3[...] + mm(t3[0], d3[:, 256:512]) + mm(t3[1, :, 384:640], d3[384:640, 0:256]) + mm(t3[2], d3[:, 384:640])
    )
    l3[...] = v.astype(BF)
    sums = mm_t(table("pick_four", 256, 256), l3[...])
    row = lax.broadcasted_iota(jnp.int32, (256, 256), 0) % 2
    lane = lax.broadcasted_iota(jnp.int32, (256, 256), 1) % 4 // 2
    sums = jnp.where(row == lane, sums, 0.0)
    head = sums.astype(BF)
    tail = (sums - head.astype(F32)).astype(BF)
    block = jnp.zeros((128, 128), F32)
    for odd in range(2):
        g = table("gather_four", 256, 128, odd * 256)
        block = block + mm(head[odd * 128 : odd * 128 + 128], g) + mm(tail[odd * 128 : odd * 128 + 128], g)
    sa[...] = block.reshape(16, 8, 128).astype(BF)
    pl.semaphore_wait(wide_sem.at[1], 2)
    me = gx * 16 + gy
    mine = pltpu.make_async_copy(sa.at[gy], rb.at[me], recva_sem)
    y_at, x_at, z_at, core_at = gx // 4 * 2 + gy // 8, gx % 4, gy // 2 % 4, gy % 2
    columns, layers = {}, {}
    for d in range(4):
        y = (y_at + d) % 4
        for e in range(4):
            columns[e, d] = y // 2 * 4 + (x_at + e) % 4
            layers[d, e] = y % 2 * 8 + (z_at + e) % 4 * 2
    hops = (0, 1, 2, 1)
    steps = [(dx, dy, dz) for dx in range(4) for dy in range(4) for dz in range(4)]
    steps.sort(key=lambda step: -sum(hops[d] for d in step))
    for dx, dy, dz in steps:
        for flip in range(2):
            if dx or dy or dz or flip:
                layer = layers[dy, dz] + (core_at + flip) % 2
                remote(sa.at[layer], rb.at[me], senda_sem, recva_sem, columns[dx, dy], layer).start()
    mine.start()
    for x in range(4):
        out3[:, x] = l3[:, x * 64 : x * 64 + 64].astype(F32).reshape(64, 4, 64).astype(BF)
    turn[...] = table("turn_four", 384, 128)
    pltpu.make_async_copy(rb, rb, recva_sem).wait()
    pltpu.make_async_copy(rb.at[0:127], rb.at[0:127], senda_sem).wait()


def last(out2_in, out3_in, rb, w4, turn, b4, out2, out3, out4, pp, l4, sem):
    leaving = [
        pltpu.make_async_copy(out2_in, out2, sem.at[0]),
        pltpu.make_async_copy(out3_in, out3, sem.at[1]),
    ]
    for copy in leaving:
        copy.start()
    for x in range(0, 8, 2):
        v = jnp.concatenate(
            [rb[k * 16 : k * 16 + 16].astype(F32).reshape(128, 128).astype(BF) for k in (x, x + 1)], axis=1
        )
        moved = mm(turn[...], v).astype(BF)
        for k in range(2):
            rows = slice((x + k) * 64, (x + k) * 64 + 64)
            for dy in range(3):
                for half in range(2):
                    start = (dy * 2 + half) * 64
                    pp[dy, rows, half * 128 : half * 128 + 128] = moved[start : start + 64, k * 128 : k * 128 + 128]
    bias = jnp.concatenate([b4[...], b4[...]], axis=1)
    size = 512 // PIECES
    for m in range(PIECES):
        operands = []
        for dx in range(3):
            start = m * size + (dx - 1) * 32
            for dy in range(3):
                if start < 0:
                    v = jnp.concatenate([pp[dy, 480:512, :], pp[dy, 0 : size - 32, :]], axis=0)
                elif start + size > 512:
                    v = jnp.concatenate([pp[dy, start:512, :], pp[dy, 0:32, :]], axis=0)
                else:
                    v = pp[dy, start : start + size, :]
                operands.append(v)
        v = leaky(mm(jnp.concatenate(operands, axis=1), w4[...].reshape(2304, 256)) + bias)
        piece = slice(m * size, m * size + size)
        l4[piece] = v.reshape(size, 2, 128).astype(BF)
        leaving.append(pltpu.make_async_copy(l4.at[piece], out4.at[piece], sem.at[2 + m]))
        leaving[-1].start()
    for copy in leaving:
        copy.wait()


def shards(features, weight_two, bias_two, weight_three, bias_three, weight_four, bias_four):
    vm = pl.BlockSpec(memory_space=pltpu.VMEM)
    hbm = pl.BlockSpec(memory_space=pltpu.HBM)
    table = jnp.asarray(TABLE)
    w3 = weight_three.transpose(0, 2, 1)
    w4 = weight_four.transpose(0, 2, 1).reshape(9, 3, 64, 128)
    dma = pltpu.SemaphoreType.DMA
    held = pl.pallas_call(
        kernel,
        out_shape=(
            jax.ShapeDtypeStruct((32, 8, 8, 128), BF),
            jax.ShapeDtypeStruct((64, 4, 4, 64), BF),
            jax.ShapeDtypeStruct((128, 8, 128), BF),
            jax.ShapeDtypeStruct((9, 4, 64, 256), BF),
            jax.ShapeDtypeStruct((384, 128), BF),
            jax.ShapeDtypeStruct((1, 128), F32),
        ),
        in_specs=[hbm] * 8,
        out_specs=(vm,) * 6,
        scratch_shapes=[
            pltpu.VMEM((10, 32, 8, 128), BF),
            pltpu.VMEM((1024, 1280), BF),
            pltpu.VMEM((2, 8, 32, 128), BF),
            pltpu.VMEM((2, 10, 32, 128), BF),
            pltpu.VMEM((27, 32, 32), BF),
            pltpu.VMEM((27, 32, 64), BF),
            pltpu.VMEM((1, 32), F32),
            pltpu.VMEM((1, 64), F32),
            pltpu.VMEM(TABLE.shape, BF),
            pltpu.VMEM((288, 128), BF),
            pltpu.VMEM((9, 256, 256), BF),
            pltpu.VMEM((3, 256, 1024), BF),
            pltpu.VMEM((4, 256, 256), F32),
            pltpu.VMEM((576, 128), BF),
            pltpu.VMEM((9, 256, 128), BF),
            pltpu.VMEM((3, 256, 640), BF),
            pltpu.VMEM((256, 128), F32),
            pltpu.VMEM((256, 128), F32),
            pltpu.VMEM((256, 128), F32),
            pltpu.VMEM((8, 256, 128), BF),
            pltpu.VMEM((4, 128, 128), BF),
            pltpu.VMEM((2, 2, 32, 128), BF),
            pltpu.VMEM((2, 4, 32, 128), BF),
            pltpu.VMEM((640, 640), BF),
            pltpu.VMEM((256, 256), F32),
            pltpu.VMEM((256, 256), BF),
            pltpu.VMEM((16, 8, 128), BF),
            dma((8,)), dma((8,)), dma((8,)), dma((8,)), dma((10,)), dma((10,)),
            dma, dma, pltpu.SemaphoreType.REGULAR((2,)),
        ],
        compiler_params=pltpu.CompilerParams(
            collective_id=0, has_side_effects=True, vmem_limit_bytes=40 * 1024 * 1024
        ),
    )(
        *(
            pltpu.with_memory_space_constraint(a, pltpu.HBM)
            for a in (features, weight_two, bias_two[None], w3, bias_three[None], w4, bias_four[None], table)
        )
    )
    level_two, level_three, bottleneck = pl.pallas_call(
        last,
        out_shape=(
            jax.ShapeDtypeStruct((32, 8, 8, 128), BF),
            jax.ShapeDtypeStruct((64, 4, 4, 64), BF),
            jax.ShapeDtypeStruct((512, 2, 128), BF),
        ),
        in_specs=[vm] * 6,
        out_specs=(hbm,) * 3,
        scratch_shapes=[
            pltpu.VMEM((3, 512, 256), BF),
            pltpu.VMEM((512, 2, 128), BF),
            dma((2 + PIECES,)),
        ],
        compiler_params=pltpu.CompilerParams(vmem_limit_bytes=40 * 1024 * 1024),
    )(*held)
    return level_two, level_three, bottleneck.reshape(16, 32, 2, 128).transpose(3, 0, 1, 2)


def solution(mesh):
    return jax.shard_map(
        shards,
        mesh=mesh,
        in_specs=(P(None, "gx", "gy", None), P(), P(), P(), P(), P(), P()),
        out_specs=(P(None, "gx", "gy", None), P(None, "gx", "gy", None), P(None, None, None, "gy")),
        check_vma=False,
    )
```

```python
import functools

import jax
import jax.numpy as jnp
import numpy as np
from jax import lax
from jax.experimental import pallas as pl
from jax.experimental.pallas import tpu as pltpu
from jax.sharding import PartitionSpec as P

BF = jnp.bfloat16
F32 = jnp.float32
MESH = pl.DeviceIdType.MESH
PIECES = 2


def tables():
    parts, at, row = [], {}, 0

    def add(name, matrix):
        nonlocal row
        rows, lanes = matrix.shape
        full = np.zeros((-(-rows // 16) * 16, 256), np.float32)
        full[:rows, :lanes] = matrix
        at[name] = row
        parts.append(full)
        row += full.shape[0]

    spread = np.zeros((8, 128, 256))
    for y in range(8):
        for dy in range(3):
            if 0 <= y + dy - 1 < 8:
                for c in range(32):
                    spread[y, dy * 32 + c, c * 8 + y + dy - 1] = 1
    add("spread_two", spread.reshape(1024, 256))
    order = np.zeros((256, 256))
    for y in range(8):
        for o in range(32):
            order[o * 8 + y, y * 32 + o] = 1
    add("order_two", order)
    edge = np.zeros((256, 64))
    for o in range(32):
        edge[o * 8, o] = 1
        edge[o * 8 + 7, 32 + o] = 1
    add("edge_two", edge)
    pool = np.zeros((2, 2, 128, 128))
    for half in range(2):
        for x in range(2):
            for z in range(128):
                pool[half, x, z, half * 64 + z // 2] = 0.125
    add("pool_two", pool.reshape(512, 128))
    select = np.zeros((64, 128))
    for c in range(32):
        select[c, c * 4] = 1
        select[32 + c, c * 4 + 3] = 1
    add("select_three", select)
    add("unit", np.eye(64))
    spread = np.zeros((4, 128, 128))
    for y in range(4):
        for dy in range(3):
            if 0 <= y + dy - 1 < 4:
                for c in range(32):
                    spread[y, dy * 32 + c, c * 4 + y + dy - 1] = 1
    add("spread_three", spread.reshape(512, 128))
    order = np.zeros((256, 256))
    for y in range(4):
        for o in range(64):
            order[o * 4 + y, y * 64 + o] = 1
    add("order_three", order)
    edge = np.zeros((256, 128))
    for o in range(64):
        edge[o * 4, o] = 1
        edge[o * 4 + 3, 64 + o] = 1
    add("edge_three", edge)
    pick = np.zeros((2, 16, 2, 2, 2, 4, 64))
    for odd in range(2):
        for target in range(16):
            for half in range(2):
                z = (2 * target - 1 + 2 * half + odd) % 32
                for x in range(2):
                    pick[odd, target, half, x, :, 2 * x : 2 * x + 2, 2 * z : 2 * z + 2] = 0.125
    add("pick_four", pick.reshape(256, 256))
    gather = np.zeros((2, 256, 128))
    for odd in range(2):
        for o in range(64):
            gather[odd, o * 4 : o * 4 + 4, odd * 64 + o] = 1
    add("gather_four", gather.reshape(512, 128))
    turn = np.zeros((3, 2, 2, 32, 16, 2, 2, 2))
    for dy in range(3):
        for half in range(2):
            for x in range(2):
                for y in range(32):
                    source = (y + dy - 1) % 32
                    turn[dy, half, x, y, source // 2, half, x, source % 2] = 1
    add("turn_four", turn.reshape(384, 128))
    return np.concatenate(parts).astype(jnp.bfloat16), at


TABLE, AT = tables()


def mm(a, b):
    return jnp.dot(a, b, preferred_element_type=F32)


def mm_t(a, b):
    return lax.dot_general(a, b, (((1,), (1,)), ((), ())), preferred_element_type=F32)


def leaky(t):
    return jnp.maximum(t, 0.1 * t)


def rolled_64(v, back):
    lane = lax.broadcasted_iota(jnp.int32, v.shape, 1) % 64
    if back:
        return jnp.where(lane == 0, pltpu.roll(v, 65, 1), pltpu.roll(v, 1, 1))
    return jnp.where(lane == 63, pltpu.roll(v, 63, 1), pltpu.roll(v, 127, 1))


def kernel(
    feat, w2_in, b2_in, w3_in, b3_in, w4_in, b4_in, tab_in,
    out2, out3, rb, w4, turn, b4,
    fx, fm, hs, hr, w2, w3, b2, b3, tab, wc2, z2, t2, a2, wc3, z3, t3, bias2, bias3,
    pooled, l2, own3, hs3, hr3, d3, a3, l3, sa,
    load_sem, feat_sem, send_sem, recv_sem, send3_sem, recv3_sem, senda_sem, recva_sem, wide_sem,
):
    gx, gy = lax.axis_index("gx"), lax.axis_index("gy")
    xp, xm = lax.rem(gx + 1, 8), lax.rem(gx + 7, 8)
    yp, ym = lax.rem(gy + 1, 16), lax.rem(gy + 15, 16)

    def table(name, rows, lanes, skip=0):
        start = AT[name] + skip
        return tab[start : start + rows, :lanes]

    barrier = pltpu.get_barrier_semaphore()

    def greet(semaphore, dx, dy):
        pl.semaphore_signal(
            semaphore, inc=1, device_id=(lax.rem(gx + dx + 8, 8), lax.rem(gy + dy + 16, 16)), device_id_type=MESH
        )

    around = [(dx, dy) for dx in (-1, 0, 1) for dy in (-1, 0, 1) if dx or dy]
    for dx, dy in around:
        greet(barrier, dx, dy)

    loads = [
        pltpu.make_async_copy(feat.at[:, x], fx.at[x + 1], feat_sem.at[x]) for x in range(8)
    ]
    others = [
        pltpu.make_async_copy(tab_in, tab, load_sem.at[0]),
        pltpu.make_async_copy(w2_in, w2, load_sem.at[1]),
        pltpu.make_async_copy(b2_in, b2, load_sem.at[2]),
        pltpu.make_async_copy(w3_in, w3, load_sem.at[3]),
        pltpu.make_async_copy(b3_in, b3, load_sem.at[4]),
        pltpu.make_async_copy(b4_in, b4, load_sem.at[5]),
        pltpu.make_async_copy(w4_in, w4.at[:, 0:3, :, 0:128], load_sem.at[6]),
        pltpu.make_async_copy(w4_in, w4.at[:, 1:4, :, 128:256], load_sem.at[7]),
    ]
    for x in (0, 7, 1, 2, 3, 4, 5, 6):
        loads[x].start()
    for copy in others:
        copy.start()


    def remote(src, dst, send, recv, x, y):
        return pltpu.make_async_remote_copy(
            src_ref=src, dst_ref=dst, send_sem=send, recv_sem=recv,
            device_id=(x, y), device_id_type=MESH,
        )

    def place(x):
        v = fx[x].astype(F32).reshape(256, 128)
        lanes = slice(x * 128, x * 128 + 128)
        fm[256:512, lanes] = v.astype(BF)

    def shift(x):
        lanes = slice(x * 128, x * 128 + 128)
        v = fm[256:512, lanes].astype(F32)
        fm[0:256, lanes] = pltpu.roll(v, 1, 1).astype(BF)
        fm[512:768, lanes] = pltpu.roll(v, 127, 1).astype(BF)

    row = lax.broadcasted_iota(jnp.int32, (64, 256), 0)
    lane = lax.broadcasted_iota(jnp.int32, (64, 256), 1)
    select = jnp.where(lane == row % 32 * 8 + row // 32 * 7, 1.0, 0.0).astype(BF)
    def cut(side_rows, x):
        for side in range(2):
            hs[side, x] = side_rows[side * 32 : side * 32 + 32]

    for x in (0, 7):
        loads[x].wait()
        place(x + 1)
        cut(mm(select, fm[256:512, x * 128 + 128 : x * 128 + 256]).astype(BF), x)
    pl.semaphore_wait(barrier, 8)
    first = [
        remote(fx.at[8], fx.at[0], send_sem.at[0], recv_sem.at[0], xp, gy),
        remote(fx.at[1], fx.at[9], send_sem.at[1], recv_sem.at[1], xm, gy),
    ]
    second = [
        remote(hs.at[1, 7], hr.at[0, 0], send_sem.at[4], recv_sem.at[4], xp, yp),
        remote(hs.at[1, 0], hr.at[0, 9], send_sem.at[5], recv_sem.at[5], xm, yp),
        remote(hs.at[0, 7], hr.at[1, 0], send_sem.at[6], recv_sem.at[6], xp, ym),
        remote(hs.at[0, 0], hr.at[1, 9], send_sem.at[7], recv_sem.at[7], xm, ym),
        remote(hs.at[1], hr.at[0, 1:9], send_sem.at[2], recv_sem.at[2], gx, yp),
        remote(hs.at[0], hr.at[1, 1:9], send_sem.at[3], recv_sem.at[3], gx, ym),
    ]
    for copy in second[:4] + first:
        copy.start()
    for x in range(1, 7):
        loads[x].wait()
        place(x + 1)
    edges = mm(select, fm[256:512, 256:1024]).astype(BF)
    for x in range(1, 7):
        cut(edges[:, (x - 1) * 128 : x * 128], x)
    for copy in second[4:]:
        copy.start()

    for x in range(1, 9):
        shift(x)
    for copy in others:
        copy.wait()
    gap = jnp.zeros((32, 32), F32)
    for dx in range(3):
        for dz in range(3):
            k = 3 * dx + dz
            wc2[k * 32 : k * 32 + 32, :] = jnp.concatenate(
                [w2[9 * dx + 3 * dy + dz].astype(F32) for dy in range(3)] + [gap], axis=1
            ).astype(BF)
    for y in range(8):
        z2[:, y * 32 : y * 32 + 32, :] = (
            mm(wc2[...], table("spread_two", 128, 256, 128 * y)).astype(BF).reshape(9, 32, 256)
        )
    for dx in range(3):
        for dz in range(3):
            t2[dx, :, dz * 256 : dz * 256 + 256] = mm(
                table("order_two", 256, 256), z2[3 * dx + dz]
            ).astype(BF)
        low = [w2[9 * dx + dz].astype(F32) for dz in range(3)]
        high = [w2[9 * dx + 6 + dz].astype(F32) for dz in range(3)]
        z_edge = jnp.concatenate(
            [
                jnp.concatenate([low[0], gap, low[1], gap, low[2], gap, gap, gap], axis=1),
                jnp.concatenate([gap, high[0], gap, high[1], gap, high[2], gap, gap], axis=1),
            ],
            axis=0,
        ).astype(BF)
        t2[dx, :, 768:1024] = mm(table("edge_two", 256, 64), z_edge).astype(BF)
    row = lax.broadcasted_iota(jnp.int32, (256, 32), 0) // 8
    lane = lax.broadcasted_iota(jnp.int32, (256, 32), 1)
    column = jnp.sum(jnp.where(row == lane, b2[...], 0.0), axis=1, keepdims=True)
    bias2[...] = jnp.broadcast_to(column, (256, 128))

    fm[0:768, 0:128] = jnp.zeros((768, 128), BF)
    fm[0:768, 1152:1280] = jnp.zeros((768, 128), BF)
    fm[960:1024, :] = jnp.zeros((64, 1280), BF)

    def inner(p, carry):
        a2[p] = mm(
            jnp.concatenate([t2[dx, :, 0:768] for dx in range(3)], axis=1),
            jnp.concatenate(
                [fm[0:768, pl.ds(pl.multiple_of((p * 2 + dx) * 128, 128), 256)] for dx in range(3)], axis=0
            ),
        )
        return carry

    lax.fori_loop(0, 4, inner, 0)

    def edge_rows(x):
        v = jnp.concatenate([hr[0, x], hr[1, x]], axis=0).astype(F32)
        lanes = slice(x * 128, x * 128 + 128)
        fm[768:832, lanes] = pltpu.roll(v, 1, 1).astype(BF)
        fm[832:896, lanes] = v.astype(BF)
        fm[896:960, lanes] = pltpu.roll(v, 127, 1).astype(BF)

    third = []

    def send3(src, dst, x, y):
        k = len(third)
        third.append(remote(src, dst, send3_sem.at[k], recv3_sem.at[k], x, y))
        third[-1].start()

    def pool_two(q):
        total = jnp.zeros((256, 128), F32)
        for half in range(2):
            p = ((3, 0), (1, 2))[q][half]
            acc = a2[p] + mm(
                jnp.concatenate([t2[dx, :, 768:1024] for dx in range(3)], axis=1),
                jnp.concatenate(
                    [fm[768:1024, (p * 2 + dx) * 128 : (p * 2 + dx + 2) * 128] for dx in range(3)], axis=0
                ),
            )
            for x in range(2):
                v = leaky(acc[:, x * 128 : x * 128 + 128] + bias2[...]).astype(BF)
                l2[2 * p + x] = v
                total = total + mm(v, table("pool_two", 128, 128, half * 256 + x * 128))
        pooled[...] = total
        mean = (pooled[pl.ds(0, 128, stride=2), :] + pooled[pl.ds(1, 128, stride=2), :]).astype(BF)
        own3[q + 1] = mean
        picked = mm(table("select_three", 64, 128), mean).astype(BF)
        hs3[0, q] = picked[0:32]
        hs3[1, q] = picked[32:64]
        if q == 0:
            for x, slot in ((xm, 3), (xp, 0)):
                send3(hs3.at[1, 0], hr3.at[0, slot], x, yp)
                send3(hs3.at[0, 0], hr3.at[1, slot], x, ym)
                send3(own3.at[1], own3.at[slot], x, gy)
        send3(hs3.at[1, q], hr3.at[0, q + 1], gx, yp)
        send3(hs3.at[0, q], hr3.at[1, q + 1], gx, ym)

    for copy in second[4:]:
        copy.wait()
    for x in range(1, 9):
        edge_rows(x)
    for copy in second[:4]:
        copy.wait()
    for x in (0, 9):
        edge_rows(x)
    for copy in first:
        copy.wait()
    for x in (0, 9):
        place(x)
        shift(x)
    a2[0, :, 0:128] += mm(t2[0, :, 0:768], fm[0:768, 0:128])
    a2[3, :, 128:256] += mm(t2[2, :, 0:768], fm[0:768, 1152:1280])
    pool_two(0)
    for dx, dy in around:
        greet(wide_sem.at[0], 2 * dx, 2 * dy)
    pool_two(1)
    for x in range(8):
        out2[:, x] = l2[x].astype(F32).reshape(32, 8, 128).astype(BF)

    for dx in range(3):
        for dz in range(3):
            k = 3 * dx + dz
            stack = jnp.concatenate(
                [w3[9 * dx + 3 * dy + dz] for dy in range(3)] + [jnp.zeros((32, 64), BF)], axis=0
            )
            wc3[k * 64 : k * 64 + 64, :] = mm_t(table("unit", 64, 64), stack).astype(BF)
    for y in range(4):
        z3[:, y * 64 : y * 64 + 64, :] = (
            mm(wc3[...], table("spread_three", 128, 128, 128 * y)).astype(BF).reshape(9, 64, 128)
        )
    gap = jnp.zeros((64, 32), F32)
    for dx in range(3):
        low, high = [], []
        for dz in range(3):
            k = 3 * dx + dz
            t3[dx, :, dz * 128 : dz * 128 + 128] = mm(table("order_three", 256, 256), z3[k]).astype(BF)
            block = wc3[k * 64 : k * 64 + 64, :].astype(F32)
            low.append(block[:, 0:32])
            high.append(block[:, 64:96])
        z_edge = jnp.concatenate(
            [
                jnp.concatenate([low[0], gap, low[1], gap, low[2], gap, gap, gap], axis=1),
                jnp.concatenate([gap, high[0], gap, high[1], gap, high[2], gap, gap], axis=1),
            ],
            axis=0,
        ).astype(BF)
        t3[dx, :, 384:640] = mm(table("edge_three", 256, 128), z_edge).astype(BF)
    row = lax.broadcasted_iota(jnp.int32, (256, 64), 0) // 4
    lane = lax.broadcasted_iota(jnp.int32, (256, 64), 1)
    column = jnp.sum(jnp.where(row == lane, b3[...], 0.0), axis=1, keepdims=True)
    bias3[...] = jnp.broadcast_to(column, (256, 128))

    w4[:, 3, :, 0:128] = jnp.zeros((9, 64, 128), BF)
    w4[:, 0, :, 128:256] = jnp.zeros((9, 64, 128), BF)

    left = lax.broadcasted_iota(jnp.int32, (128, 128), 1) < 64

    def three(rows, lanes, v):
        for dz, u in enumerate((rolled_64(v, True), v, rolled_64(v, False))):
            start = dz * 128 if rows == 128 else 384 + dz * 64
            d3[start : start + rows, lanes * 128 : lanes * 128 + 128] = u.astype(BF)

    outer, middle = own3[1].astype(F32), own3[2].astype(F32)
    outer_turned, middle_turned = pltpu.roll(outer, 64, 1), pltpu.roll(middle, 64, 1)
    three(128, 0, jnp.where(left, outer_turned, middle_turned))
    three(128, 1, jnp.where(left, middle_turned, outer_turned))
    three(128, 3, middle)
    bias = bias3[...]
    a3[...] = mm(t3[1, :, 0:384], d3[0:384, 0:256]) + jnp.concatenate([bias, bias], axis=1)
    d3[576:640, :] = jnp.zeros((64, 640), BF)
    pl.semaphore_wait(wide_sem.at[0], 8)
    for dy in (-4, 4):
        greet(wide_sem.at[1], 0, dy)
    for copy in third:
        copy.wait()
    three(128, 2, jnp.where(left, own3[0].astype(F32), outer))
    three(128, 4, jnp.where(left, outer, own3[3].astype(F32)))
    edge = [jnp.concatenate([hr3[0, t], hr3[1, t]], axis=0).astype(F32) for t in range(4)]
    turned = [pltpu.roll(edge[t], 64, 1) for t in (1, 2)]
    left = lax.broadcasted_iota(jnp.int32, (64, 128), 1) < 64
    three(64, 0, jnp.where(left, turned[0], turned[1]))
    three(64, 1, jnp.where(left, turned[1], turned[0]))
    three(64, 2, jnp.where(left, edge[0], edge[1]))
    three(64, 3, edge[2])
    three(64, 4, jnp.where(left, edge[1], edge[3]))
    v = leaky(
        a3[...] + mm(t3[0], d3[:, 256:512]) + mm(t3[1, :, 384:640], d3[384:640, 0:256]) + mm(t3[2], d3[:, 384:640])
    )
    l3[...] = v.astype(BF)
    sums = mm_t(table("pick_four", 256, 256), l3[...])
    row = lax.broadcasted_iota(jnp.int32, (256, 256), 0) % 2
    lane = lax.broadcasted_iota(jnp.int32, (256, 256), 1) % 4 // 2
    sums = jnp.where(row == lane, sums, 0.0)
    head = sums.astype(BF)
    tail = (sums - head.astype(F32)).astype(BF)
    block = jnp.zeros((128, 128), F32)
    for odd in range(2):
        g = table("gather_four", 256, 128, odd * 256)
        block = block + mm(head[odd * 128 : odd * 128 + 128], g) + mm(tail[odd * 128 : odd * 128 + 128], g)
    sa[...] = block.reshape(16, 8, 128).astype(BF)
    pl.semaphore_wait(wide_sem.at[1], 2)
    me = gx * 16 + gy
    mine = pltpu.make_async_copy(sa.at[gy], rb.at[me], recva_sem)
    y_at, x_at, z_at, core_at = gx // 4 * 2 + gy // 8, gx % 4, gy // 2 % 4, gy % 2
    columns, layers = {}, {}
    for d in range(4):
        y = (y_at + d) % 4
        for e in range(4):
            columns[e, d] = y // 2 * 4 + (x_at + e) % 4
            layers[d, e] = y % 2 * 8 + (z_at + e) % 4 * 2
    hops = (0, 1, 2, 1)
    steps = [(dx, dy, dz) for dx in range(4) for dy in range(4) for dz in range(4)]
    steps.sort(key=lambda step: -sum(hops[d] for d in step))
    for dx, dy, dz in steps:
        for flip in range(2):
            if dx or dy or dz or flip:
                layer = layers[dy, dz] + (core_at + flip) % 2
                remote(sa.at[layer], rb.at[me], senda_sem, recva_sem, columns[dx, dy], layer).start()
    mine.start()
    for x in range(4):
        out3[:, x] = l3[:, x * 64 : x * 64 + 64].astype(F32).reshape(64, 4, 64).astype(BF)
    turn[...] = table("turn_four", 384, 128)
    pltpu.make_async_copy(rb, rb, recva_sem).wait()
    pltpu.make_async_copy(rb.at[0:127], rb.at[0:127], senda_sem).wait()


def last(out2_in, out3_in, rb, w4, turn, b4, out2, out3, out4, pp, l4, sem):
    leaving = [
        pltpu.make_async_copy(out2_in, out2, sem.at[0]),
        pltpu.make_async_copy(out3_in, out3, sem.at[1]),
    ]
    for copy in leaving:
        copy.start()
    for x in range(0, 8, 2):
        v = jnp.concatenate(
            [rb[k * 16 : k * 16 + 16].astype(F32).reshape(128, 128).astype(BF) for k in (x, x + 1)], axis=1
        )
        moved = mm(turn[...], v).astype(BF)
        for k in range(2):
            rows = slice((x + k) * 64, (x + k) * 64 + 64)
            for dy in range(3):
                for half in range(2):
                    start = (dy * 2 + half) * 64
                    pp[dy, rows, half * 128 : half * 128 + 128] = moved[start : start + 64, k * 128 : k * 128 + 128]
    bias = jnp.concatenate([b4[...], b4[...]], axis=1)
    size = 512 // PIECES
    for m in range(PIECES):
        operands = []
        for dx in range(3):
            start = m * size + (dx - 1) * 32
            for dy in range(3):
                if start < 0:
                    v = jnp.concatenate([pp[dy, 480:512, :], pp[dy, 0 : size - 32, :]], axis=0)
                elif start + size > 512:
                    v = jnp.concatenate([pp[dy, start:512, :], pp[dy, 0:32, :]], axis=0)
                else:
                    v = pp[dy, start : start + size, :]
                operands.append(v)
        v = leaky(mm(jnp.concatenate(operands, axis=1), w4[...].reshape(2304, 256)) + bias)
        piece = slice(m * size, m * size + size)
        l4[piece] = v.reshape(size, 2, 128).astype(BF)
        leaving.append(pltpu.make_async_copy(l4.at[piece], out4.at[piece], sem.at[2 + m]))
        leaving[-1].start()
    for copy in leaving:
        copy.wait()


def shards(features, weight_two, bias_two, weight_three, bias_three, weight_four, bias_four):
    vm = pl.BlockSpec(memory_space=pltpu.VMEM)
    hbm = pl.BlockSpec(memory_space=pltpu.HBM)
    table = jnp.asarray(TABLE)
    w3 = weight_three.transpose(0, 2, 1)
    w4 = weight_four.transpose(0, 2, 1).reshape(9, 3, 64, 128)
    dma = pltpu.SemaphoreType.DMA
    held = pl.pallas_call(
        kernel,
        out_shape=(
            jax.ShapeDtypeStruct((32, 8, 8, 128), BF),
            jax.ShapeDtypeStruct((64, 4, 4, 64), BF),
            jax.ShapeDtypeStruct((128, 8, 128), BF),
            jax.ShapeDtypeStruct((9, 4, 64, 256), BF),
            jax.ShapeDtypeStruct((384, 128), BF),
            jax.ShapeDtypeStruct((1, 128), F32),
        ),
        in_specs=[hbm] * 8,
        out_specs=(vm,) * 6,
        scratch_shapes=[
            pltpu.VMEM((10, 32, 8, 128), BF),
            pltpu.VMEM((1024, 1280), BF),
            pltpu.VMEM((2, 8, 32, 128), BF),
            pltpu.VMEM((2, 10, 32, 128), BF),
            pltpu.VMEM((27, 32, 32), BF),
            pltpu.VMEM((27, 32, 64), BF),
            pltpu.VMEM((1, 32), F32),
            pltpu.VMEM((1, 64), F32),
            pltpu.VMEM(TABLE.shape, BF),
            pltpu.VMEM((288, 128), BF),
            pltpu.VMEM((9, 256, 256), BF),
            pltpu.VMEM((3, 256, 1024), BF),
            pltpu.VMEM((4, 256, 256), F32),
            pltpu.VMEM((576, 128), BF),
            pltpu.VMEM((9, 256, 128), BF),
            pltpu.VMEM((3, 256, 640), BF),
            pltpu.VMEM((256, 128), F32),
            pltpu.VMEM((256, 128), F32),
            pltpu.VMEM((256, 128), F32),
            pltpu.VMEM((8, 256, 128), BF),
            pltpu.VMEM((4, 128, 128), BF),
            pltpu.VMEM((2, 2, 32, 128), BF),
            pltpu.VMEM((2, 4, 32, 128), BF),
            pltpu.VMEM((640, 640), BF),
            pltpu.VMEM((256, 256), F32),
            pltpu.VMEM((256, 256), BF),
            pltpu.VMEM((16, 8, 128), BF),
            dma((8,)), dma((8,)), dma((8,)), dma((8,)), dma((10,)), dma((10,)),
            dma, dma, pltpu.SemaphoreType.REGULAR((2,)),
        ],
        compiler_params=pltpu.CompilerParams(
            collective_id=0, has_side_effects=True, vmem_limit_bytes=40 * 1024 * 1024
        ),
    )(
        *(
            pltpu.with_memory_space_constraint(a, pltpu.HBM)
            for a in (features, weight_two, bias_two[None], w3, bias_three[None], w4, bias_four[None], table)
        )
    )
    level_two, level_three, bottleneck = pl.pallas_call(
        last,
        out_shape=(
            jax.ShapeDtypeStruct((32, 8, 8, 128), BF),
            jax.ShapeDtypeStruct((64, 4, 4, 64), BF),
            jax.ShapeDtypeStruct((512, 2, 128), BF),
        ),
        in_specs=[vm] * 6,
        out_specs=(hbm,) * 3,
        scratch_shapes=[
            pltpu.VMEM((3, 512, 256), BF),
            pltpu.VMEM((512, 2, 128), BF),
            dma((2 + PIECES,)),
        ],
        compiler_params=pltpu.CompilerParams(vmem_limit_bytes=40 * 1024 * 1024),
    )(*held)
    return level_two, level_three, bottleneck.reshape(16, 32, 2, 128).transpose(3, 0, 1, 2)


def solution(mesh):
    return jax.shard_map(
        shards,
        mesh=mesh,
        in_specs=(P(None, "gx", "gy", None), P(), P(), P(), P(), P(), P()),
        out_specs=(P(None, "gx", "gy", None), P(None, "gx", "gy", None), P(None, None, None, "gy")),
        check_vma=False,
    )
```

```python
import functools

import jax
import jax.numpy as jnp
import numpy as np
from jax import lax
from jax.experimental import pallas as pl
from jax.experimental.pallas import tpu as pltpu
from jax.sharding import PartitionSpec as P

BF = jnp.bfloat16
F32 = jnp.float32
MESH = pl.DeviceIdType.MESH
PIECES = 2


def tables():
    parts, at, row = [], {}, 0

    def add(name, matrix):
        nonlocal row
        rows, lanes = matrix.shape
        full = np.zeros((-(-rows // 16) * 16, 256), np.float32)
        full[:rows, :lanes] = matrix
        at[name] = row
        parts.append(full)
        row += full.shape[0]

    spread = np.zeros((8, 128, 256))
    for y in range(8):
        for dy in range(3):
            if 0 <= y + dy - 1 < 8:
                for c in range(32):
                    spread[y, dy * 32 + c, c * 8 + y + dy - 1] = 1
    add("spread_two", spread.reshape(1024, 256))
    order = np.zeros((256, 256))
    for y in range(8):
        for o in range(32):
            order[o * 8 + y, y * 32 + o] = 1
    add("order_two", order)
    edge = np.zeros((256, 64))
    for o in range(32):
        edge[o * 8, o] = 1
        edge[o * 8 + 7, 32 + o] = 1
    add("edge_two", edge)
    pool = np.zeros((2, 2, 128, 128))
    for half in range(2):
        for x in range(2):
            for z in range(128):
                pool[half, x, z, half * 64 + z // 2] = 0.125
    add("pool_two", pool.reshape(512, 128))
    select = np.zeros((64, 128))
    for c in range(32):
        select[c, c * 4] = 1
        select[32 + c, c * 4 + 3] = 1
    add("select_three", select)
    add("unit", np.eye(64))
    spread = np.zeros((4, 128, 128))
    for y in range(4):
        for dy in range(3):
            if 0 <= y + dy - 1 < 4:
                for c in range(32):
                    spread[y, dy * 32 + c, c * 4 + y + dy - 1] = 1
    add("spread_three", spread.reshape(512, 128))
    order = np.zeros((256, 256))
    for y in range(4):
        for o in range(64):
            order[o * 4 + y, y * 64 + o] = 1
    add("order_three", order)
    edge = np.zeros((256, 128))
    for o in range(64):
        edge[o * 4, o] = 1
        edge[o * 4 + 3, 64 + o] = 1
    add("edge_three", edge)
    pick = np.zeros((2, 16, 2, 2, 2, 4, 64))
    for odd in range(2):
        for target in range(16):
            for half in range(2):
                z = (2 * target - 1 + 2 * half + odd) % 32
                for x in range(2):
                    pick[odd, target, half, x, :, 2 * x : 2 * x + 2, 2 * z : 2 * z + 2] = 0.125
    add("pick_four", pick.reshape(256, 256))
    gather = np.zeros((2, 256, 128))
    for odd in range(2):
        for o in range(64):
            gather[odd, o * 4 : o * 4 + 4, odd * 64 + o] = 1
    add("gather_four", gather.reshape(512, 128))
    turn = np.zeros((3, 2, 2, 32, 16, 2, 2, 2))
    for dy in range(3):
        for half in range(2):
            for x in range(2):
                for y in range(32):
                    source = (y + dy - 1) % 32
                    turn[dy, half, x, y, source // 2, half, x, source % 2] = 1
    add("turn_four", turn.reshape(384, 128))
    return np.concatenate(parts).astype(jnp.bfloat16), at


TABLE, AT = tables()


def mm(a, b):
    return jnp.dot(a, b, preferred_element_type=F32)


def mm_t(a, b):
    return lax.dot_general(a, b, (((1,), (1,)), ((), ())), preferred_element_type=F32)


def leaky(t):
    return jnp.maximum(t, 0.1 * t)


def rolled_64(v, back):
    lane = lax.broadcasted_iota(jnp.int32, v.shape, 1) % 64
    if back:
        return jnp.where(lane == 0, pltpu.roll(v, 65, 1), pltpu.roll(v, 1, 1))
    return jnp.where(lane == 63, pltpu.roll(v, 63, 1), pltpu.roll(v, 127, 1))


def kernel(
    feat, w2_in, b2_in, w3_in, b3_in, w4_in, b4_in, tab_in,
    out2, out3, rb, w4, turn, b4,
    fx, fm, hs, hr, w2, w3, b2, b3, tab, wc2, z2, t2, a2, wc3, z3, t3, bias2, bias3,
    pooled, l2, own3, hs3, hr3, d3, a3, l3, sa,
    load_sem, feat_sem, send_sem, recv_sem, send3_sem, recv3_sem, senda_sem, recva_sem, wide_sem,
):
    gx, gy = lax.axis_index("gx"), lax.axis_index("gy")
    xp, xm = lax.rem(gx + 1, 8), lax.rem(gx + 7, 8)
    yp, ym = lax.rem(gy + 1, 16), lax.rem(gy + 15, 16)

    def table(name, rows, lanes, skip=0):
        start = AT[name] + skip
        return tab[start : start + rows, :lanes]

    barrier = pltpu.get_barrier_semaphore()

    def greet(semaphore, dx, dy):
        pl.semaphore_signal(
            semaphore, inc=1, device_id=(lax.rem(gx + dx + 8, 8), lax.rem(gy + dy + 16, 16)), device_id_type=MESH
        )

    around = [(dx, dy) for dx in (-1, 0, 1) for dy in (-1, 0, 1) if dx or dy]
    for dx, dy in around:
        greet(barrier, dx, dy)

    loads = [
        pltpu.make_async_copy(feat.at[:, x], fx.at[x + 1], feat_sem.at[x]) for x in range(8)
    ]
    others = [
        pltpu.make_async_copy(tab_in, tab, load_sem.at[0]),
        pltpu.make_async_copy(w2_in, w2, load_sem.at[1]),
        pltpu.make_async_copy(b2_in, b2, load_sem.at[2]),
        pltpu.make_async_copy(w3_in, w3, load_sem.at[3]),
        pltpu.make_async_copy(b3_in, b3, load_sem.at[4]),
        pltpu.make_async_copy(b4_in, b4, load_sem.at[5]),
        pltpu.make_async_copy(w4_in, w4.at[:, 0:3, :, 0:128], load_sem.at[6]),
        pltpu.make_async_copy(w4_in, w4.at[:, 1:4, :, 128:256], load_sem.at[7]),
    ]
    for x in (0, 7, 1, 2, 3, 4, 5, 6):
        loads[x].start()
    for copy in others:
        copy.start()


    def remote(src, dst, send, recv, x, y):
        return pltpu.make_async_remote_copy(
            src_ref=src, dst_ref=dst, send_sem=send, recv_sem=recv,
            device_id=(x, y), device_id_type=MESH,
        )

    def place(x):
        v = fx[x].astype(F32).reshape(256, 128)
        lanes = slice(x * 128, x * 128 + 128)
        fm[256:512, lanes] = v.astype(BF)

    def shift(x):
        lanes = slice(x * 128, x * 128 + 128)
        v = fm[256:512, lanes].astype(F32)
        fm[0:256, lanes] = pltpu.roll(v, 1, 1).astype(BF)
        fm[512:768, lanes] = pltpu.roll(v, 127, 1).astype(BF)

    row = lax.broadcasted_iota(jnp.int32, (64, 256), 0)
    lane = lax.broadcasted_iota(jnp.int32, (64, 256), 1)
    select = jnp.where(lane == row % 32 * 8 + row // 32 * 7, 1.0, 0.0).astype(BF)
    def cut(side_rows, x):
        for side in range(2):
            hs[side, x] = side_rows[side * 32 : side * 32 + 32]

    for x in (0, 7):
        loads[x].wait()
        place(x + 1)
        cut(mm(select, fm[256:512, x * 128 + 128 : x * 128 + 256]).astype(BF), x)
    pl.semaphore_wait(barrier, 8)
    first = [
        remote(fx.at[8], fx.at[0], send_sem.at[0], recv_sem.at[0], xp, gy),
        remote(fx.at[1], fx.at[9], send_sem.at[1], recv_sem.at[1], xm, gy),
    ]
    second = [
        remote(hs.at[1, 7], hr.at[0, 0], send_sem.at[4], recv_sem.at[4], xp, yp),
        remote(hs.at[1, 0], hr.at[0, 9], send_sem.at[5], recv_sem.at[5], xm, yp),
        remote(hs.at[0, 7], hr.at[1, 0], send_sem.at[6], recv_sem.at[6], xp, ym),
        remote(hs.at[0, 0], hr.at[1, 9], send_sem.at[7], recv_sem.at[7], xm, ym),
        remote(hs.at[1], hr.at[0, 1:9], send_sem.at[2], recv_sem.at[2], gx, yp),
        remote(hs.at[0], hr.at[1, 1:9], send_sem.at[3], recv_sem.at[3], gx, ym),
    ]
    for copy in second[:4] + first:
        copy.start()
    for x in range(1, 7):
        loads[x].wait()
        place(x + 1)
    edges = mm(select, fm[256:512, 256:1024]).astype(BF)
    for x in range(1, 7):
        cut(edges[:, (x - 1) * 128 : x * 128], x)
    for copy in second[4:]:
        copy.start()
    for dx, dy in around:
        greet(wide_sem.at[2], dx, dy)

    for x in range(1, 9):
        shift(x)
    for copy in others:
        copy.wait()
    gap = jnp.zeros((32, 32), F32)
    for dx in range(3):
        for dz in range(3):
            k = 3 * dx + dz
            wc2[k * 32 : k * 32 + 32, :] = jnp.concatenate(
                [w2[9 * dx + 3 * dy + dz].astype(F32) for dy in range(3)] + [gap], axis=1
            ).astype(BF)
    for y in range(8):
        z2[:, y * 32 : y * 32 + 32, :] = (
            mm(wc2[...], table("spread_two", 128, 256, 128 * y)).astype(BF).reshape(9, 32, 256)
        )
    for dx in range(3):
        for dz in range(3):
            t2[dx, :, dz * 256 : dz * 256 + 256] = mm(
                table("order_two", 256, 256), z2[3 * dx + dz]
            ).astype(BF)
        low = [w2[9 * dx + dz].astype(F32) for dz in range(3)]
        high = [w2[9 * dx + 6 + dz].astype(F32) for dz in range(3)]
        z_edge = jnp.concatenate(
            [
                jnp.concatenate([low[0], gap, low[1], gap, low[2], gap, gap, gap], axis=1),
                jnp.concatenate([gap, high[0], gap, high[1], gap, high[2], gap, gap], axis=1),
            ],
            axis=0,
        ).astype(BF)
        t2[dx, :, 768:1024] = mm(table("edge_two", 256, 64), z_edge).astype(BF)
    row = lax.broadcasted_iota(jnp.int32, (256, 32), 0) // 8
    lane = lax.broadcasted_iota(jnp.int32, (256, 32), 1)
    column = jnp.sum(jnp.where(row == lane, b2[...], 0.0), axis=1, keepdims=True)
    bias2[...] = jnp.broadcast_to(column, (256, 128))

    fm[0:768, 0:128] = jnp.zeros((768, 128), BF)
    fm[0:768, 1152:1280] = jnp.zeros((768, 128), BF)
    fm[960:1024, :] = jnp.zeros((64, 1280), BF)

    def inner(p, carry):
        a2[p] = mm(
            jnp.concatenate([t2[dx, :, 0:768] for dx in range(3)], axis=1),
            jnp.concatenate(
                [fm[0:768, pl.ds(pl.multiple_of((p * 2 + dx) * 128, 128), 256)] for dx in range(3)], axis=0
            ),
        )
        return carry

    lax.fori_loop(0, 4, inner, 0)
    pl.semaphore_wait(wide_sem.at[2], 8)
    for dx, dy in around:
        greet(wide_sem.at[0], 2 * dx, 2 * dy)

    def edge_rows(x):
        v = jnp.concatenate([hr[0, x], hr[1, x]], axis=0).astype(F32)
        lanes = slice(x * 128, x * 128 + 128)
        fm[768:832, lanes] = pltpu.roll(v, 1, 1).astype(BF)
        fm[832:896, lanes] = v.astype(BF)
        fm[896:960, lanes] = pltpu.roll(v, 127, 1).astype(BF)

    third = []

    def send3(src, dst, x, y):
        k = len(third)
        third.append(remote(src, dst, send3_sem.at[k], recv3_sem.at[k], x, y))
        third[-1].start()

    def pool_two(q):
        total = jnp.zeros((256, 128), F32)
        for half in range(2):
            p = ((3, 0), (1, 2))[q][half]
            acc = a2[p] + mm(
                jnp.concatenate([t2[dx, :, 768:1024] for dx in range(3)], axis=1),
                jnp.concatenate(
                    [fm[768:1024, (p * 2 + dx) * 128 : (p * 2 + dx + 2) * 128] for dx in range(3)], axis=0
                ),
            )
            for x in range(2):
                v = leaky(acc[:, x * 128 : x * 128 + 128] + bias2[...]).astype(BF)
                l2[2 * p + x] = v
                total = total + mm(v, table("pool_two", 128, 128, half * 256 + x * 128))
        pooled[...] = total
        mean = (pooled[pl.ds(0, 128, stride=2), :] + pooled[pl.ds(1, 128, stride=2), :]).astype(BF)
        own3[q + 1] = mean
        picked = mm(table("select_three", 64, 128), mean).astype(BF)
        hs3[0, q] = picked[0:32]
        hs3[1, q] = picked[32:64]
        if q == 0:
            for x, slot in ((xm, 3), (xp, 0)):
                send3(hs3.at[1, 0], hr3.at[0, slot], x, yp)
                send3(hs3.at[0, 0], hr3.at[1, slot], x, ym)
                send3(own3.at[1], own3.at[slot], x, gy)
        send3(hs3.at[1, q], hr3.at[0, q + 1], gx, yp)
        send3(hs3.at[0, q], hr3.at[1, q + 1], gx, ym)

    for copy in second[4:]:
        copy.wait()
    for x in range(1, 9):
        edge_rows(x)
    for copy in second[:4]:
        copy.wait()
    for x in (0, 9):
        edge_rows(x)
    for copy in first:
        copy.wait()
    for x in (0, 9):
        place(x)
        shift(x)
    a2[0, :, 0:128] += mm(t2[0, :, 0:768], fm[0:768, 0:128])
    a2[3, :, 128:256] += mm(t2[2, :, 0:768], fm[0:768, 1152:1280])
    pool_two(0)
    pool_two(1)
    for x in range(8):
        out2[:, x] = l2[x].astype(F32).reshape(32, 8, 128).astype(BF)

    for dx in range(3):
        for dz in range(3):
            k = 3 * dx + dz
            stack = jnp.concatenate(
                [w3[9 * dx + 3 * dy + dz] for dy in range(3)] + [jnp.zeros((32, 64), BF)], axis=0
            )
            wc3[k * 64 : k * 64 + 64, :] = mm_t(table("unit", 64, 64), stack).astype(BF)
    for y in range(4):
        z3[:, y * 64 : y * 64 + 64, :] = (
            mm(wc3[...], table("spread_three", 128, 128, 128 * y)).astype(BF).reshape(9, 64, 128)
        )
    gap = jnp.zeros((64, 32), F32)
    for dx in range(3):
        low, high = [], []
        for dz in range(3):
            k = 3 * dx + dz
            t3[dx, :, dz * 128 : dz * 128 + 128] = mm(table("order_three", 256, 256), z3[k]).astype(BF)
            block = wc3[k * 64 : k * 64 + 64, :].astype(F32)
            low.append(block[:, 0:32])
            high.append(block[:, 64:96])
        z_edge = jnp.concatenate(
            [
                jnp.concatenate([low[0], gap, low[1], gap, low[2], gap, gap, gap], axis=1),
                jnp.concatenate([gap, high[0], gap, high[1], gap, high[2], gap, gap], axis=1),
            ],
            axis=0,
        ).astype(BF)
        t3[dx, :, 384:640] = mm(table("edge_three", 256, 128), z_edge).astype(BF)
    row = lax.broadcasted_iota(jnp.int32, (256, 64), 0) // 4
    lane = lax.broadcasted_iota(jnp.int32, (256, 64), 1)
    column = jnp.sum(jnp.where(row == lane, b3[...], 0.0), axis=1, keepdims=True)
    bias3[...] = jnp.broadcast_to(column, (256, 128))

    w4[:, 3, :, 0:128] = jnp.zeros((9, 64, 128), BF)
    w4[:, 0, :, 128:256] = jnp.zeros((9, 64, 128), BF)

    left = lax.broadcasted_iota(jnp.int32, (128, 128), 1) < 64

    def three(rows, lanes, v):
        for dz, u in enumerate((rolled_64(v, True), v, rolled_64(v, False))):
            start = dz * 128 if rows == 128 else 384 + dz * 64
            d3[start : start + rows, lanes * 128 : lanes * 128 + 128] = u.astype(BF)

    outer, middle = own3[1].astype(F32), own3[2].astype(F32)
    outer_turned, middle_turned = pltpu.roll(outer, 64, 1), pltpu.roll(middle, 64, 1)
    three(128, 0, jnp.where(left, outer_turned, middle_turned))
    three(128, 1, jnp.where(left, middle_turned, outer_turned))
    three(128, 3, middle)
    bias = bias3[...]
    a3[...] = mm(t3[1, :, 0:384], d3[0:384, 0:256]) + jnp.concatenate([bias, bias], axis=1)
    d3[576:640, :] = jnp.zeros((64, 640), BF)
    pl.semaphore_wait(wide_sem.at[0], 8)
    for dy in (-4, 4):
        greet(wide_sem.at[1], 0, dy)
    for copy in third:
        copy.wait()
    three(128, 2, jnp.where(left, own3[0].astype(F32), outer))
    three(128, 4, jnp.where(left, outer, own3[3].astype(F32)))
    edge = [jnp.concatenate([hr3[0, t], hr3[1, t]], axis=0).astype(F32) for t in range(4)]
    turned = [pltpu.roll(edge[t], 64, 1) for t in (1, 2)]
    left = lax.broadcasted_iota(jnp.int32, (64, 128), 1) < 64
    three(64, 0, jnp.where(left, turned[0], turned[1]))
    three(64, 1, jnp.where(left, turned[1], turned[0]))
    three(64, 2, jnp.where(left, edge[0], edge[1]))
    three(64, 3, edge[2])
    three(64, 4, jnp.where(left, edge[1], edge[3]))
    v = leaky(
        a3[...] + mm(t3[0], d3[:, 256:512]) + mm(t3[1, :, 384:640], d3[384:640, 0:256]) + mm(t3[2], d3[:, 384:640])
    )
    l3[...] = v.astype(BF)
    sums = mm_t(table("pick_four", 256, 256), l3[...])
    row = lax.broadcasted_iota(jnp.int32, (256, 256), 0) % 2
    lane = lax.broadcasted_iota(jnp.int32, (256, 256), 1) % 4 // 2
    sums = jnp.where(row == lane, sums, 0.0)
    head = sums.astype(BF)
    tail = (sums - head.astype(F32)).astype(BF)
    block = jnp.zeros((128, 128), F32)
    for odd in range(2):
        g = table("gather_four", 256, 128, odd * 256)
        block = block + mm(head[odd * 128 : odd * 128 + 128], g) + mm(tail[odd * 128 : odd * 128 + 128], g)
    sa[...] = block.reshape(16, 8, 128).astype(BF)
    pl.semaphore_wait(wide_sem.at[1], 2)
    me = gx * 16 + gy
    mine = pltpu.make_async_copy(sa.at[gy], rb.at[me], recva_sem)
    y_at, x_at, z_at, core_at = gx // 4 * 2 + gy // 8, gx % 4, gy // 2 % 4, gy % 2
    columns, layers = {}, {}
    for d in range(4):
        y = (y_at + d) % 4
        for e in range(4):
            columns[e, d] = y // 2 * 4 + (x_at + e) % 4
            layers[d, e] = y % 2 * 8 + (z_at + e) % 4 * 2
    hops = (0, 1, 2, 1)
    steps = [(dx, dy, dz) for dx in range(4) for dy in range(4) for dz in range(4)]
    steps.sort(key=lambda step: -sum(hops[d] for d in step))
    for dx, dy, dz in steps:
        for flip in range(2):
            if dx or dy or dz or flip:
                layer = layers[dy, dz] + (core_at + flip) % 2
                remote(sa.at[layer], rb.at[me], senda_sem, recva_sem, columns[dx, dy], layer).start()
    mine.start()
    for x in range(4):
        out3[:, x] = l3[:, x * 64 : x * 64 + 64].astype(F32).reshape(64, 4, 64).astype(BF)
    turn[...] = table("turn_four", 384, 128)
    pltpu.make_async_copy(rb, rb, recva_sem).wait()
    pltpu.make_async_copy(rb.at[0:127], rb.at[0:127], senda_sem).wait()


def last(out2_in, out3_in, rb, w4, turn, b4, out2, out3, out4, pp, l4, sem):
    leaving = [
        pltpu.make_async_copy(out2_in, out2, sem.at[0]),
        pltpu.make_async_copy(out3_in, out3, sem.at[1]),
    ]
    for copy in leaving:
        copy.start()
    for x in range(0, 8, 2):
        v = jnp.concatenate(
            [rb[k * 16 : k * 16 + 16].astype(F32).reshape(128, 128).astype(BF) for k in (x, x + 1)], axis=1
        )
        moved = mm(turn[...], v).astype(BF)
        for k in range(2):
            rows = slice((x + k) * 64, (x + k) * 64 + 64)
            for dy in range(3):
                for half in range(2):
                    start = (dy * 2 + half) * 64
                    pp[dy, rows, half * 128 : half * 128 + 128] = moved[start : start + 64, k * 128 : k * 128 + 128]
    bias = jnp.concatenate([b4[...], b4[...]], axis=1)
    size = 512 // PIECES
    for m in range(PIECES):
        operands = []
        for dx in range(3):
            start = m * size + (dx - 1) * 32
            for dy in range(3):
                if start < 0:
                    v = jnp.concatenate([pp[dy, 480:512, :], pp[dy, 0 : size - 32, :]], axis=0)
                elif start + size > 512:
                    v = jnp.concatenate([pp[dy, start:512, :], pp[dy, 0:32, :]], axis=0)
                else:
                    v = pp[dy, start : start + size, :]
                operands.append(v)
        v = leaky(mm(jnp.concatenate(operands, axis=1), w4[...].reshape(2304, 256)) + bias)
        piece = slice(m * size, m * size + size)
        l4[piece] = v.reshape(size, 2, 128).astype(BF)
        leaving.append(pltpu.make_async_copy(l4.at[piece], out4.at[piece], sem.at[2 + m]))
        leaving[-1].start()
    for copy in leaving:
        copy.wait()


def shards(features, weight_two, bias_two, weight_three, bias_three, weight_four, bias_four):
    vm = pl.BlockSpec(memory_space=pltpu.VMEM)
    hbm = pl.BlockSpec(memory_space=pltpu.HBM)
    table = jnp.asarray(TABLE)
    w3 = weight_three.transpose(0, 2, 1)
    w4 = weight_four.transpose(0, 2, 1).reshape(9, 3, 64, 128)
    dma = pltpu.SemaphoreType.DMA
    held = pl.pallas_call(
        kernel,
        out_shape=(
            jax.ShapeDtypeStruct((32, 8, 8, 128), BF),
            jax.ShapeDtypeStruct((64, 4, 4, 64), BF),
            jax.ShapeDtypeStruct((128, 8, 128), BF),
            jax.ShapeDtypeStruct((9, 4, 64, 256), BF),
            jax.ShapeDtypeStruct((384, 128), BF),
            jax.ShapeDtypeStruct((1, 128), F32),
        ),
        in_specs=[hbm] * 8,
        out_specs=(vm,) * 6,
        scratch_shapes=[
            pltpu.VMEM((10, 32, 8, 128), BF),
            pltpu.VMEM((1024, 1280), BF),
            pltpu.VMEM((2, 8, 32, 128), BF),
            pltpu.VMEM((2, 10, 32, 128), BF),
            pltpu.VMEM((27, 32, 32), BF),
            pltpu.VMEM((27, 32, 64), BF),
            pltpu.VMEM((1, 32), F32),
            pltpu.VMEM((1, 64), F32),
            pltpu.VMEM(TABLE.shape, BF),
            pltpu.VMEM((288, 128), BF),
            pltpu.VMEM((9, 256, 256), BF),
            pltpu.VMEM((3, 256, 1024), BF),
            pltpu.VMEM((4, 256, 256), F32),
            pltpu.VMEM((576, 128), BF),
            pltpu.VMEM((9, 256, 128), BF),
            pltpu.VMEM((3, 256, 640), BF),
            pltpu.VMEM((256, 128), F32),
            pltpu.VMEM((256, 128), F32),
            pltpu.VMEM((256, 128), F32),
            pltpu.VMEM((8, 256, 128), BF),
            pltpu.VMEM((4, 128, 128), BF),
            pltpu.VMEM((2, 2, 32, 128), BF),
            pltpu.VMEM((2, 4, 32, 128), BF),
            pltpu.VMEM((640, 640), BF),
            pltpu.VMEM((256, 256), F32),
            pltpu.VMEM((256, 256), BF),
            pltpu.VMEM((16, 8, 128), BF),
            dma((8,)), dma((8,)), dma((8,)), dma((8,)), dma((10,)), dma((10,)),
            dma, dma, pltpu.SemaphoreType.REGULAR((3,)),
        ],
        compiler_params=pltpu.CompilerParams(
            collective_id=0, has_side_effects=True, vmem_limit_bytes=40 * 1024 * 1024
        ),
    )(
        *(
            pltpu.with_memory_space_constraint(a, pltpu.HBM)
            for a in (features, weight_two, bias_two[None], w3, bias_three[None], w4, bias_four[None], table)
        )
    )
    level_two, level_three, bottleneck = pl.pallas_call(
        last,
        out_shape=(
            jax.ShapeDtypeStruct((32, 8, 8, 128), BF),
            jax.ShapeDtypeStruct((64, 4, 4, 64), BF),
            jax.ShapeDtypeStruct((512, 2, 128), BF),
        ),
        in_specs=[vm] * 6,
        out_specs=(hbm,) * 3,
        scratch_shapes=[
            pltpu.VMEM((3, 512, 256), BF),
            pltpu.VMEM((512, 2, 128), BF),
            dma((2 + PIECES,)),
        ],
        compiler_params=pltpu.CompilerParams(vmem_limit_bytes=40 * 1024 * 1024),
    )(*held)
    return level_two, level_three, bottleneck.reshape(16, 32, 2, 128).transpose(3, 0, 1, 2)


def solution(mesh):
    return jax.shard_map(
        shards,
        mesh=mesh,
        in_specs=(P(None, "gx", "gy", None), P(), P(), P(), P(), P(), P()),
        out_specs=(P(None, "gx", "gy", None), P(None, "gx", "gy", None), P(None, None, None, "gy")),
        check_vma=False,
    )
```

```python
import functools

import jax
import jax.numpy as jnp
import numpy as np
from jax import lax
from jax.experimental import pallas as pl
from jax.experimental.pallas import tpu as pltpu
from jax.sharding import PartitionSpec as P

BF = jnp.bfloat16
F32 = jnp.float32
MESH = pl.DeviceIdType.MESH
PIECES = 2


def tables():
    parts, at, row = [], {}, 0

    def add(name, matrix):
        nonlocal row
        rows, lanes = matrix.shape
        full = np.zeros((-(-rows // 16) * 16, 256), np.float32)
        full[:rows, :lanes] = matrix
        at[name] = row
        parts.append(full)
        row += full.shape[0]

    spread = np.zeros((8, 128, 256))
    for y in range(8):
        for dy in range(3):
            if 0 <= y + dy - 1 < 8:
                for c in range(32):
                    spread[y, dy * 32 + c, c * 8 + y + dy - 1] = 1
    add("spread_two", spread.reshape(1024, 256))
    order = np.zeros((256, 256))
    for y in range(8):
        for o in range(32):
            order[o * 8 + y, y * 32 + o] = 1
    add("order_two", order)
    edge = np.zeros((256, 64))
    for o in range(32):
        edge[o * 8, o] = 1
        edge[o * 8 + 7, 32 + o] = 1
    add("edge_two", edge)
    pool = np.zeros((2, 2, 128, 128))
    for half in range(2):
        for x in range(2):
            for z in range(128):
                pool[half, x, z, half * 64 + z // 2] = 0.125
    add("pool_two", pool.reshape(512, 128))
    select = np.zeros((64, 128))
    for c in range(32):
        select[c, c * 4] = 1
        select[32 + c, c * 4 + 3] = 1
    add("select_three", select)
    add("unit", np.eye(64))
    spread = np.zeros((4, 128, 128))
    for y in range(4):
        for dy in range(3):
            if 0 <= y + dy - 1 < 4:
                for c in range(32):
                    spread[y, dy * 32 + c, c * 4 + y + dy - 1] = 1
    add("spread_three", spread.reshape(512, 128))
    order = np.zeros((256, 256))
    for y in range(4):
        for o in range(64):
            order[o * 4 + y, y * 64 + o] = 1
    add("order_three", order)
    edge = np.zeros((256, 128))
    for o in range(64):
        edge[o * 4, o] = 1
        edge[o * 4 + 3, 64 + o] = 1
    add("edge_three", edge)
    pick = np.zeros((2, 16, 2, 2, 2, 4, 64))
    for odd in range(2):
        for target in range(16):
            for half in range(2):
                z = (2 * target - 1 + 2 * half + odd) % 32
                for x in range(2):
                    pick[odd, target, half, x, :, 2 * x : 2 * x + 2, 2 * z : 2 * z + 2] = 0.125
    add("pick_four", pick.reshape(256, 256))
    gather = np.zeros((2, 256, 128))
    for odd in range(2):
        for o in range(64):
            gather[odd, o * 4 : o * 4 + 4, odd * 64 + o] = 1
    add("gather_four", gather.reshape(512, 128))
    turn = np.zeros((3, 2, 2, 32, 16, 2, 2, 2))
    for dy in range(3):
        for half in range(2):
            for x in range(2):
                for y in range(32):
                    source = (y + dy - 1) % 32
                    turn[dy, half, x, y, source // 2, half, x, source % 2] = 1
    add("turn_four", turn.reshape(384, 128))
    return np.concatenate(parts).astype(jnp.bfloat16), at


TABLE, AT = tables()


def mm(a, b):
    return jnp.dot(a, b, preferred_element_type=F32)


def mm_t(a, b):
    return lax.dot_general(a, b, (((1,), (1,)), ((), ())), preferred_element_type=F32)


def leaky(t):
    return jnp.maximum(t, 0.1 * t)


def rolled_64(v, back):
    lane = lax.broadcasted_iota(jnp.int32, v.shape, 1) % 64
    if back:
        return jnp.where(lane == 0, pltpu.roll(v, 65, 1), pltpu.roll(v, 1, 1))
    return jnp.where(lane == 63, pltpu.roll(v, 63, 1), pltpu.roll(v, 127, 1))


def kernel(
    feat, w2_in, b2_in, w3_in, b3_in, w4_in, b4_in, tab_in,
    out2, out3, rb, w4, turn, b4,
    fx, fm, hs, hr, w2, w3, b2, b3, tab, wc2, z2, t2, a2, wc3, z3, t3, bias2, bias3,
    pooled, l2, own3, hs3, hr3, d3, a3, l3, sa,
    load_sem, feat_sem, send_sem, recv_sem, send3_sem, recv3_sem, senda_sem, recva_sem, wide_sem,
):
    gx, gy = lax.axis_index("gx"), lax.axis_index("gy")
    xp, xm = lax.rem(gx + 1, 8), lax.rem(gx + 7, 8)
    yp, ym = lax.rem(gy + 1, 16), lax.rem(gy + 15, 16)

    def table(name, rows, lanes, skip=0):
        start = AT[name] + skip
        return tab[start : start + rows, :lanes]

    barrier = pltpu.get_barrier_semaphore()

    def greet(semaphore, dx, dy):
        pl.semaphore_signal(
            semaphore, inc=1, device_id=(lax.rem(gx + dx + 8, 8), lax.rem(gy + dy + 16, 16)), device_id_type=MESH
        )

    around = [(dx, dy) for dx in (-1, 0, 1) for dy in (-1, 0, 1) if dx or dy]
    for dx, dy in around:
        greet(barrier, dx, dy)

    loads = [
        pltpu.make_async_copy(feat.at[:, x], fx.at[x + 1], feat_sem.at[x]) for x in range(8)
    ]
    others = [
        pltpu.make_async_copy(tab_in, tab, load_sem.at[0]),
        pltpu.make_async_copy(w2_in, w2, load_sem.at[1]),
        pltpu.make_async_copy(b2_in, b2, load_sem.at[2]),
        pltpu.make_async_copy(w3_in, w3, load_sem.at[3]),
        pltpu.make_async_copy(b3_in, b3, load_sem.at[4]),
        pltpu.make_async_copy(b4_in, b4, load_sem.at[5]),
        pltpu.make_async_copy(w4_in, w4.at[:, 0:3, :, 0:128], load_sem.at[6]),
        pltpu.make_async_copy(w4_in, w4.at[:, 1:4, :, 128:256], load_sem.at[7]),
    ]
    for x in (0, 7, 1, 2, 3, 4, 5, 6):
        loads[x].start()
    for copy in others:
        copy.start()


    def remote(src, dst, send, recv, x, y):
        return pltpu.make_async_remote_copy(
            src_ref=src, dst_ref=dst, send_sem=send, recv_sem=recv,
            device_id=(x, y), device_id_type=MESH,
        )

    def place(x):
        v = fx[x].astype(F32).reshape(256, 128)
        lanes = slice(x * 128, x * 128 + 128)
        fm[256:512, lanes] = v.astype(BF)

    def shift(x):
        lanes = slice(x * 128, x * 128 + 128)
        v = fm[256:512, lanes].astype(F32)
        fm[0:256, lanes] = pltpu.roll(v, 1, 1).astype(BF)
        fm[512:768, lanes] = pltpu.roll(v, 127, 1).astype(BF)

    row = lax.broadcasted_iota(jnp.int32, (64, 256), 0)
    lane = lax.broadcasted_iota(jnp.int32, (64, 256), 1)
    select = jnp.where(lane == row % 32 * 8 + row // 32 * 7, 1.0, 0.0).astype(BF)
    def cut(side_rows, x):
        for side in range(2):
            hs[side, x] = side_rows[side * 32 : side * 32 + 32]

    for x in (0, 7):
        loads[x].wait()
        place(x + 1)
        cut(mm(select, fm[256:512, x * 128 + 128 : x * 128 + 256]).astype(BF), x)
    pl.semaphore_wait(barrier, 8)
    first = [
        remote(fx.at[8], fx.at[0], send_sem.at[0], recv_sem.at[0], xp, gy),
        remote(fx.at[1], fx.at[9], send_sem.at[1], recv_sem.at[1], xm, gy),
    ]
    second = [
        remote(hs.at[1, 7], hr.at[0, 0], send_sem.at[4], recv_sem.at[4], xp, yp),
        remote(hs.at[1, 0], hr.at[0, 9], send_sem.at[5], recv_sem.at[5], xm, yp),
        remote(hs.at[0, 7], hr.at[1, 0], send_sem.at[6], recv_sem.at[6], xp, ym),
        remote(hs.at[0, 0], hr.at[1, 9], send_sem.at[7], recv_sem.at[7], xm, ym),
        remote(hs.at[1], hr.at[0, 1:9], send_sem.at[2], recv_sem.at[2], gx, yp),
        remote(hs.at[0], hr.at[1, 1:9], send_sem.at[3], recv_sem.at[3], gx, ym),
    ]
    for copy in second[:4] + first:
        copy.start()
    for x in range(1, 7):
        loads[x].wait()
        place(x + 1)
    edges = mm(select, fm[256:512, 256:1024]).astype(BF)
    for x in range(1, 7):
        cut(edges[:, (x - 1) * 128 : x * 128], x)
    for copy in second[4:]:
        copy.start()

    for x in range(1, 9):
        shift(x)
    for copy in others:
        copy.wait()
    gap = jnp.zeros((32, 32), F32)
    for dx in range(3):
        for dz in range(3):
            k = 3 * dx + dz
            wc2[k * 32 : k * 32 + 32, :] = jnp.concatenate(
                [w2[9 * dx + 3 * dy + dz].astype(F32) for dy in range(3)] + [gap], axis=1
            ).astype(BF)
    for y in range(8):
        z2[:, y * 32 : y * 32 + 32, :] = (
            mm(wc2[...], table("spread_two", 128, 256, 128 * y)).astype(BF).reshape(9, 32, 256)
        )
    for dx in range(3):
        for dz in range(3):
            t2[dx, :, dz * 256 : dz * 256 + 256] = mm(
                table("order_two", 256, 256), z2[3 * dx + dz]
            ).astype(BF)
        low = [w2[9 * dx + dz].astype(F32) for dz in range(3)]
        high = [w2[9 * dx + 6 + dz].astype(F32) for dz in range(3)]
        z_edge = jnp.concatenate(
            [
                jnp.concatenate([low[0], gap, low[1], gap, low[2], gap, gap, gap], axis=1),
                jnp.concatenate([gap, high[0], gap, high[1], gap, high[2], gap, gap], axis=1),
            ],
            axis=0,
        ).astype(BF)
        t2[dx, :, 768:1024] = mm(table("edge_two", 256, 64), z_edge).astype(BF)
    row = lax.broadcasted_iota(jnp.int32, (256, 32), 0) // 8
    lane = lax.broadcasted_iota(jnp.int32, (256, 32), 1)
    column = jnp.sum(jnp.where(row == lane, b2[...], 0.0), axis=1, keepdims=True)
    bias2[...] = jnp.broadcast_to(column, (256, 128))

    fm[0:768, 0:128] = jnp.zeros((768, 128), BF)
    fm[0:768, 1152:1280] = jnp.zeros((768, 128), BF)
    fm[960:1024, :] = jnp.zeros((64, 1280), BF)

    def inner(p, carry):
        a2[p] = mm(
            jnp.concatenate([t2[dx, :, 0:768] for dx in range(3)], axis=1),
            jnp.concatenate(
                [fm[0:768, pl.ds(pl.multiple_of((p * 2 + dx) * 128, 128), 256)] for dx in range(3)], axis=0
            ),
        )
        return carry

    lax.fori_loop(0, 4, inner, 0)

    def edge_rows(x):
        v = jnp.concatenate([hr[0, x], hr[1, x]], axis=0).astype(F32)
        lanes = slice(x * 128, x * 128 + 128)
        fm[768:832, lanes] = pltpu.roll(v, 1, 1).astype(BF)
        fm[832:896, lanes] = v.astype(BF)
        fm[896:960, lanes] = pltpu.roll(v, 127, 1).astype(BF)

    third = []

    def send3(src, dst, x, y):
        k = len(third)
        third.append(remote(src, dst, send3_sem.at[k], recv3_sem.at[k], x, y))
        third[-1].start()

    def pool_two(q):
        total = jnp.zeros((256, 128), F32)
        for half in range(2):
            p = ((3, 0), (1, 2))[q][half]
            acc = a2[p] + mm(
                jnp.concatenate([t2[dx, :, 768:1024] for dx in range(3)], axis=1),
                jnp.concatenate(
                    [fm[768:1024, (p * 2 + dx) * 128 : (p * 2 + dx + 2) * 128] for dx in range(3)], axis=0
                ),
            )
            for x in range(2):
                v = leaky(acc[:, x * 128 : x * 128 + 128] + bias2[...]).astype(BF)
                l2[2 * p + x] = v
                total = total + mm(v, table("pool_two", 128, 128, half * 256 + x * 128))
        pooled[...] = total
        mean = (pooled[pl.ds(0, 128, stride=2), :] + pooled[pl.ds(1, 128, stride=2), :]).astype(BF)
        own3[q + 1] = mean
        picked = mm(table("select_three", 64, 128), mean).astype(BF)
        hs3[0, q] = picked[0:32]
        hs3[1, q] = picked[32:64]
        if q == 0:
            for x, slot in ((xm, 3), (xp, 0)):
                send3(hs3.at[1, 0], hr3.at[0, slot], x, yp)
                send3(hs3.at[0, 0], hr3.at[1, slot], x, ym)
                send3(own3.at[1], own3.at[slot], x, gy)
        send3(hs3.at[1, q], hr3.at[0, q + 1], gx, yp)
        send3(hs3.at[0, q], hr3.at[1, q + 1], gx, ym)

    for copy in second[4:]:
        copy.wait()
    for x in range(1, 9):
        edge_rows(x)
    for copy in second[:4]:
        copy.wait()
    for x in (0, 9):
        edge_rows(x)
    for copy in first:
        copy.wait()
    for dx, dy in around:
        greet(wide_sem.at[0], 2 * dx, 2 * dy)
    for x in (0, 9):
        place(x)
        shift(x)
    a2[0, :, 0:128] += mm(t2[0, :, 0:768], fm[0:768, 0:128])
    a2[3, :, 128:256] += mm(t2[2, :, 0:768], fm[0:768, 1152:1280])
    pool_two(0)
    pool_two(1)
    for x in range(8):
        out2[:, x] = l2[x].astype(F32).reshape(32, 8, 128).astype(BF)

    for dx in range(3):
        for dz in range(3):
            k = 3 * dx + dz
            stack = jnp.concatenate(
                [w3[9 * dx + 3 * dy + dz] for dy in range(3)] + [jnp.zeros((32, 64), BF)], axis=0
            )
            wc3[k * 64 : k * 64 + 64, :] = mm_t(table("unit", 64, 64), stack).astype(BF)
    for y in range(4):
        z3[:, y * 64 : y * 64 + 64, :] = (
            mm(wc3[...], table("spread_three", 128, 128, 128 * y)).astype(BF).reshape(9, 64, 128)
        )
    gap = jnp.zeros((64, 32), F32)
    for dx in range(3):
        low, high = [], []
        for dz in range(3):
            k = 3 * dx + dz
            t3[dx, :, dz * 128 : dz * 128 + 128] = mm(table("order_three", 256, 256), z3[k]).astype(BF)
            block = wc3[k * 64 : k * 64 + 64, :].astype(F32)
            low.append(block[:, 0:32])
            high.append(block[:, 64:96])
        z_edge = jnp.concatenate(
            [
                jnp.concatenate([low[0], gap, low[1], gap, low[2], gap, gap, gap], axis=1),
                jnp.concatenate([gap, high[0], gap, high[1], gap, high[2], gap, gap], axis=1),
            ],
            axis=0,
        ).astype(BF)
        t3[dx, :, 384:640] = mm(table("edge_three", 256, 128), z_edge).astype(BF)
    row = lax.broadcasted_iota(jnp.int32, (256, 64), 0) // 4
    lane = lax.broadcasted_iota(jnp.int32, (256, 64), 1)
    column = jnp.sum(jnp.where(row == lane, b3[...], 0.0), axis=1, keepdims=True)
    bias3[...] = jnp.broadcast_to(column, (256, 128))

    w4[:, 3, :, 0:128] = jnp.zeros((9, 64, 128), BF)
    w4[:, 0, :, 128:256] = jnp.zeros((9, 64, 128), BF)

    left = lax.broadcasted_iota(jnp.int32, (128, 128), 1) < 64

    def three(rows, lanes, v):
        for dz, u in enumerate((rolled_64(v, True), v, rolled_64(v, False))):
            start = dz * 128 if rows == 128 else 384 + dz * 64
            d3[start : start + rows, lanes * 128 : lanes * 128 + 128] = u.astype(BF)

    outer, middle = own3[1].astype(F32), own3[2].astype(F32)
    outer_turned, middle_turned = pltpu.roll(outer, 64, 1), pltpu.roll(middle, 64, 1)
    three(128, 0, jnp.where(left, outer_turned, middle_turned))
    three(128, 1, jnp.where(left, middle_turned, outer_turned))
    three(128, 3, middle)
    bias = bias3[...]
    a3[...] = mm(t3[1, :, 0:384], d3[0:384, 0:256]) + jnp.concatenate([bias, bias], axis=1)
    d3[576:640, :] = jnp.zeros((64, 640), BF)
    pl.semaphore_wait(wide_sem.at[0], 8)
    for dy in (-4, 4):
        greet(wide_sem.at[1], 0, dy)
    for copy in third:
        copy.wait()
    three(128, 2, jnp.where(left, own3[0].astype(F32), outer))
    three(128, 4, jnp.where(left, outer, own3[3].astype(F32)))
    edge = [jnp.concatenate([hr3[0, t], hr3[1, t]], axis=0).astype(F32) for t in range(4)]
    turned = [pltpu.roll(edge[t], 64, 1) for t in (1, 2)]
    left = lax.broadcasted_iota(jnp.int32, (64, 128), 1) < 64
    three(64, 0, jnp.where(left, turned[0], turned[1]))
    three(64, 1, jnp.where(left, turned[1], turned[0]))
    three(64, 2, jnp.where(left, edge[0], edge[1]))
    three(64, 3, edge[2])
    three(64, 4, jnp.where(left, edge[1], edge[3]))
    v = leaky(
        a3[...] + mm(t3[0], d3[:, 256:512]) + mm(t3[1, :, 384:640], d3[384:640, 0:256]) + mm(t3[2], d3[:, 384:640])
    )
    l3[...] = v.astype(BF)
    sums = mm_t(table("pick_four", 256, 256), l3[...])
    row = lax.broadcasted_iota(jnp.int32, (256, 256), 0) % 2
    lane = lax.broadcasted_iota(jnp.int32, (256, 256), 1) % 4 // 2
    sums = jnp.where(row == lane, sums, 0.0)
    head = sums.astype(BF)
    tail = (sums - head.astype(F32)).astype(BF)
    block = jnp.zeros((128, 128), F32)
    for odd in range(2):
        g = table("gather_four", 256, 128, odd * 256)
        block = block + mm(head[odd * 128 : odd * 128 + 128], g) + mm(tail[odd * 128 : odd * 128 + 128], g)
    sa[...] = block.reshape(16, 8, 128).astype(BF)
    pl.semaphore_wait(wide_sem.at[1], 2)
    me = gx * 16 + gy
    mine = pltpu.make_async_copy(sa.at[gy], rb.at[me], recva_sem)
    y_at, x_at, z_at, core_at = gx // 4 * 2 + gy // 8, gx % 4, gy // 2 % 4, gy % 2
    columns, layers = {}, {}
    for d in range(4):
        y = (y_at + d) % 4
        for e in range(4):
            columns[e, d] = y // 2 * 4 + (x_at + e) % 4
            layers[d, e] = y % 2 * 8 + (z_at + e) % 4 * 2
    hops = (0, 1, 2, 1)
    steps = [(dx, dy, dz) for dx in range(4) for dy in range(4) for dz in range(4)]
    steps.sort(key=lambda step: -sum(hops[d] for d in step))
    for dx, dy, dz in steps:
        for flip in range(2):
            if dx or dy or dz or flip:
                layer = layers[dy, dz] + (core_at + flip) % 2
                remote(sa.at[layer], rb.at[me], senda_sem, recva_sem, columns[dx, dy], layer).start()
    mine.start()
    for x in range(4):
        out3[:, x] = l3[:, x * 64 : x * 64 + 64].astype(F32).reshape(64, 4, 64).astype(BF)
    turn[...] = table("turn_four", 384, 128)
    pltpu.make_async_copy(rb, rb, recva_sem).wait()
    pltpu.make_async_copy(rb.at[0:127], rb.at[0:127], senda_sem).wait()


def last(out2_in, out3_in, rb, w4, turn, b4, out2, out3, out4, pp, l4, sem):
    leaving = [
        pltpu.make_async_copy(out2_in, out2, sem.at[0]),
        pltpu.make_async_copy(out3_in, out3, sem.at[1]),
    ]
    for copy in leaving:
        copy.start()
    for x in range(0, 8, 2):
        v = jnp.concatenate(
            [rb[k * 16 : k * 16 + 16].astype(F32).reshape(128, 128).astype(BF) for k in (x, x + 1)], axis=1
        )
        moved = mm(turn[...], v).astype(BF)
        for k in range(2):
            rows = slice((x + k) * 64, (x + k) * 64 + 64)
            for dy in range(3):
                for half in range(2):
                    start = (dy * 2 + half) * 64
                    pp[dy, rows, half * 128 : half * 128 + 128] = moved[start : start + 64, k * 128 : k * 128 + 128]
    bias = jnp.concatenate([b4[...], b4[...]], axis=1)
    size = 512 // PIECES
    for m in range(PIECES):
        operands = []
        for dx in range(3):
            start = m * size + (dx - 1) * 32
            for dy in range(3):
                if start < 0:
                    v = jnp.concatenate([pp[dy, 480:512, :], pp[dy, 0 : size - 32, :]], axis=0)
                elif start + size > 512:
                    v = jnp.concatenate([pp[dy, start:512, :], pp[dy, 0:32, :]], axis=0)
                else:
                    v = pp[dy, start : start + size, :]
                operands.append(v)
        v = leaky(mm(jnp.concatenate(operands, axis=1), w4[...].reshape(2304, 256)) + bias)
        piece = slice(m * size, m * size + size)
        l4[piece] = v.reshape(size, 2, 128).astype(BF)
        leaving.append(pltpu.make_async_copy(l4.at[piece], out4.at[piece], sem.at[2 + m]))
        leaving[-1].start()
    for copy in leaving:
        copy.wait()


def shards(features, weight_two, bias_two, weight_three, bias_three, weight_four, bias_four):
    vm = pl.BlockSpec(memory_space=pltpu.VMEM)
    hbm = pl.BlockSpec(memory_space=pltpu.HBM)
    table = jnp.asarray(TABLE)
    w3 = weight_three.transpose(0, 2, 1)
    w4 = weight_four.transpose(0, 2, 1).reshape(9, 3, 64, 128)
    dma = pltpu.SemaphoreType.DMA
    held = pl.pallas_call(
        kernel,
        out_shape=(
            jax.ShapeDtypeStruct((32, 8, 8, 128), BF),
            jax.ShapeDtypeStruct((64, 4, 4, 64), BF),
            jax.ShapeDtypeStruct((128, 8, 128), BF),
            jax.ShapeDtypeStruct((9, 4, 64, 256), BF),
            jax.ShapeDtypeStruct((384, 128), BF),
            jax.ShapeDtypeStruct((1, 128), F32),
        ),
        in_specs=[hbm] * 8,
        out_specs=(vm,) * 6,
        scratch_shapes=[
            pltpu.VMEM((10, 32, 8, 128), BF),
            pltpu.VMEM((1024, 1280), BF),
            pltpu.VMEM((2, 8, 32, 128), BF),
            pltpu.VMEM((2, 10, 32, 128), BF),
            pltpu.VMEM((27, 32, 32), BF),
            pltpu.VMEM((27, 32, 64), BF),
            pltpu.VMEM((1, 32), F32),
            pltpu.VMEM((1, 64), F32),
            pltpu.VMEM(TABLE.shape, BF),
            pltpu.VMEM((288, 128), BF),
            pltpu.VMEM((9, 256, 256), BF),
            pltpu.VMEM((3, 256, 1024), BF),
            pltpu.VMEM((4, 256, 256), F32),
            pltpu.VMEM((576, 128), BF),
            pltpu.VMEM((9, 256, 128), BF),
            pltpu.VMEM((3, 256, 640), BF),
            pltpu.VMEM((256, 128), F32),
            pltpu.VMEM((256, 128), F32),
            pltpu.VMEM((256, 128), F32),
            pltpu.VMEM((8, 256, 128), BF),
            pltpu.VMEM((4, 128, 128), BF),
            pltpu.VMEM((2, 2, 32, 128), BF),
            pltpu.VMEM((2, 4, 32, 128), BF),
            pltpu.VMEM((640, 640), BF),
            pltpu.VMEM((256, 256), F32),
            pltpu.VMEM((256, 256), BF),
            pltpu.VMEM((16, 8, 128), BF),
            dma((8,)), dma((8,)), dma((8,)), dma((8,)), dma((10,)), dma((10,)),
            dma, dma, pltpu.SemaphoreType.REGULAR((2,)),
        ],
        compiler_params=pltpu.CompilerParams(
            collective_id=0, has_side_effects=True, vmem_limit_bytes=40 * 1024 * 1024
        ),
    )(
        *(
            pltpu.with_memory_space_constraint(a, pltpu.HBM)
            for a in (features, weight_two, bias_two[None], w3, bias_three[None], w4, bias_four[None], table)
        )
    )
    level_two, level_three, bottleneck = pl.pallas_call(
        last,
        out_shape=(
            jax.ShapeDtypeStruct((32, 8, 8, 128), BF),
            jax.ShapeDtypeStruct((64, 4, 4, 64), BF),
            jax.ShapeDtypeStruct((512, 2, 128), BF),
        ),
        in_specs=[vm] * 6,
        out_specs=(hbm,) * 3,
        scratch_shapes=[
            pltpu.VMEM((3, 512, 256), BF),
            pltpu.VMEM((512, 2, 128), BF),
            dma((2 + PIECES,)),
        ],
        compiler_params=pltpu.CompilerParams(vmem_limit_bytes=40 * 1024 * 1024),
    )(*held)
    return level_two, level_three, bottleneck.reshape(16, 32, 2, 128).transpose(3, 0, 1, 2)


def solution(mesh):
    return jax.shard_map(
        shards,
        mesh=mesh,
        in_specs=(P(None, "gx", "gy", None), P(), P(), P(), P(), P(), P()),
        out_specs=(P(None, "gx", "gy", None), P(None, "gx", "gy", None), P(None, None, None, "gy")),
        check_vma=False,
    )
```
